128 devices in a mesh: dp: 8 (over z_lo, y), seq: 16 (over z_hi, x, core).
Axes of the slice: x: 4, y: 4, z: 4 (z_hi: 2, z_lo: 2; z = z_hi * 2 + z_lo), core: 2. Of those that a mesh axis runs over, the one named last changes fastest.
Arguments:
- inputs: bfloat16 [16384, 1024], P(('dp', 'seq')), may hold values from -6 to 6
- segments: int32 [16384], P(('dp', 'seq')), may hold values from 0 to 4, as said below
- cotangent: bfloat16 [16384, 1024], P(('dp', 'seq')), may hold values from -6 to 6
- attn_gain: bfloat16 [1024], P(('dp', 'seq')), may hold values from 0.5 to 1.5
- w_query: bfloat16 [1024, 256], P(('dp', 'seq')), may hold values from -0.1875 to 0.1875
- w_key: bfloat16 [1024, 256], P(('dp', 'seq')), may hold values from -0.1875 to 0.1875
- w_value: bfloat16 [1024, 1024], P(('dp', 'seq')), may hold values from -0.1875 to 0.1875
- w_conv_gate: bfloat16 [1024, 1024], P(('dp', 'seq')), may hold values from -0.1875 to 0.1875
- conv_kernel: bfloat16 [3, 1024], P(None, ('dp', 'seq')), may hold values from -3 to 3
- w_output: bfloat16 [1024, 1024], P(('dp', 'seq')), may hold values from -0.1875 to 0.1875
- ffn_gain: bfloat16 [1024], P(('dp', 'seq')), may hold values from 0.5 to 1.5
- w_ffn_gate: bfloat16 [1024, 2816], P(('dp', 'seq')), may hold values from -0.1875 to 0.1875
- w_ffn_up: bfloat16 [1024, 2816], P(('dp', 'seq')), may hold values from -0.1875 to 0.1875
- w_ffn_down: bfloat16 [2816, 1024], P(('dp', 'seq')), may hold values from -0.109375 to 0.109375
Outputs:
- result: bfloat16 [16384, 1024], P(('dp', 'seq'))
- d_inputs: bfloat16 [16384, 1024], P(('dp', 'seq'))
- grad_attn_gain: float32 [1024], P(('dp', 'seq'))
- grad_query: float32 [1024, 256], P(('dp', 'seq'))
- grad_key: float32 [1024, 256], P(('dp', 'seq'))
- grad_value: float32 [1024, 1024], P(('dp', 'seq'))
- grad_conv_gate: float32 [1024, 1024], P(('dp', 'seq'))
- grad_conv_kernel: float32 [3, 1024], P(None, ('dp', 'seq'))
- grad_output: float32 [1024, 1024], P(('dp', 'seq'))
- grad_ffn_gain: float32 [1024], P(('dp', 'seq'))
- grad_ffn_gate: float32 [1024, 2816], P(('dp', 'seq'))
- grad_ffn_up: float32 [1024, 2816], P(('dp', 'seq'))
- grad_ffn_down: float32 [2816, 1024], P(('dp', 'seq'))
The draws below stay inside these ranges and needn't reach their ends.
Inputs may be any that keep to these rules, and one draw needn't show every extreme that they name: `segments`: within each sequence of 2048 tokens the numbers never fall; in each sequence one document runs from inside the first block of 128 tokens to inside the last one.
All inputs are finite; a program needn't handle non-finite values.
Results may differ from the reference program's by a relative error of at most 0.02.
Values may be sent and summed in bfloat16 or wider, within the bound.
No kernel may reach another device: no remote copies, remote signals or barrier semaphores. Data moves between devices by JAX's collectives and lax.ppermute only.
A program may use at most 192 MiB of HBM per device.

```python
import math
import jax
import jax.numpy as jnp
from jax import lax

D = 1024
HEADS = 16
FEAT = 16
FF = 2816
CONV = 3
TOK_DEV = 128
HF = 256
LENGTH = 2048
SEQS = 8
TOKENS = 16384


def draw_segments(key, part):
    key = jax.random.fold_in(key, 11)
    first, second, third, fourth = jax.random.split(key, 4)
    start = jax.random.randint(first, (SEQS,), 1, TOK_DEV)
    opening = jax.random.randint(second, (SEQS,), 1, start + 1)
    finish = LENGTH - jax.random.randint(third, (SEQS,), 1, TOK_DEV)
    closing = jax.random.randint(fourth, (SEQS,), finish, LENGTH)
    place = jnp.arange(LENGTH)[None, :]
    labels = (place >= opening[:, None]).astype(jnp.int32)
    labels = labels + (place >= start[:, None]).astype(jnp.int32)
    labels = labels + (place >= finish[:, None]).astype(jnp.int32)
    labels = labels + (place >= closing[:, None]).astype(jnp.int32)
    return labels.reshape(SEQS * LENGTH)


def block_scale(key, shape, pieces, smallest, largest):
    level = 1.0
    for position, shards_of in pieces:
        draws = jax.random.uniform(jax.random.fold_in(jax.random.fold_in(key, 6), position), (shards_of,), jnp.float32, smallest / len(pieces), largest / len(pieces))
        level = level * jnp.repeat(jnp.exp(draws), shape[position] // shards_of).reshape((-1,) + (1,) * (len(shape) - 1 - position))
    return level


def centred(key, shape, deviation, reach, shards=(), kind=jnp.bfloat16):
    result = deviation * jax.random.normal(key, shape, jnp.float32)
    if shards:
        result = result * block_scale(key, shape, shards, -0.22, 0.18)
    return jnp.clip(result, -reach, reach).astype(kind)


def setup_inputs(seed: int = 0) -> dict:
    arg_keys = jax.random.split(jax.random.key(seed), 15)
    inputs = centred(arg_keys[0], (TOKENS, D), 1.0, 6.0, ((0, 128),))
    segments = draw_segments(jax.random.fold_in(arg_keys[14], 71), 0)
    cotangent = centred(arg_keys[2], (TOKENS, D), 1.0, 6.0, ((0, 128),))
    attn_gain = jnp.clip(1.0 + 0.1 * jax.random.normal(arg_keys[3], (D,), jnp.float32), 0.5, 1.5).astype(jnp.bfloat16)
    w_query = centred(arg_keys[4], (D, HF), D ** -0.5, 0.1875, ((0, 128),))
    w_key = centred(arg_keys[5], (D, HF), D ** -0.5, 0.1875, ((0, 128),))
    w_value = centred(arg_keys[6], (D, D), D ** -0.5, 0.1875, ((0, 128),))
    w_conv_gate = centred(arg_keys[7], (D, D), D ** -0.5, 0.1875, ((0, 128),))
    conv_kernel = centred(arg_keys[8], (CONV, D), 0.5, 3.0, ((1, 128),))
    w_output = centred(arg_keys[9], (D, D), D ** -0.5, 0.1875, ((0, 128),))
    ffn_gain = jnp.clip(1.0 + 0.1 * jax.random.normal(arg_keys[10], (D,), jnp.float32), 0.5, 1.5).astype(jnp.bfloat16)
    w_ffn_gate = centred(arg_keys[11], (D, FF), D ** -0.5, 0.1875, ((0, 128),))
    w_ffn_up = centred(arg_keys[12], (D, FF), D ** -0.5, 0.1875, ((0, 128),))
    w_ffn_down = centred(arg_keys[13], (FF, D), FF ** -0.5, 0.109375, ((0, 128),))
    return dict(inputs=inputs, segments=segments, cotangent=cotangent, attn_gain=attn_gain, w_query=w_query, w_key=w_key, w_value=w_value, w_conv_gate=w_conv_gate, conv_kernel=conv_kernel, w_output=w_output, ffn_gain=ffn_gain, w_ffn_gate=w_ffn_gate, w_ffn_up=w_ffn_up, w_ffn_down=w_ffn_down)


EPSILON = 1e-05
OUTER_SCALE = 0.25 / math.sqrt(2.0)
PRECISE = lax.Precision.HIGHEST

@jax.custom_vjp
def low(v):
    return lax.optimization_barrier(v.astype(jnp.bfloat16)).astype(jnp.float32)

@jax.custom_vjp
def low_back(v):
    return v

def low_keep(v):
    return (low(v), None)

def low_pass(kept, grad):
    return (grad,)

def back_keep(v):
    return (v, None)

def back_low(kept, grad):
    return (low(grad),)
low.defvjp(low_keep, low_pass)
low_back.defvjp(back_keep, back_low)

def rms_norm(field):
    return field * lax.rsqrt(lax.optimization_barrier(jnp.mean(field * field, -1, keepdims=True)) + EPSILON)

def matmul_hi(left, right):
    return jnp.dot(left, right, precision=PRECISE)

def lift_features(field):
    width = field.shape[-1]
    ones = jnp.ones(field.shape[:-1] + (1,), field.dtype)
    outer = (field[..., :, None] * field[..., None, :]).reshape(field.shape[:-1] + (width * width,))
    return jnp.concatenate([ones, field * 0.5, outer * OUTER_SCALE], -1)

def with_ones(values, heads):
    rows = values.shape[0]
    split = values.reshape(rows, heads, values.shape[1] // heads)
    return jnp.concatenate([split, jnp.ones((rows, heads, 1), values.dtype)], -1)

def attend_block(queries, keys_in, values, labels, carried_state, carried_label):
    rows, heads = (queries.shape[0], queries.shape[1])
    extended = with_ones(values, heads)
    inner = jnp.einsum('thf,shf->hts', queries, keys_in, precision=PRECISE)
    weights = 1.0 + inner * 0.25 + inner * inner * (1.0 / 32.0)
    place = jnp.arange(rows)
    allowed = (place[:, None] >= place[None, :]) & (labels[:, None] == labels[None, :])
    weights = jnp.where(allowed[None], weights, 0.0)
    inside = jnp.einsum('hts,she->the', weights, extended, precision=PRECISE)
    carried = jnp.einsum('thp,hpe->the', lift_features(queries), carried_state, precision=PRECISE)
    usable = (labels == carried_label)[:, None, None]
    total = inside + jnp.where(usable, carried, 0.0)
    attended = total[..., :-1] / total[..., -1:]
    normed = attended * lax.rsqrt(lax.optimization_barrier(jnp.mean(attended * attended, -1, keepdims=True)) + EPSILON)
    return normed.reshape(rows, -1)

def state_element(keys_in, values, labels):
    heads = keys_in.shape[1]
    extended = with_ones(values, heads)
    keep = (labels == labels[-1]).astype(keys_in.dtype)
    lifted = lift_features(keys_in) * keep[:, None, None]
    return jnp.einsum('thp,the->hpe', lifted, extended, precision=PRECISE)

def linear_attention(queries, keys_in, values, labels):
    length = queries.shape[0]
    block = math.gcd(length, 512)
    count = length // block
    query_blocks = queries.reshape(count, block, HEADS, FEAT)
    key_blocks = keys_in.reshape(count, block, HEADS, FEAT)
    value_blocks = values.reshape(count, block, values.shape[1])
    label_blocks = labels.reshape(count, block)

    def advance(carry, item):
        carried_state, carried_label = carry
        query_part, key_part, value_part, label_part = item
        output = attend_block(query_part, key_part, value_part, label_part, carried_state, carried_label)
        element = state_element(key_part, value_part, label_part)
        last_label = label_part[-1]
        merged = element + jnp.where(carried_label == last_label, carried_state, 0.0)
        return ((merged, last_label), output)
    start_state = jnp.zeros((HEADS, 1 + FEAT + FEAT * FEAT, values.shape[1] // HEADS + 1), jnp.float32)
    start_label = jnp.full((), -1.0, jnp.float32)
    _, outputs = lax.scan(jax.checkpoint(advance), (start_state, start_label), (query_blocks, key_blocks, value_blocks, label_blocks))
    return outputs.reshape(length, -1)

def short_conv(values, labels, kernel):
    total = kernel[0] * values
    for shift in range(1, kernel.shape[0]):
        moved = jnp.concatenate([jnp.zeros((shift, values.shape[1]), values.dtype), values[:-shift]], 0)
        moved_labels = jnp.concatenate([jnp.full((shift,), -1.0, labels.dtype), labels[:-shift]], 0)
        total = total + kernel[shift] * jnp.where((moved_labels == labels)[:, None], moved, 0.0)
    return total

def layer_forward(inputs_f, labels, weights):
    attn_gain, w_query, w_key, w_value, w_conv_gate, conv_kernel, w_output, ffn_gain, w_ffn_gate, w_ffn_up, w_ffn_down = weights
    act_one = low(rms_norm(inputs_f) * attn_gain)
    queries = low_back(low(matmul_hi(act_one, w_query)))
    keys_proj = low_back(low(matmul_hi(act_one, w_key)))
    values = low_back(low(matmul_hi(act_one, w_value)))
    conv_gate = low_back(matmul_hi(act_one, w_conv_gate))
    attended = linear_attention(queries, keys_proj, values, labels)
    conv_out = short_conv(values, labels, conv_kernel)
    mixed = low(attended + conv_out * conv_gate)
    after_mixer = inputs_f + low_back(matmul_hi(mixed, w_output))
    act_two = low(rms_norm(after_mixer) * ffn_gain)
    gate_pre = low_back(matmul_hi(act_two, w_ffn_gate))
    up_proj = low_back(matmul_hi(act_two, w_ffn_up))
    hidden = low(jax.nn.silu(gate_pre) * up_proj)
    return after_mixer + matmul_hi(hidden, w_ffn_down)

def reference(inputs, segments, cotangent, attn_gain, w_query, w_key, w_value, w_conv_gate, conv_kernel, w_output, ffn_gain, w_ffn_gate, w_ffn_up, w_ffn_down):
    params = tuple((weight.astype(jnp.float32) for weight in (attn_gain, w_query, w_key, w_value, w_conv_gate, conv_kernel, w_output, ffn_gain, w_ffn_gate, w_ffn_up, w_ffn_down)))
    seq_inputs = inputs.astype(jnp.float32).reshape(SEQS, LENGTH, D)
    seq_labels = segments.astype(jnp.float32).reshape(SEQS, LENGTH)
    seq_cotangent = cotangent.astype(jnp.float32).reshape(SEQS, LENGTH, D)

    def one_sequence(totals, item):
        rows_in, labels, cot_rows = item

        def forward(field, weights):
            return layer_forward(field, labels, weights)
        output, pull = jax.vjp(forward, rows_in, params)
        grad_rows, grad_params = pull(cot_rows)
        totals = tuple((total + grad for total, grad in zip(totals, grad_params)))
        return (totals, (output.astype(jnp.bfloat16), grad_rows.astype(jnp.bfloat16)))
    zeros = tuple((jnp.zeros_like(weight) for weight in params))
    totals, (outputs, grads_in) = lax.scan(one_sequence, zeros, (seq_inputs, seq_labels, seq_cotangent))
    return (outputs.reshape(TOKENS, D), grads_in.reshape(TOKENS, D), totals[0], totals[1], totals[2], totals[3], totals[4], totals[5], totals[6], totals[7], totals[8], totals[9], totals[10])
```

```python
import functools

import jax
import jax.numpy as jnp
from jax import lax
from jax.experimental import pallas as pl
from jax.experimental.pallas import tpu as pltpu
from jax.sharding import Mesh, PartitionSpec as P

EPSILON = 1e-05
BF = jnp.bfloat16
F32 = jnp.float32

AXES = ("zl", "y", "zh", "x", "core")
SIZES = (2, 4, 2, 4, 2)
GROUP = ("zl", "y", "zh")
TEAM = ("x", "core")
ROWS = 128
TEAM_ROWS = 1024
TILE = 256
KLANE = 32
ONE = 64
STATE = 384
TAIL = 2 * STATE
PAYLOAD = TAIL + 32


def from_x(block, hop):
    return lax.ppermute(block, "x", [(i, (i - hop) % 4) for i in range(4)])


def to_x(block, hop):
    return lax.ppermute(block, "x", [(i, (i + hop) % 4) for i in range(4)])


def swap_core(block):
    return lax.ppermute(block, "core", [(0, 1), (1, 0)])


def team_gather(block):
    own = jnp.concatenate([block] + [from_x(block, hop) for hop in (1, 2, 3)], 0)
    return jnp.concatenate([own, swap_core(own)], 0)


def team_scatter(partial):
    partial = partial.astype(BF)
    half = partial.shape[0] // 2
    mine = partial[:half].astype(F32) + swap_core(partial[half:]).astype(F32)
    came = [
        to_x(mine[hop * ROWS : (hop + 1) * ROWS].astype(BF), hop).astype(F32)
        for hop in (1, 2, 3)
    ]
    return mine[:ROWS] + came[0] + came[1] + came[2]


def dot(left, right):
    return jnp.dot(left, right, preferred_element_type=F32)


def dot_nt(left, right):
    return lax.dot_general(left, right, (((1,), (1,)), ((), ())), preferred_element_type=F32)


def dot_tn(left, right):
    return lax.dot_general(left, right, (((0,), (0,)), ((), ())), preferred_element_type=F32)


def iota(shape, dim):
    return lax.broadcasted_iota(jnp.int32, shape, dim)


def one_hot(condition):
    return jnp.where(condition, 1.0, 0.0).astype(BF)


def spread(first, which):
    row, lane = iota((256, 128), 0), iota((256, 128), 1)
    part = row // 16 if which == 0 else row % 16
    return one_hot(lane == first + part)


def q_to_k(head):
    row, lane = iota((128, 128), 0), iota((128, 128), 1)
    low = 16 * head
    return one_hot((lane == row + KLANE) & (row >= low) & (row < low + 16))


def identity():
    return one_hot(iota((128, 128), 0) == iota((128, 128), 1))


def head_lanes(head, rows):
    lane = iota((rows, 128), 1)
    return lane < 64 if head == 0 else lane >= 64


def one_lane(head):
    return 64 if head == 0 else 0


def extended(values, head):
    rows = values.shape[0]
    lane = iota((rows, 128), 1)
    ones = jnp.where(lane == one_lane(head), 1.0, 0.0).astype(values.dtype)
    return jnp.where(head_lanes(head, rows), values, ones)


def column(labels_row):
    return jnp.transpose(jnp.broadcast_to(labels_row, (128, TEAM_ROWS)))


def shift_down(field, by, head_rows):
    moved = pltpu.roll(field, by, 0)
    row = iota(field.shape, 0)
    for at in range(by):
        moved = jnp.where(row == at, head_rows[at : at + 1], moved)
    return moved


def conv_parts(values, tail, labels, carried):
    back_1 = shift_down(values, 1, tail[15:16])
    back_2 = shift_down(values, 2, tail[14:16])
    carried_2 = jnp.broadcast_to(carried, (2, 128))
    mask_1 = shift_down(labels, 1, carried_2) == labels
    mask_2 = shift_down(labels, 2, carried_2) == labels
    return (
        jnp.where(mask_1, back_1, 0.0),
        jnp.where(mask_2, back_2, 0.0),
        mask_1,
        mask_2,
    )


def tile_mask(labels_col, labels_row, i, j):
    col = labels_col[i * TILE : (i + 1) * TILE]
    col = jnp.concatenate([col] * (TILE // 128), 1)
    row = labels_row[:, j * TILE : (j + 1) * TILE]
    return col == row


def state_kernel(order, p_ref, lab_ref, pabs_ref, pay_ref):
    for block in range(8):
        start = pl.multiple_of(order[block] * ROWS, ROWS)
        pabs_ref[block * ROWS : (block + 1) * ROWS, :] = p_ref[pl.ds(start, ROWS), :]
    lane = iota((TEAM_ROWS, 128), 1)
    packed = pabs_ref[:, 256:384]
    packed = jnp.where(lane == ONE, jnp.ones_like(packed), packed)
    pabs_ref[:, 256:384] = packed
    values = pabs_ref[:, 0:128]
    labels = column(lab_ref[...])
    last = labels[TEAM_ROWS - 1 : TEAM_ROWS]
    keep = labels == last
    turned = dot_nt(identity(), packed).astype(BF)
    for head in range(2):
        ext = jnp.where(keep, extended(values, head), jnp.zeros_like(values))
        first = KLANE + 16 * head
        outer = dot_nt(spread(first, 0), packed) * dot_nt(spread(first, 1), packed)
        at = head * STATE
        pay_ref[at : at + 256, :] = dot(outer.astype(BF), ext).astype(BF)
        pay_ref[at + 256 : at + 384, :] = dot(turned, ext).astype(BF)
    tail = jnp.where(keep, values, jnp.zeros_like(values))
    pay_ref[TAIL : TAIL + 16, :] = tail[TEAM_ROWS - 16 :]
    pay_ref[TAIL + 16 : TAIL + 32, :] = jnp.broadcast_to(last + 1.0, (16, 128)).astype(BF)


def local_kernel(pabs_ref, lab_ref, tot_ref):
    packed = pabs_ref[:, 256:384]
    values = pabs_ref[:, 0:128]
    labels_row = lab_ref[...]
    labels = column(labels_row)
    order = iota((TILE, TILE), 0) >= iota((TILE, TILE), 1)
    moved = [dot(packed, q_to_k(head)).astype(BF) for head in range(2)]
    ext = [extended(values, head) for head in range(2)]
    count = TEAM_ROWS // TILE
    for i in range(count):
        rows = slice(i * TILE, (i + 1) * TILE)
        total = [jnp.zeros((TILE, 128), F32) for _ in range(2)]
        for j in range(i + 1):
            cols = slice(j * TILE, (j + 1) * TILE)
            mask = tile_mask(labels, labels_row, i, j)
            if i == j:
                mask = mask & order
            for head in range(2):
                inner = dot_nt(moved[head][rows], packed[cols])
                weight = 1.0 + inner * (0.25 + inner * (1.0 / 32.0))
                weight = jnp.where(mask, weight, 0.0).astype(BF)
                total[head] = total[head] + dot(weight, ext[head][cols])
        for head in range(2):
            tot_ref[head, rows, :] = total[head]


def normalised(total, head):
    lane = iota(total.shape, 1)
    mass = jnp.sum(jnp.where(lane == one_lane(head), total, 0.0), 1, keepdims=True)
    inside = head_lanes(head, total.shape[0])
    attended = jnp.where(inside, total / mass, 0.0)
    mean = jnp.sum(attended * attended, 1, keepdims=True) * (1.0 / 64.0)
    return attended, mass, lax.rsqrt(mean + EPSILON)


def carried_query(packed, head):
    lane = iota(packed.shape, 1)
    moved = dot(packed, q_to_k(head)) * 0.25
    return jnp.where(lane == ONE, 1.0, moved).astype(BF)


def join_kernel(order, pabs_ref, lab_ref, local_ref, came_ref, taps_ref, tot_ref, mixed_ref):
    packed = pabs_ref[:, 256:384]
    values = pabs_ref[:, 0:128].astype(F32)
    labels = column(lab_ref[...])
    carried = came_ref[TAIL + 16 : TAIL + 17, :].astype(F32) - 1.0
    usable = labels == carried
    attn = jnp.zeros((TEAM_ROWS, 128), F32)
    for head in range(2):
        at = head * STATE
        first = 16 * head
        outer = dot_nt(packed, spread(first, 0)) * dot_nt(packed, spread(first, 1))
        brought = dot(outer.astype(BF), came_ref[at : at + 256, :]) * (1.0 / 32.0)
        brought = brought + dot(carried_query(packed, head), came_ref[at + 256 : at + 384, :])
        total = local_ref[head] + jnp.where(usable, brought, 0.0)
        tot_ref[head] = total
        attended, _, scale = normalised(total, head)
        attn = attn + attended * scale
    tail = came_ref[TAIL : TAIL + 16, :].astype(F32)
    back_1, back_2, _, _ = conv_parts(values, tail, labels, carried)
    conv = taps_ref[0:1] * values + taps_ref[1:2] * back_1 + taps_ref[2:3] * back_2
    mixed = (attn + conv * pabs_ref[:, 128:256].astype(F32)).astype(BF)
    for block in range(8):
        start = pl.multiple_of(order[block] * ROWS, ROWS)
        mixed_ref[pl.ds(start, ROWS), :] = mixed[block * ROWS : (block + 1) * ROWS]


def back_state_kernel(
    order, pabs_ref, lab_ref, tot_ref, came_ref, taps_ref, dmix_ref,
    de_ref, dvconv_ref, dgate_ref, dtaps_ref, pay_ref, dm_ref,
):
    for block in range(8):
        start = pl.multiple_of(order[block] * ROWS, ROWS)
        dm_ref[block * ROWS : (block + 1) * ROWS, :] = dmix_ref[pl.ds(start, ROWS), :]
    d_mixed = dm_ref[...]
    packed = pabs_ref[:, 256:384]
    values = pabs_ref[:, 0:128].astype(F32)
    labels = column(lab_ref[...])
    carried = came_ref[TAIL + 16 : TAIL + 17, :].astype(F32) - 1.0
    usable = labels == carried
    lane = iota((TEAM_ROWS, 128), 1)
    for head in range(2):
        attended, mass, scale = normalised(tot_ref[head], head)
        d_attn = jnp.where(head_lanes(head, TEAM_ROWS), d_mixed, 0.0)
        pull = jnp.sum(d_attn * attended, 1, keepdims=True) * (1.0 / 64.0)
        d_att = scale * (d_attn - attended * (scale * scale * pull))
        d_mass = -jnp.sum(d_att * attended, 1, keepdims=True) / mass
        d_ext = jnp.where(lane == one_lane(head), d_mass, d_att / mass).astype(BF)
        de_ref[head] = d_ext
        d_ext = jnp.where(usable, d_ext, jnp.zeros_like(d_ext))
        first = 16 * head
        at = head * STATE
        outer = dot_nt(spread(first, 0), packed) * dot_nt(spread(first, 1), packed)
        pay_ref[at : at + 256, :] = (dot(outer.astype(BF), d_ext) * (1.0 / 32.0)).astype(BF)
        turned = dot_nt(identity(), carried_query(packed, head)).astype(BF)
        pay_ref[at + 256 : at + 384, :] = dot(turned, d_ext).astype(BF)
    tail = came_ref[TAIL : TAIL + 16, :].astype(F32)
    back_1, back_2, mask_1, mask_2 = conv_parts(values, tail, labels, carried)
    conv = taps_ref[0:1] * values + taps_ref[1:2] * back_1 + taps_ref[2:3] * back_2
    dgate_ref[...] = (d_mixed * conv).astype(BF)
    d_conv = d_mixed * pabs_ref[:, 128:256].astype(F32)
    row8 = iota((8, 128), 0)
    sums = [jnp.sum(d_conv * part, 0, keepdims=True) for part in (values, back_1, back_2)]
    d_taps = jnp.zeros((8, 128), F32)
    for at in range(3):
        d_taps = jnp.where(row8 == at, sums[at], d_taps)
    dtaps_ref[...] = d_taps
    part_1 = jnp.where(mask_1, taps_ref[1:2] * d_conv, 0.0)
    part_2 = jnp.where(mask_2, taps_ref[2:3] * d_conv, 0.0)
    row = iota((TEAM_ROWS, 128), 0)
    up_1 = jnp.where(row < TEAM_ROWS - 1, pltpu.roll(part_1, TEAM_ROWS - 1, 0), 0.0)
    up_2 = jnp.where(row < TEAM_ROWS - 2, pltpu.roll(part_2, TEAM_ROWS - 2, 0), 0.0)
    dvconv_ref[...] = taps_ref[0:1] * d_conv + up_1 + up_2
    row16 = iota((16, 128), 0)
    edge = jnp.where(row16 == 14, part_2[0:1], 0.0)
    edge = jnp.where(row16 == 15, part_1[0:1] + part_2[1:2], edge)
    pay_ref[TAIL : TAIL + 16, :] = edge.astype(BF)
    pay_ref[TAIL + 16 : TAIL + 32, :] = jnp.zeros((16, 128), BF)


def back_local_kernel(pabs_ref, lab_ref, de_ref, came_ref, dqk_ref, dv_ref, dqt_ref):
    packed = pabs_ref[:, 256:384]
    values = pabs_ref[:, 0:128]
    labels_row = lab_ref[...]
    labels = column(labels_row)
    order = iota((TILE, TILE), 0) <= iota((TILE, TILE), 1)
    moved = [dot(packed, q_to_k(head)).astype(BF) for head in range(2)]
    keys_t = [dot_nt(q_to_k(head), packed).astype(BF) for head in range(2)]
    ext = [extended(values, head) for head in range(2)]
    inside = [head_lanes(head, TILE) for head in range(2)]
    count = TEAM_ROWS // TILE
    dqt_ref[...] = jnp.zeros((128, TEAM_ROWS), F32)
    for j in range(count):
        cols = slice(j * TILE, (j + 1) * TILE)
        d_key = jnp.zeros((TILE, 128), F32)
        d_val = jnp.zeros((TILE, 128), F32)
        for i in range(j, count):
            rows = slice(i * TILE, (i + 1) * TILE)
            mask = tile_mask(labels, labels_row, j, i)
            if i == j:
                mask = mask & order
            for head in range(2):
                d_ext = de_ref[head, rows, :]
                inner = dot_nt(packed[cols], moved[head][rows])
                weight = 1.0 + inner * (0.25 + inner * (1.0 / 32.0))
                weight = jnp.where(mask, weight, 0.0).astype(BF)
                d_weight = dot_nt(ext[head][cols], d_ext)
                d_inner = jnp.where(mask, d_weight * (0.25 + inner * (1.0 / 16.0)), 0.0).astype(BF)
                d_sum = jnp.where(inside[head], d_ext, jnp.zeros_like(d_ext))
                d_val = d_val + dot(weight, d_sum)
                d_key = d_key + dot(d_inner, moved[head][rows])
                dqt_ref[:, rows] += dot(keys_t[head][:, cols], d_inner)
        dqk_ref[cols, :] = d_key
        dv_ref[cols, :] = d_val
    carried = came_ref[TAIL + 16 : TAIL + 17, :].astype(F32) - 1.0
    usable = labels == carried
    total = dqk_ref[...] + jnp.transpose(dqt_ref[...])
    for head in range(2):
        d_ext = de_ref[head]
        d_ext = jnp.where(usable, d_ext, jnp.zeros_like(d_ext))
        at = head * STATE
        first = 16 * head
        d_outer = dot_nt(d_ext, came_ref[at : at + 256, :]) * dot_nt(packed, spread(first, 1))
        total = total + dot((d_outer * (1.0 / 16.0)).astype(BF), spread(first, 0))
        d_line = dot_nt(d_ext, came_ref[at + 256 : at + 384, :]) * 0.25
        total = total + dot_nt(d_line.astype(BF), q_to_k(head))
    dqk_ref[...] = total


def back_join_kernel(order, pabs_ref, lab_ref, dqk_ref, dv_ref, dvconv_ref, dgate_ref, came_ref, out_ref):
    packed = pabs_ref[:, 256:384]
    values = pabs_ref[:, 0:128]
    labels = column(lab_ref[...])
    keep = labels == labels[TEAM_ROWS - 1 : TEAM_ROWS]
    lane = iota((TEAM_ROWS, 128), 1)
    d_val = dv_ref[...] + dvconv_ref[...]
    d_qk = dqk_ref[...]
    edge = jnp.where(keep[TEAM_ROWS - 16 :], came_ref[TAIL : TAIL + 16, :].astype(F32), 0.0)
    edge = jnp.concatenate([jnp.zeros((TEAM_ROWS - 16, 128), F32), edge], 0)
    d_val = d_val + edge
    for head in range(2):
        at = head * STATE
        first = KLANE + 16 * head
        d_two = came_ref[at : at + 256, :]
        d_one = came_ref[at + 256 : at + 384, :]
        ext = jnp.where(keep, extended(values, head), jnp.zeros_like(values))
        left = dot_nt(packed, spread(first, 0))
        right = dot_nt(packed, spread(first, 1))
        key_lanes = (lane >= first) & (lane < first + 16)
        line = jnp.where(key_lanes | (lane == ONE), packed, jnp.zeros_like(packed))
        d_ext = dot((left * right).astype(BF), d_two) + dot(line, d_one)
        d_val = d_val + jnp.where(keep & head_lanes(head, TEAM_ROWS), d_ext, 0.0)
        d_outer = dot_nt(ext, d_two) * right
        d_qk = d_qk + dot((d_outer * 2.0).astype(BF), spread(first, 0))
        d_qk = d_qk + jnp.where(key_lanes, dot_nt(ext, d_one), 0.0)
    d_val = d_val.astype(BF)
    d_qk = d_qk.astype(BF)
    for block in range(8):
        start = pl.multiple_of(order[block] * ROWS, ROWS)
        rows = slice(block * ROWS, (block + 1) * ROWS)
        out_ref[pl.ds(start, ROWS), 0:128] = d_val[rows]
        out_ref[pl.ds(start, ROWS), 128:256] = dgate_ref[rows, :]
        out_ref[pl.ds(start, ROWS), 256:384] = d_qk[rows]


def call(kernel, outs, args, ordered, scratch=(), flops=0):
    specs = [pl.BlockSpec(memory_space=pltpu.VMEM) for _ in args]
    if ordered:
        specs[0] = pl.BlockSpec(memory_space=pltpu.SMEM)
    moved = sum(a.size * a.dtype.itemsize for a in args) + sum(o.size * o.dtype.itemsize for o in outs)
    return pl.pallas_call(
        kernel,
        out_shape=tuple(outs),
        in_specs=specs,
        out_specs=tuple(pl.BlockSpec(memory_space=pltpu.VMEM) for _ in outs),
        scratch_shapes=list(scratch),
        cost_estimate=pl.CostEstimate(flops=flops, bytes_accessed=moved, transcendentals=0),
        compiler_params=pltpu.CompilerParams(vmem_limit_bytes=48 * 1024 * 1024),
    )(*args)


def shape(rows, cols, kind):
    return jax.ShapeDtypeStruct((rows, cols), kind)


def exchange(blocks, axes):
    return lax.all_to_all(blocks, axes, 0, 0, tiled=True)


def teams(weight, width):
    return weight.reshape(8, 8, width).transpose(1, 0, 2)


def untie(blocks):
    return blocks.transpose(1, 0, 2).reshape(8, -1)


def scaled(weight, gain):
    return (weight.astype(F32) * gain.astype(F32)[:, None]).astype(BF)


def unit(field):
    scale = lax.rsqrt(jnp.mean(field * field, -1, keepdims=True) + EPSILON)
    return field * scale, scale


def unit_back(field, scale, upstream):
    pull = jnp.mean(field * upstream, -1, keepdims=True)
    return scale * upstream - field * (scale * scale * scale * pull)


def per_device(
    inputs, segments, cotangent, attn_gain, w_query, w_key, w_value, w_conv_gate,
    conv_kernel, w_output, ffn_gain, w_ffn_gate, w_ffn_up, w_ffn_down,
):
    x, core = lax.axis_index("x"), lax.axis_index("core")
    team = x * 2 + core
    block = jnp.arange(8, dtype=jnp.int32)
    order = ((block % 2) ^ core) * 4 + (block // 2 - x) % 4

    pack_1 = jnp.concatenate(
        [
            teams(scaled(w_value, attn_gain), 128),
            teams(scaled(w_conv_gate, attn_gain), 128),
            teams(scaled(w_query, attn_gain), 32),
            teams(scaled(w_key, attn_gain), 32),
            jnp.zeros((8, 8, 64), BF),
        ],
        -1,
    )
    weight_1 = exchange(jnp.tile(pack_1, (16, 1, 1)), AXES).reshape(1024, 384)
    labels_tile = jnp.pad(segments.astype(BF)[None], ((0, 15), (0, 1024 - ROWS)))
    gathered = [inputs, labels_tile]
    gathered = team_gather(jnp.concatenate(gathered, 0)).reshape(8, ROWS + 16, 1024)
    field = gathered[:, :ROWS].reshape(TEAM_ROWS, 1024).astype(F32)
    labels = gathered[:, ROWS, :ROWS].astype(F32)
    labels = jnp.take(labels, order, axis=0).reshape(1, TEAM_ROWS)

    owned = jnp.concatenate(
        [w_output, w_ffn_down, jnp.pad(conv_kernel.reshape(1, 24), ((0, 1), (0, 1000)))], 0
    )
    owned = lax.ppermute(owned, AXES, [(f, (f % 16) * 8 + f // 16) for f in range(128)])
    owned, weight_1 = lax.optimization_barrier((owned, weight_1))
    owned = exchange(jnp.broadcast_to(owned[None], (16, 32, 1024)), GROUP)
    weight_o = owned[:, 0:8].reshape(128, 1024)
    weight_d = jnp.pad(owned[:, 8:30].reshape(352, 1024), ((0, 32), (0, 0)))
    taps = owned[:, 30, :24].reshape(16, 3, 8).transpose(1, 0, 2).reshape(3, 128)
    taps = jnp.pad(taps.astype(F32), ((0, 5), (0, 0)))

    pack_2 = jnp.concatenate(
        [
            jnp.pad(teams(scaled(weight, ffn_gain), 352), ((0, 0), (0, 0), (0, 32)))
            for weight in (w_ffn_gate, w_ffn_up)
        ],
        -1,
    )
    pack_2, _ = lax.optimization_barrier((pack_2, owned))
    weight_2 = exchange(jnp.tile(pack_2, (16, 1, 1)), AXES).reshape(1024, 768)

    act_one = unit(field)[0].astype(BF)
    projected = dot(act_one, weight_1).astype(BF)
    pabs, payload = call(
        state_kernel,
        [shape(TEAM_ROWS, 384, BF), shape(PAYLOAD, 128, BF)],
        (order, projected, labels),
        True,
    )
    came = lax.ppermute(payload, "zh", [(0, 1)])
    (local,) = call(
        local_kernel, [jax.ShapeDtypeStruct((2, TEAM_ROWS, 128), F32)], (pabs, labels), False
    )
    total, mixed = call(
        join_kernel,
        [jax.ShapeDtypeStruct((2, TEAM_ROWS, 128), F32), shape(TEAM_ROWS, 128, BF)],
        (order, pabs, labels, local, came, taps),
        True,
    )
    own_inputs = inputs.astype(F32)
    after_mixer = own_inputs + team_scatter(dot(mixed, weight_o))

    own_two, scale_two = unit(after_mixer)
    act_two = team_gather(own_two.astype(BF))
    cot = team_gather(cotangent)
    gate_up = dot(act_two, weight_2)
    gate_pre, up_proj = gate_up[:, :384], gate_up[:, 384:]
    sigma = jax.nn.sigmoid(gate_pre)
    swish = gate_pre * sigma
    hidden = (swish * up_proj).astype(BF)
    d_hidden = dot_nt(cot, weight_d)
    d_gate = (d_hidden * up_proj * sigma * (1.0 + gate_pre * (1.0 - sigma))).astype(BF)
    d_up = (d_hidden * swish).astype(BF)
    d_pair = jnp.concatenate([d_gate, d_up], 1)
    d_two = team_scatter(dot_nt(d_pair, weight_2))
    own_cot = cotangent.astype(F32)
    d_after = own_cot + unit_back(after_mixer, scale_two, d_two)
    d_branch = team_gather(d_after.astype(BF))
    result = (after_mixer + team_scatter(dot(hidden, weight_d))).astype(BF)
    grad_2 = dot_tn(act_two, d_pair).astype(BF).reshape(128, 8, 768)
    grad_2 = exchange(grad_2, AXES)

    d_mixed = dot_nt(d_branch, weight_o)
    d_ext, d_val_conv, d_gate_c, d_taps, payload_2 = call(
        back_state_kernel,
        [
            jax.ShapeDtypeStruct((2, TEAM_ROWS, 128), BF),
            shape(TEAM_ROWS, 128, F32),
            shape(TEAM_ROWS, 128, BF),
            shape(8, 128, F32),
            shape(PAYLOAD, 128, BF),
        ],
        (order, pabs, labels, total, came, taps, d_mixed),
        True,
        [pltpu.VMEM((TEAM_ROWS, 128), F32)],
    )
    came_2 = lax.ppermute(payload_2, "zh", [(1, 0)])
    d_qk, d_val = call(
        back_local_kernel,
        [shape(TEAM_ROWS, 128, F32), shape(TEAM_ROWS, 128, F32)],
        (pabs, labels, d_ext, came),
        False,
        [pltpu.VMEM((128, TEAM_ROWS), F32)],
    )
    (d_projected,) = call(
        back_join_kernel,
        [shape(TEAM_ROWS, 384, BF)],
        (order, pabs, labels, d_qk, d_val, d_val_conv, d_gate_c, came_2),
        True,
    )
    grad_o = dot_tn(mixed, d_branch).astype(BF).reshape(16, 8, 1024)
    grad_d = dot_tn(hidden, cot).astype(BF)[:352].reshape(16, 22, 1024)
    grad_3 = jnp.concatenate([grad_o, grad_d, jnp.zeros((16, 2, 1024), BF)], 1)
    grad_3, grad_2 = lax.optimization_barrier((grad_3, grad_2))
    grad_3 = exchange(grad_3, GROUP)
    rows_3 = jnp.sum(grad_3.astype(F32), 0)
    rows_3 = lax.ppermute(rows_3, AXES, [((f % 16) * 8 + f // 16, f) for f in range(128)])

    d_one = team_scatter(dot_nt(d_projected, weight_1))
    grad_1 = dot_tn(act_one, d_projected).astype(BF)
    taps_block = jnp.pad(d_taps[:3].T.astype(BF), ((0, 0), (320, 61)))
    mine = lax.dynamic_slice(grad_1, (team * 128, 0), (128, 384)) + taps_block
    grad_1 = lax.dynamic_update_slice(grad_1, mine, (team * 128, 0))
    grad_1, _ = lax.optimization_barrier((grad_1, grad_3))
    grad_1 = exchange(grad_1.reshape(128, 8, 384), AXES)
    _, scale_one = unit(own_inputs)
    d_inputs = (d_after + unit_back(own_inputs, scale_one, d_one)).astype(BF)

    sum_1 = jnp.sum(grad_1.astype(F32).reshape(16, 8, 8, 384), 0)
    raw = (
        untie(sum_1[:, :, 256:288]),
        untie(sum_1[:, :, 288:320]),
        untie(sum_1[:, :, 0:128]),
        untie(sum_1[:, :, 128:256]),
    )
    own = (w_query, w_key, w_value, w_conv_gate)
    grad_gain_one = sum(jnp.sum(w.astype(F32) * r, 1) for w, r in zip(own, raw))
    gain_one = attn_gain.astype(F32)[:, None]
    grads_one = [r * gain_one for r in raw]
    grad_taps = jnp.sum(sum_1[:, :, 320:323], 0).T
    sum_2 = jnp.sum(grad_2.astype(F32).reshape(16, 8, 8, 768), 0)
    raw = (untie(sum_2[:, :, 0:352]), untie(sum_2[:, :, 384:736]))
    own = (w_ffn_gate, w_ffn_up)
    grad_gain_two = sum(jnp.sum(w.astype(F32) * r, 1) for w, r in zip(own, raw))
    gain_two = ffn_gain.astype(F32)[:, None]
    grads_two = [r * gain_two for r in raw]
    return (
        result,
        d_inputs,
        grad_gain_one,
        grads_one[0],
        grads_one[1],
        grads_one[2],
        grads_one[3],
        grad_taps,
        rows_3[0:8],
        grad_gain_two,
        grads_two[0],
        grads_two[1],
        rows_3[8:30],
    )


def solution(mesh):
    fine = Mesh(mesh.devices.reshape(SIZES), AXES)
    row, vector, taps = P(AXES, None), P(AXES), P(None, AXES)
    return jax.shard_map(
        per_device,
        mesh=fine,
        in_specs=(row, vector, row, vector, row, row, row, row, taps, row, vector, row, row, row),
        out_specs=(row, row, vector, row, row, row, row, taps, row, vector, row, row, row),
        check_vma=False,
    )
```

```python
import functools

import jax
import jax.numpy as jnp
from jax import lax
from jax.experimental import pallas as pl
from jax.experimental.pallas import tpu as pltpu
from jax.sharding import Mesh, PartitionSpec as P

EPSILON = 1e-05
BF = jnp.bfloat16
F32 = jnp.float32

AXES = ("zl", "y", "zh", "x", "core")
SIZES = (2, 4, 2, 4, 2)
GROUP = ("zl", "y", "zh")
TEAM = ("x", "core")
ROWS = 128
BLOCK = 144
TEAM_ROWS = 1024
TILE = 256
KLANE = 32
ONE = 64
STATE = 384
TAIL = 2 * STATE
PAYLOAD = TAIL + 32
MIB = 1024 * 1024
TIMES = {
    "pack_kernel": 2,
    "block_kernel": 1,
    "spread_mixer_kernel": 1.2,
    "state_kernel": 0.2,
    "local_kernel": 0.2,
    "join_kernel": 2.6,
    "mix_sum_kernel": 1,
    "spread_ffn_kernel": 1.8,
    "norm_kernel": 1,
    "ffn_weights_kernel": 3,
    "ffn_kernel": 3.8,
    "add_kernel": 0.3,
    "ffn_grad_kernel": 4.2,
    "norm_back_kernel": 1,
    "norm_mid_kernel": 30,
    "send_kernel": 0.7,
    "back_state_kernel": 0.2,
    "back_local_kernel": 0.2,
    "back_join_kernel": 0.2,
    "mixer_grad_kernel": 0.2,
    "back_sum_kernel": 1.6,
    "sum_ffn_kernel": 2,
    "sum_mixer_kernel": 0.8,
    "result_kernel": 0.8,
    "owner_kernel": 2,
}


def from_x(block, hop):
    return lax.ppermute(block, "x", [(i, (i - hop) % 4) for i in range(4)])


def to_x(block, hop):
    return lax.ppermute(block, "x", [(i, (i + hop) % 4) for i in range(4)])


def swap_core(block):
    return lax.ppermute(block, "core", [(0, 1), (1, 0)])


def own_gather(block):
    return [block] + [from_x(block, hop) for hop in (1, 2, 3)]


def other_gather(own):
    return [swap_core(part) for part in own]


def own_scatter(pieces):
    return [to_x(piece, hop) for hop, piece in zip((1, 2, 3), pieces)]


def tie(value, *before):
    return lax.optimization_barrier((value,) + before)[0]


def tie_all(values, *before):
    return list(lax.optimization_barrier((*values, *before)))[: len(values)]


def dot(left, right):
    return jnp.dot(left, right, preferred_element_type=F32)


def dot_nt(left, right):
    return lax.dot_general(left, right, (((1,), (1,)), ((), ())), preferred_element_type=F32)


def dot_tn(left, right):
    return lax.dot_general(left, right, (((0,), (0,)), ((), ())), preferred_element_type=F32)


def iota(shape, dim):
    return lax.broadcasted_iota(jnp.int32, shape, dim)


def one_hot(condition):
    return jnp.where(condition, 1.0, 0.0).astype(BF)


def spread(first, which):
    row, lane = iota((256, 128), 0), iota((256, 128), 1)
    part = row // 16 if which == 0 else row % 16
    return one_hot(lane == first + part)


def q_to_k(head):
    row, lane = iota((128, 128), 0), iota((128, 128), 1)
    low = 16 * head
    return one_hot((lane == row + KLANE) & (row >= low) & (row < low + 16))


def identity():
    return one_hot(iota((128, 128), 0) == iota((128, 128), 1))


def head_lanes(head, rows):
    lane = iota((rows, 128), 1)
    return lane < 64 if head == 0 else lane >= 64


def one_lane(head):
    return 64 if head == 0 else 0


def extended(values, head):
    rows = values.shape[0]
    lane = iota((rows, 128), 1)
    ones = jnp.where(lane == one_lane(head), 1.0, 0.0).astype(values.dtype)
    return jnp.where(head_lanes(head, rows), values, ones)


def column(labels_row):
    return jnp.transpose(jnp.broadcast_to(labels_row, (128, TEAM_ROWS)))


def shift_down(field, by, head_rows):
    moved = pltpu.roll(field, by, 0)
    row = iota(field.shape, 0)
    for at in range(by):
        moved = jnp.where(row == at, head_rows[at : at + 1], moved)
    return moved


def conv_parts(values, tail, labels, carried):
    back_1 = shift_down(values, 1, tail[15:16])
    back_2 = shift_down(values, 2, tail[14:16])
    carried_2 = jnp.broadcast_to(carried, (2, 128))
    mask_1 = shift_down(labels, 1, carried_2) == labels
    mask_2 = shift_down(labels, 2, carried_2) == labels
    return (
        jnp.where(mask_1, back_1, 0.0),
        jnp.where(mask_2, back_2, 0.0),
        mask_1,
        mask_2,
    )


def tile_mask(labels_col, labels_row, i, j):
    col = labels_col[i * TILE : (i + 1) * TILE]
    col = jnp.concatenate([col] * (TILE // 128), 1)
    row = labels_row[:, j * TILE : (j + 1) * TILE]
    return col == row


def fetch(sources, held, sems):
    copies = [pltpu.make_async_copy(a, b, sems.at[i]) for i, (a, b) in enumerate(zip(sources, held))]
    for copy in copies:
        copy.start()
    for copy in copies:
        copy.wait()


def block_kernel(inputs_ref, labels_ref, after_ref, block_ref, sem):
    block_ref[ROWS:BLOCK, :] = jnp.zeros((BLOCK - ROWS, 1024), BF)
    labels = jnp.broadcast_to(labels_ref[...], (BLOCK - ROWS, ROWS)).astype(F32)
    block_ref[ROWS:BLOCK, 0:ROWS] = labels.astype(BF)
    fetch([inputs_ref], [block_ref.at[0:ROWS]], sem)


def pack_kernel(*refs):
    sources, (team_ref, whole_ref), held, sems = refs[:9], refs[9:11], refs[11:20], refs[20]
    fetch(sources, held, sems)
    wq, wk, wv, wc, wg, wu, wo, wd, small = held
    turned = jnp.transpose(jnp.concatenate([small[...], jnp.zeros((8, 120), F32)], 1))[0:8]
    one, two = turned[:, 0:1], turned[:, 1:2]
    value, gate_c = wv[...].astype(F32) * one, wc[...].astype(F32) * one
    query, key = wq[...].astype(F32) * one, wk[...].astype(F32) * one
    gate, up = wg[...].astype(F32) * two, wu[...].astype(F32) * two
    spare = jnp.concatenate([turned[:, 2:5], jnp.zeros((8, 61), F32)], 1)
    for t in range(8):
        team_ref[t, :, 0:128] = value[:, t * 128 : (t + 1) * 128].astype(BF)
        team_ref[t, :, 128:256] = gate_c[:, t * 128 : (t + 1) * 128].astype(BF)
        narrow = [query[:, t * 32 : (t + 1) * 32], key[:, t * 32 : (t + 1) * 32], spare]
        team_ref[t, :, 256:384] = jnp.concatenate(narrow, 1).astype(BF)
        for first, wide in ((384, gate), (768, up)):
            part = [wide[:, t * 352 : (t + 1) * 352], jnp.zeros((8, 32), F32)]
            team_ref[t, :, first : first + 384] = jnp.concatenate(part, 1).astype(BF)
    out = wo[...].astype(F32)
    down = wd[...].astype(F32)
    rows = [out[:, :512], out[:, 512:], down[:, :512], down[:, 512:], jnp.zeros((4, 512), F32)]
    whole_ref[...] = jnp.concatenate(rows, 0).astype(BF)


def spread_mixer_kernel(mine_ref, whole_ref, out_ref):
    rows = [mine_ref[:, l * 128 : (l + 1) * 128] for l in range(3)]
    rows += [whole_ref[0:16, l * 128 : (l + 1) * 128] for l in range(4)]
    rows = jnp.concatenate(rows, 0)
    for g in range(16):
        out_ref[g] = rows


def spread_ffn_kernel(mine_ref, whole_ref, out_ref):
    rows = [mine_ref[:, 384 + l * 256 : 640 + l * 256] for l in range(3)]
    rows += [whole_ref[16:64, l * 256 : (l + 1) * 256] for l in range(2)]
    rows = jnp.concatenate(rows, 0)
    for g in range(16):
        out_ref[g] = rows


def ffn_weights_kernel(came_ref, two_ref, down_ref):
    down_ref[352:384, :] = jnp.zeros((32, 1024), BF)
    for g in range(16):
        for l in range(3):
            two_ref[g * 64 : (g + 1) * 64, l * 256 : (l + 1) * 256] = came_ref[g, l * 64 : (l + 1) * 64]
    for g in range(0, 16, 8):
        rows = []
        for at in range(g, g + 8):
            part = [came_ref[at, 192 + l * 48 : 240 + l * 48].astype(F32) for l in range(2)]
            rows.append(jnp.concatenate([p[0:22] for p in part] + [p[22:44] for p in part], 1))
        down_ref[g * 22 : (g + 8) * 22, :] = jnp.concatenate(rows, 0).astype(BF)


def state_kernel(order, *refs):
    blocks, came_ref = refs[:8], refs[8]
    act_ref, pabs_ref, pay_ref, lab_ref, taps_ref, w_ref, wo_ref, rel_ref, code_ref = refs[9:]
    for g in range(16):
        for l in range(3):
            w_ref[g * 64 : (g + 1) * 64, l * 128 : (l + 1) * 128] = came_ref[g, l * 64 : (l + 1) * 64]
        part = [came_ref[g, 192 + l * 16 : 208 + l * 16].astype(F32) for l in range(4)]
        rows = jnp.concatenate([p[0:8] for p in part] + [p[8:16] for p in part], 1)
        wo_ref[g * 8 : (g + 1) * 8, :] = rows.astype(BF)
    start = pl.multiple_of(order[8] * 128, 128)
    taps_ref[...] = jnp.transpose(w_ref[pl.ds(start, 128), 256:384].astype(F32))[64:72]
    for place in range(8):
        ref = blocks[place]
        act_ref[place * ROWS : (place + 1) * ROWS, :] = unit(ref[0:ROWS, :].astype(F32))[0].astype(BF)
        code_ref[place : place + 1, :] = ref[ROWS : ROWS + 16, 0:ROWS].astype(F32)[0:1]
    for half in range(2):
        rows = slice(half * 512, (half + 1) * 512)
        rel_ref[rows, :] = dot(act_ref[rows, :], w_ref[...]).astype(BF)
    lane = iota((ROWS, 128), 1)
    for block in range(8):
        rows = slice(block * ROWS, (block + 1) * ROWS)
        start = pl.multiple_of(order[block] * ROWS, ROWS)
        pabs_ref[rows, :] = rel_ref[pl.ds(start, ROWS), :]
        packed = pabs_ref[rows, 256:384]
        packed = jnp.where(lane == ONE, jnp.ones_like(packed), packed)
        pabs_ref[rows, 256:384] = jnp.where(lane > ONE, jnp.zeros_like(packed), packed)
        lab_ref[:, rows] = code_ref[pl.ds(order[block], 1), :]
    packed = pabs_ref[:, 256:384]
    values = pabs_ref[:, 0:128]
    labels = column(lab_ref[...])
    last = labels[TEAM_ROWS - 1 : TEAM_ROWS]
    keep = labels == last
    turned = dot_nt(identity(), packed).astype(BF)
    for head in range(2):
        ext = jnp.where(keep, extended(values, head), jnp.zeros_like(values))
        first = KLANE + 16 * head
        outer = dot_nt(spread(first, 0), packed) * dot_nt(spread(first, 1), packed)
        at = head * STATE
        pay_ref[at : at + 256, :] = dot(outer.astype(BF), ext).astype(BF)
        pay_ref[at + 256 : at + 384, :] = dot(turned, ext).astype(BF)
    tail = jnp.where(keep, values, jnp.zeros_like(values))
    pay_ref[TAIL : TAIL + 16, :] = tail[TEAM_ROWS - 16 :]
    pay_ref[TAIL + 16 : TAIL + 32, :] = jnp.broadcast_to(last + 1.0, (16, 128)).astype(BF)


def local_kernel(pabs_ref, lab_ref, tot_ref):
    packed = pabs_ref[:, 256:384]
    values = pabs_ref[:, 0:128]
    labels_row = lab_ref[...]
    labels = column(labels_row)
    order = iota((TILE, TILE), 0) >= iota((TILE, TILE), 1)
    moved = [dot(packed, q_to_k(head)).astype(BF) for head in range(2)]
    ext = [extended(values, head) for head in range(2)]
    count = TEAM_ROWS // TILE
    for i in range(count):
        rows = slice(i * TILE, (i + 1) * TILE)
        total = [jnp.zeros((TILE, 128), F32) for _ in range(2)]
        for j in range(i + 1):
            cols = slice(j * TILE, (j + 1) * TILE)
            mask = tile_mask(labels, labels_row, i, j)
            if i == j:
                mask = mask & order
            for head in range(2):
                inner = dot_nt(moved[head][rows], packed[cols])
                weight = 1.0 + inner * (0.25 + inner * (1.0 / 32.0))
                weight = jnp.where(mask, weight, 0.0).astype(BF)
                total[head] = total[head] + dot(weight, ext[head][cols])
        for head in range(2):
            tot_ref[head, rows, :] = total[head]


def normalised(total, head):
    lane = iota(total.shape, 1)
    mass = jnp.sum(jnp.where(lane == one_lane(head), total, 0.0), 1, keepdims=True)
    inside = head_lanes(head, total.shape[0])
    attended = jnp.where(inside, total / mass, 0.0)
    mean = jnp.sum(attended * attended, 1, keepdims=True) * (1.0 / 64.0)
    return attended, mass, lax.rsqrt(mean + EPSILON)


def carried_query(packed, head):
    lane = iota(packed.shape, 1)
    moved = dot(packed, q_to_k(head)) * 0.25
    return jnp.where(lane == ONE, 1.0, moved).astype(BF)


def join_kernel(order, pabs_ref, lab_ref, local_ref, came_ref, taps_ref, wo_ref, tot_ref, mixed_ref, *send_refs):
    packed = pabs_ref[:, 256:384]
    values = pabs_ref[:, 0:128].astype(F32)
    labels = column(lab_ref[...])
    carried = came_ref[TAIL + 16 : TAIL + 17, :].astype(F32) - 1.0
    usable = labels == carried
    attn = jnp.zeros((TEAM_ROWS, 128), F32)
    for head in range(2):
        at = head * STATE
        first = 16 * head
        outer = dot_nt(packed, spread(first, 0)) * dot_nt(packed, spread(first, 1))
        brought = dot(outer.astype(BF), came_ref[at : at + 256, :]) * (1.0 / 32.0)
        brought = brought + dot(carried_query(packed, head), came_ref[at + 256 : at + 384, :])
        total = local_ref[head] + jnp.where(usable, brought, 0.0)
        tot_ref[head] = total
        attended, _, scale = normalised(total, head)
        attn = attn + attended * scale
    tail = came_ref[TAIL : TAIL + 16, :].astype(F32)
    back_1, back_2, _, _ = conv_parts(values, tail, labels, carried)
    conv = taps_ref[0:1] * values + taps_ref[1:2] * back_1 + taps_ref[2:3] * back_2
    mixed = (attn + conv * pabs_ref[:, 128:256].astype(F32)).astype(BF)
    for block in range(8):
        start = pl.multiple_of(order[block] * ROWS, ROWS)
        mixed_ref[pl.ds(start, ROWS), :] = mixed[block * ROWS : (block + 1) * ROWS]
    part = dot(mixed_ref[512:, :], wo_ref[...])
    for hop in range(4):
        send_refs[hop][...] = part[hop * ROWS : (hop + 1) * ROWS].astype(BF)


def split_sum(total, got_refs, own_ref, piece_refs):
    own_ref[...] = total(0) + got_refs[0][...].astype(F32)
    for hop in (1, 2, 3):
        piece_refs[hop - 1][...] = (total(hop) + got_refs[hop][...].astype(F32)).astype(BF)


def mix_sum_kernel(left_ref, right_ref, *refs):
    total = dot(left_ref[0:512, :], right_ref[...])
    split_sum(lambda hop: total[hop * ROWS : (hop + 1) * ROWS], refs[:4], refs[4], refs[5:])


def add_kernel(mine_ref, *refs):
    split_sum(lambda hop: mine_ref[hop * ROWS : (hop + 1) * ROWS, :], refs[:4], refs[4], refs[5:])


def back_sum_kernel(left_ref, right_ref, *refs):
    total = dot_nt(left_ref[0:512, :], right_ref[...])
    split_sum(lambda hop: total[hop * ROWS : (hop + 1) * ROWS], refs[:4], refs[4], refs[5:])


def send_kernel(left_ref, right_ref, *send_refs):
    total = dot(left_ref[...], right_ref[...])
    for hop in range(4):
        send_refs[hop][...] = total[hop * ROWS : (hop + 1) * ROWS].astype(BF)


def norm_kernel(field_ref, own_ref, a_ref, b_ref, c_ref, after_ref, act_ref):
    came = a_ref[...].astype(F32) + b_ref[...].astype(F32) + c_ref[...].astype(F32)
    after = field_ref[...].astype(F32) + own_ref[...] + came
    after_ref[...] = after
    act_ref[...] = unit(after)[0].astype(BF)


def result_kernel(after_ref, own_ref, a_ref, b_ref, c_ref, out_ref):
    came = a_ref[...].astype(F32) + b_ref[...].astype(F32) + c_ref[...].astype(F32)
    out_ref[...] = (after_ref[...] + own_ref[...] + came).astype(BF)


def norm_back_kernel(field_ref, base_ref, own_ref, a_ref, b_ref, c_ref, *out_refs):
    upstream = a_ref[...].astype(F32) + b_ref[...].astype(F32) + c_ref[...].astype(F32)
    upstream = upstream + own_ref[...]
    field = field_ref[...].astype(F32)
    total = base_ref[...].astype(F32) + unit_back(field, unit(field)[1], upstream)
    for ref in out_refs:
        ref[...] = total.astype(ref.dtype)


def norm_mid_kernel(*refs):
    norm_back_kernel(*refs)


def ffn_kernel(*refs):
    acts, cots, (w_ref, wd_ref) = refs[0:4], refs[4:8], refs[8:10]
    hidden_ref, pair_ref, part_refs = refs[10], refs[11], refs[12:]
    for at in range(2):
        rows = slice(at * TILE, (at + 1) * TILE)
        act = jnp.concatenate([ref[...] for ref in acts[2 * at : 2 * at + 2]], 0)
        cot = jnp.concatenate([ref[...] for ref in cots[2 * at : 2 * at + 2]], 0)
        both = dot(act, w_ref[...])
        gate, up = both[:, 0:384], both[:, 384:768]
        d_hidden = dot_nt(cot, wd_ref[...])
        sigma = 1.0 / (1.0 + jnp.exp(-gate))
        swish = gate * sigma
        hidden_ref[rows, :] = (swish * up).astype(BF)
        pair_ref[rows, 0:384] = (d_hidden * up * sigma * (1.0 + gate * (1.0 - sigma))).astype(BF)
        pair_ref[rows, 384:768] = (d_hidden * swish).astype(BF)
        part = dot_nt(pair_ref[rows, :], w_ref[...])
        if len(part_refs) == 1:
            part_refs[0][rows, :] = part
        else:
            part_refs[2 * at][...] = part[0:ROWS].astype(BF)
            part_refs[2 * at + 1][...] = part[ROWS:].astype(BF)


def ffn_grad_kernel(*refs):
    acts, cots, (pair_1, pair_2, hid_1, hid_2) = refs[0:8], refs[8:16], refs[16:20]
    out_ref, act_ref, cot_ref, sum_ref = refs[20:]
    for place in range(8):
        rows = slice(place * ROWS, (place + 1) * ROWS)
        act_ref[rows, :] = acts[place][...]
        cot_ref[rows, :] = cots[place][...]
    for at in range(0, 1024, TILE):
        cols = slice(at, at + TILE)
        total = dot_tn(act_ref[0:512, cols], pair_1[...]) + dot_tn(act_ref[512:, cols], pair_2[...])
        for g in range(4):
            for l in range(3):
                part = total[g * 64 : (g + 1) * 64, l * 256 : (l + 1) * 256]
                out_ref[at // 64 + g, l * 64 : (l + 1) * 64] = part.astype(BF)
    for at in range(0, 384, 128):
        cols = slice(at, at + 128)
        total = dot_tn(hid_1[:, cols], cot_ref[0:512, :]) + dot_tn(hid_2[:, cols], cot_ref[512:, :])
        sum_ref[cols, :] = total
    for g in range(16):
        rows = sum_ref[g * 22 : (g + 1) * 22, :]
        for l in range(2):
            left, right = rows[:, l * 256 : (l + 1) * 256], rows[:, 512 + l * 256 : 768 + l * 256]
            part = jnp.concatenate([left, right, jnp.zeros((4, 256), F32)], 0)
            out_ref[g, 192 + l * 48 : 240 + l * 48] = part.astype(BF)


def sum_ffn_kernel(came_ref, two_ref, down_ref):
    total = came_ref[0].astype(F32)
    for g in range(1, 16):
        total = total + came_ref[g].astype(F32)
    two_ref[...] = total[0:192]
    down_ref[...] = total[192:288]


def owner_kernel(*refs):
    sources, (gq, gk, gv, gc, gg, gu, gd, go, d1_ref, d2_ref, dt_ref) = refs[:10], refs[10:21]
    held, sems = refs[21:31], refs[31]
    fetch(sources, held, sems)
    sum_ref, down_ref, out_ref, wq, wk, wv, wc, wg, wu, small = held
    parts = [down_ref[l * 48 : l * 48 + 48] for l in range(2)]
    gd[...] = jnp.concatenate([p[0:22] for p in parts] + [p[22:44] for p in parts], 1)
    parts = [out_ref[l * 16 : l * 16 + 16] for l in range(4)]
    go[...] = jnp.concatenate([p[0:8] for p in parts] + [p[8:16] for p in parts], 1)
    turned = jnp.transpose(jnp.concatenate([small[...], jnp.zeros((8, 120), F32)], 1))[0:8]
    taps = jnp.zeros((8, 128), F32)
    for t in range(8):
        taps = taps + sum_ref[t, :, 256:384]
    dt_ref[...] = jnp.transpose(taps)[64:67, 0:8]
    diagonal = iota((8, 128), 0) == iota((8, 128), 1)
    one, two = turned[:, 0:1], turned[:, 1:2]
    raw = [sum_ref[t] for t in range(8)]
    value = jnp.concatenate([part[:, 0:128] for part in raw], 1)
    gate_c = jnp.concatenate([part[:, 128:256] for part in raw], 1)
    query = jnp.concatenate([part[:, 256:288] for part in raw], 1)
    key = jnp.concatenate([part[:, 288:320] for part in raw], 1)
    gate = jnp.concatenate([part[:, 384:736] for part in raw], 1)
    up = jnp.concatenate([part[:, 768:1120] for part in raw], 1)
    total = jnp.zeros((8, 1), F32)
    for weight, field, out in ((wq, query, gq), (wk, key, gk), (wv, value, gv), (wc, gate_c, gc)):
        total = total + jnp.sum(weight[...].astype(F32) * field, 1, keepdims=True)
        out[...] = field * one
    d1_ref[...] = jnp.sum(jnp.where(diagonal, total, 0.0), 0, keepdims=True)[:, 0:8]
    total = jnp.zeros((8, 1), F32)
    for weight, field, out in ((wg, gate, gg), (wu, up, gu)):
        total = total + jnp.sum(weight[...].astype(F32) * field, 1, keepdims=True)
        out[...] = field * two
    d2_ref[...] = jnp.sum(jnp.where(diagonal, total, 0.0), 0, keepdims=True)[:, 0:8]


def back_state_kernel(order, *refs):
    blocks, (pabs_ref, lab_ref, tot_ref, came_ref, taps_ref, wo_ref) = refs[:8], refs[8:14]
    de_ref, dvconv_ref, dgate_ref, dtaps_ref, pay_ref, dm_ref = refs[14:]
    for place in range(8):
        start = pl.multiple_of(order[9 + place] * ROWS, ROWS)
        dm_ref[pl.ds(start, ROWS), :] = dot_nt(blocks[place][...], wo_ref[...])
    d_mixed = dm_ref[...]
    packed = pabs_ref[:, 256:384]
    values = pabs_ref[:, 0:128].astype(F32)
    labels = column(lab_ref[...])
    carried = came_ref[TAIL + 16 : TAIL + 17, :].astype(F32) - 1.0
    usable = labels == carried
    lane = iota((TEAM_ROWS, 128), 1)
    for head in range(2):
        attended, mass, scale = normalised(tot_ref[head], head)
        d_attn = jnp.where(head_lanes(head, TEAM_ROWS), d_mixed, 0.0)
        pull = jnp.sum(d_attn * attended, 1, keepdims=True) * (1.0 / 64.0)
        d_att = scale * (d_attn - attended * (scale * scale * pull))
        d_mass = -jnp.sum(d_att * attended, 1, keepdims=True) / mass
        d_ext = jnp.where(lane == one_lane(head), d_mass, d_att / mass).astype(BF)
        de_ref[head] = d_ext
        d_ext = jnp.where(usable, d_ext, jnp.zeros_like(d_ext))
        first = 16 * head
        at = head * STATE
        outer = dot_nt(spread(first, 0), packed) * dot_nt(spread(first, 1), packed)
        pay_ref[at : at + 256, :] = (dot(outer.astype(BF), d_ext) * (1.0 / 32.0)).astype(BF)
        turned = dot_nt(identity(), carried_query(packed, head)).astype(BF)
        pay_ref[at + 256 : at + 384, :] = dot(turned, d_ext).astype(BF)
    tail = came_ref[TAIL : TAIL + 16, :].astype(F32)
    back_1, back_2, mask_1, mask_2 = conv_parts(values, tail, labels, carried)
    conv = taps_ref[0:1] * values + taps_ref[1:2] * back_1 + taps_ref[2:3] * back_2
    dgate_ref[...] = (d_mixed * conv).astype(BF)
    d_conv = d_mixed * pabs_ref[:, 128:256].astype(F32)
    row8 = iota((8, 128), 0)
    sums = [jnp.sum(d_conv * part, 0, keepdims=True) for part in (values, back_1, back_2)]
    d_taps = jnp.zeros((8, 128), F32)
    for at in range(3):
        d_taps = jnp.where(row8 == at, sums[at], d_taps)
    dtaps_ref[...] = d_taps
    part_1 = jnp.where(mask_1, taps_ref[1:2] * d_conv, 0.0)
    part_2 = jnp.where(mask_2, taps_ref[2:3] * d_conv, 0.0)
    row = iota((TEAM_ROWS, 128), 0)
    up_1 = jnp.where(row < TEAM_ROWS - 1, pltpu.roll(part_1, TEAM_ROWS - 1, 0), 0.0)
    up_2 = jnp.where(row < TEAM_ROWS - 2, pltpu.roll(part_2, TEAM_ROWS - 2, 0), 0.0)
    dvconv_ref[...] = taps_ref[0:1] * d_conv + up_1 + up_2
    row16 = iota((16, 128), 0)
    edge = jnp.where(row16 == 14, part_2[0:1], 0.0)
    edge = jnp.where(row16 == 15, part_1[0:1] + part_2[1:2], edge)
    pay_ref[TAIL : TAIL + 16, :] = edge.astype(BF)
    pay_ref[TAIL + 16 : TAIL + 32, :] = jnp.zeros((16, 128), BF)


def back_local_kernel(pabs_ref, lab_ref, de_ref, came_ref, dqk_ref, dv_ref, dqt_ref):
    packed = pabs_ref[:, 256:384]
    values = pabs_ref[:, 0:128]
    labels_row = lab_ref[...]
    labels = column(labels_row)
    order = iota((TILE, TILE), 0) <= iota((TILE, TILE), 1)
    moved = [dot(packed, q_to_k(head)).astype(BF) for head in range(2)]
    keys_t = [dot_nt(q_to_k(head), packed).astype(BF) for head in range(2)]
    ext = [extended(values, head) for head in range(2)]
    inside = [head_lanes(head, TILE) for head in range(2)]
    count = TEAM_ROWS // TILE
    dqt_ref[...] = jnp.zeros((128, TEAM_ROWS), F32)
    for j in range(count):
        cols = slice(j * TILE, (j + 1) * TILE)
        d_key = jnp.zeros((TILE, 128), F32)
        d_val = jnp.zeros((TILE, 128), F32)
        for i in range(j, count):
            rows = slice(i * TILE, (i + 1) * TILE)
            mask = tile_mask(labels, labels_row, j, i)
            if i == j:
                mask = mask & order
            for head in range(2):
                d_ext = de_ref[head, rows, :]
                inner = dot_nt(packed[cols], moved[head][rows])
                weight = 1.0 + inner * (0.25 + inner * (1.0 / 32.0))
                weight = jnp.where(mask, weight, 0.0).astype(BF)
                d_weight = dot_nt(ext[head][cols], d_ext)
                d_inner = jnp.where(mask, d_weight * (0.25 + inner * (1.0 / 16.0)), 0.0).astype(BF)
                d_sum = jnp.where(inside[head], d_ext, jnp.zeros_like(d_ext))
                d_val = d_val + dot(weight, d_sum)
                d_key = d_key + dot(d_inner, moved[head][rows])
                dqt_ref[:, rows] += dot(keys_t[head][:, cols], d_inner)
        dqk_ref[cols, :] = d_key
        dv_ref[cols, :] = d_val
    carried = came_ref[TAIL + 16 : TAIL + 17, :].astype(F32) - 1.0
    usable = labels == carried
    total = dqk_ref[...] + jnp.transpose(dqt_ref[...])
    for head in range(2):
        d_ext = de_ref[head]
        d_ext = jnp.where(usable, d_ext, jnp.zeros_like(d_ext))
        at = head * STATE
        first = 16 * head
        d_outer = dot_nt(d_ext, came_ref[at : at + 256, :]) * dot_nt(packed, spread(first, 1))
        total = total + dot((d_outer * (1.0 / 16.0)).astype(BF), spread(first, 0))
        d_line = dot_nt(d_ext, came_ref[at + 256 : at + 384, :]) * 0.25
        total = total + dot_nt(d_line.astype(BF), q_to_k(head))
    dqk_ref[...] = total


def back_join_kernel(order, pabs_ref, lab_ref, dqk_ref, dv_ref, dvconv_ref, dgate_ref, came_ref, w_ref, out_ref, *send_refs):
    packed = pabs_ref[:, 256:384]
    values = pabs_ref[:, 0:128]
    labels = column(lab_ref[...])
    keep = labels == labels[TEAM_ROWS - 1 : TEAM_ROWS]
    lane = iota((TEAM_ROWS, 128), 1)
    d_val = dv_ref[...] + dvconv_ref[...]
    d_qk = dqk_ref[...]
    edge = jnp.where(keep[TEAM_ROWS - 16 :], came_ref[TAIL : TAIL + 16, :].astype(F32), 0.0)
    edge = jnp.concatenate([jnp.zeros((TEAM_ROWS - 16, 128), F32), edge], 0)
    d_val = d_val + edge
    for head in range(2):
        at = head * STATE
        first = KLANE + 16 * head
        d_two = came_ref[at : at + 256, :]
        d_one = came_ref[at + 256 : at + 384, :]
        ext = jnp.where(keep, extended(values, head), jnp.zeros_like(values))
        left = dot_nt(packed, spread(first, 0))
        right = dot_nt(packed, spread(first, 1))
        key_lanes = (lane >= first) & (lane < first + 16)
        line = jnp.where(key_lanes | (lane == ONE), packed, jnp.zeros_like(packed))
        d_ext = dot((left * right).astype(BF), d_two) + dot(line, d_one)
        d_val = d_val + jnp.where(keep & head_lanes(head, TEAM_ROWS), d_ext, 0.0)
        d_outer = dot_nt(ext, d_two) * right
        d_qk = d_qk + dot((d_outer * 2.0).astype(BF), spread(first, 0))
        d_qk = d_qk + jnp.where(key_lanes, dot_nt(ext, d_one), 0.0)
    d_val = d_val.astype(BF)
    d_qk = d_qk.astype(BF)
    for block in range(8):
        start = pl.multiple_of(order[block] * ROWS, ROWS)
        rows = slice(block * ROWS, (block + 1) * ROWS)
        out_ref[pl.ds(start, ROWS), 0:128] = d_val[rows]
        out_ref[pl.ds(start, ROWS), 128:256] = dgate_ref[rows, :]
        out_ref[pl.ds(start, ROWS), 256:384] = d_qk[rows]
    part = dot_nt(out_ref[512:, :], w_ref[...])
    for hop in range(4):
        send_refs[hop][...] = part[hop * ROWS : (hop + 1) * ROWS].astype(BF)


def mixer_grad_kernel(order, *refs):
    blocks, (mixed_ref, dtaps_ref, act_ref, dp_ref) = refs[:8], refs[8:12]
    grad_ref, sum_ref = refs[12:]
    for at in range(0, 1024, TILE):
        sum_ref[at : at + TILE, :] = dot_tn(act_ref[:, at : at + TILE], dp_ref[...])
    start = pl.multiple_of(order[8] * 128, 128)
    spare = [jnp.zeros((64, 128), F32), dtaps_ref[...], jnp.zeros((56, 128), F32)]
    sum_ref[pl.ds(start, 128), 256:384] += jnp.transpose(jnp.concatenate(spare, 0))
    d_out = jnp.zeros((128, 1024), F32)
    for place in range(8):
        rows = slice(place * ROWS, (place + 1) * ROWS)
        d_out = d_out + dot_tn(mixed_ref[rows, :], blocks[place][...])
    for g in range(16):
        for l in range(3):
            part = sum_ref[g * 64 : (g + 1) * 64, l * 128 : (l + 1) * 128]
            grad_ref[g, l * 64 : (l + 1) * 64] = part.astype(BF)
        rows = d_out[g * 8 : (g + 1) * 8]
        for l in range(4):
            part = [rows[:, l * 128 : (l + 1) * 128], rows[:, 512 + l * 128 : 640 + l * 128]]
            grad_ref[g, 192 + l * 16 : 208 + l * 16] = jnp.concatenate(part, 0).astype(BF)


def sum_mixer_kernel(came_ref, other_ref, sum_ref, out_ref):
    total = came_ref[0].astype(F32)
    for g in range(1, 16):
        total = total + came_ref[g].astype(F32)
    for l in range(3):
        for t in range(8):
            rows = slice(l * 64 + t * 8, l * 64 + t * 8 + 8)
            sum_ref[t, :, l * 128 : (l + 1) * 128] = total[rows]
            sum_ref[t, :, 384 + l * 256 : 640 + l * 256] = other_ref[rows, :]
    out_ref[...] = total[192:256]


def call(kernel, outs, args, ordered=False, scratch=(), anywhere=0, last_anywhere=0, grant=16):
    specs = [pl.BlockSpec(memory_space=pl.ANY)] * anywhere
    specs += [pl.BlockSpec(memory_space=pltpu.VMEM) for _ in args[anywhere:]]
    if last_anywhere:
        specs[-1] = pl.BlockSpec(memory_space=pl.ANY)
    if ordered:
        specs[0] = pl.BlockSpec(memory_space=pltpu.SMEM)
    micros = TIMES[kernel.__name__]
    return pl.pallas_call(
        kernel,
        out_shape=tuple(outs),
        in_specs=specs,
        out_specs=tuple(pl.BlockSpec(memory_space=pltpu.VMEM) for _ in outs),
        scratch_shapes=list(scratch),
        cost_estimate=pl.CostEstimate(
            flops=int(micros * 1.15e9), bytes_accessed=int(micros * 3.6e6), transcendentals=0
        ),
        compiler_params=pltpu.CompilerParams(vmem_limit_bytes=grant * MIB),
    )(*args)


def shape(*sizes):
    return jax.ShapeDtypeStruct(sizes[:-1], sizes[-1])


def exchange(blocks, axes):
    return lax.all_to_all(blocks, axes, 0, 0, tiled=True)


def unit(field):
    scale = lax.rsqrt(jnp.mean(field * field, -1, keepdims=True) + EPSILON)
    return field * scale, scale


def unit_back(field, scale, upstream):
    pull = jnp.mean(field * upstream, -1, keepdims=True)
    return scale * upstream - field * (scale * scale * scale * pull)


def per_device(
    inputs, segments, cotangent, attn_gain, w_query, w_key, w_value, w_conv_gate,
    conv_kernel, w_output, ffn_gain, w_ffn_gate, w_ffn_up, w_ffn_down,
):
    x, core = lax.axis_index("x"), lax.axis_index("core")
    block = jnp.arange(8, dtype=jnp.int32)
    order = ((block % 2) ^ core) * 4 + (block // 2 - x) % 4
    back = 2 * ((block % 4 + x) % 4) + ((block // 4) ^ core)
    order = jnp.concatenate([order, jnp.full((1,), x * 2 + core, jnp.int32), back])
    small = jnp.concatenate([attn_gain[None], ffn_gain[None], conv_kernel], 0).astype(F32)
    small = jnp.pad(small, ((0, 3), (0, 0)))
    to_team = [(f, (f % 16) * 8 + f // 16) for f in range(128)]
    to_owner = [(place, f) for f, place in to_team]

    def held(arrays):
        return [pltpu.VMEM(a.shape, a.dtype) for a in arrays]

    weights = (
        w_query, w_key, w_value, w_conv_gate, w_ffn_gate, w_ffn_up, w_output, w_ffn_down, small,
    )
    pack, whole = call(
        pack_kernel,
        [shape(8, 8, 1152, BF), shape(64, 512, BF)],
        weights,
        scratch=held(weights) + [pltpu.SemaphoreType.DMA((9,))],
        anywhere=9,
        grant=60,
    )
    mine = exchange(pack, TEAM).reshape(64, 1152)
    whole = lax.ppermute(whole, AXES, to_team)
    (tiles,) = call(spread_mixer_kernel, [shape(16, 256, 128, BF)], (mine, whole))
    mixer_came = exchange(tiles, GROUP)

    (block,) = call(
        block_kernel,
        [shape(BLOCK, 1024, BF)],
        (inputs, segments[None], pack),
        scratch=[pltpu.SemaphoreType.DMA((1,))],
        anywhere=1,
        last_anywhere=1,
    )
    own_x = own_gather(block)
    other_x = other_gather(own_x)
    own_cot = own_gather(tie(cotangent, *own_x[1:]))
    other_cot = other_gather(own_cot)

    act_one, pabs, payload, labels, taps, weight_1, weight_o = call(
        state_kernel,
        [
            shape(TEAM_ROWS, 1024, BF),
            shape(TEAM_ROWS, 384, BF),
            shape(PAYLOAD, 128, BF),
            shape(1, TEAM_ROWS, F32),
            shape(8, 128, F32),
            shape(1024, 384, BF),
            shape(128, 1024, BF),
        ],
        (order, *own_x, *other_x, mixer_came),
        True,
        [pltpu.VMEM((TEAM_ROWS, 384), BF), pltpu.VMEM((8, 128), F32)],
    )
    came = lax.ppermute(payload, "zh", [(0, 1)])
    (local,) = call(local_kernel, [shape(2, TEAM_ROWS, 128, F32)], (pabs, labels))
    rows_f, rows_b = shape(ROWS, 1024, F32), shape(ROWS, 1024, BF)
    total, mixed, *sends = call(
        join_kernel,
        [shape(2, TEAM_ROWS, 128, F32), shape(TEAM_ROWS, 128, BF)] + [rows_b] * 4,
        (order, pabs, labels, local, tie(came, *own_cot[1:]), taps, weight_o),
        True,
    )
    pieces = [rows_f] + [rows_b] * 3
    got = other_gather(sends)
    own, *rest = call(mix_sum_kernel, pieces, (mixed, weight_o, *got))
    (tiles,) = call(spread_ffn_kernel, [shape(16, 288, 256, BF)], (tie(mine, mixer_came), whole))
    ffn_came = exchange(tie(tiles, came), GROUP)
    after_mixer, own_two = call(norm_kernel, [rows_f, rows_b], (inputs, own, *own_scatter(rest)))
    own_act = own_gather(own_two)
    weight_2, weight_d = call(
        ffn_weights_kernel,
        [shape(1024, 768, BF), shape(384, 1024, BF)],
        (tie(ffn_came, own_act[1]),),
        grant=60,
    )
    other_act = other_gather(own_act)

    def ffn(acts, blocks, parts):
        return call(
            ffn_kernel,
            [shape(512, 384, BF), shape(512, 768, BF)] + parts,
            (*acts, *blocks, weight_2, weight_d),
        )

    other_hidden, other_pair, *sends = ffn(other_act, other_cot, [rows_b] * 4)
    got = other_gather(sends)
    own_hidden, own_pair, part = ffn(own_act, own_cot, [shape(512, 1024, F32)])
    own, *rest = call(add_kernel, pieces, (part, *got))
    (grad_2,) = call(
        ffn_grad_kernel,
        [shape(16, 288, 256, BF)],
        (
            *own_act, *other_act, *own_cot, *tie_all(other_cot, own),
            own_pair, other_pair, own_hidden, other_hidden,
        ),
        scratch=[
            pltpu.VMEM((1024, 1024), BF),
            pltpu.VMEM((1024, 1024), BF),
            pltpu.VMEM((384, 1024), F32),
        ],
    )
    two_came = own_scatter(rest)
    d_after, own_branch = call(
        norm_mid_kernel, [rows_f, rows_b], (after_mixer, cotangent, own, *two_came)
    )
    own_branch = tie(own_branch, grad_2)
    grad_2 = exchange(grad_2, GROUP)
    sends = call(send_kernel, [rows_b] * 4, (tie(other_hidden, own_branch), weight_d))
    got = other_gather(sends)
    own_branch = own_gather(own_branch)
    d_branch = (*own_branch, *other_gather(own_branch))
    result_own, *rest = call(mix_sum_kernel, pieces, (own_hidden, weight_d, *got))
    result_came = own_scatter(tie_all(rest, *own_branch))

    d_ext, d_val_conv, d_gate_c, d_taps, payload = call(
        back_state_kernel,
        [
            shape(2, TEAM_ROWS, 128, BF),
            shape(TEAM_ROWS, 128, F32),
            shape(TEAM_ROWS, 128, BF),
            shape(8, 128, F32),
            shape(PAYLOAD, 128, BF),
        ],
        (order, *d_branch, pabs, labels, total, came, taps, weight_o),
        True,
        [pltpu.VMEM((TEAM_ROWS, 128), F32)],
    )
    came_2 = lax.ppermute(payload, "zh", [(1, 0)])
    d_qk, d_val = call(
        back_local_kernel,
        [shape(TEAM_ROWS, 128, F32), shape(TEAM_ROWS, 128, F32)],
        (pabs, labels, d_ext, came),
        scratch=[pltpu.VMEM((128, TEAM_ROWS), F32)],
    )
    d_projected, *sends = call(
        back_join_kernel,
        [shape(TEAM_ROWS, 384, BF)] + [rows_b] * 4,
        (
            order, pabs, labels, d_qk, d_val, d_val_conv, d_gate_c, tie(came_2, *result_came),
            weight_1,
        ),
        True,
    )
    got = other_gather(sends)
    (grad_1,) = call(
        mixer_grad_kernel,
        [shape(16, 256, 128, BF)],
        (order, *d_branch, mixed, d_taps, act_one, d_projected),
        True,
        [pltpu.VMEM((TEAM_ROWS, 384), F32)],
    )
    sum_2, sum_d = call(
        sum_ffn_kernel, [shape(192, 256, F32), shape(96, 256, F32)], (grad_2,)
    )
    own, *rest = call(back_sum_kernel, pieces, (d_projected, weight_1, *got))
    grad_1 = exchange(tie(grad_1, grad_2), GROUP)
    last = own_scatter(rest)
    grad_1 = tie(grad_1, last[0])
    (d_inputs,) = call(norm_back_kernel, [rows_b], (inputs, d_after, own, *last))
    (result,) = call(result_kernel, [rows_b], (after_mixer, result_own, *result_came))

    sum_d = lax.ppermute(sum_d, AXES, to_owner)
    sums, sum_o = call(
        sum_mixer_kernel, [shape(8, 8, 1152, F32), shape(64, 128, F32)], (grad_1, sum_2)
    )
    sum_o = lax.ppermute(sum_o, AXES, to_owner)
    sums = exchange(sums, TEAM)
    gq, gk, gv, gc, gg, gu, gd, go, gain_grad_1, gain_grad_2, grad_taps = call(
        owner_kernel,
        [shape(8, cols, F32) for cols in (256, 256, 1024, 1024, 2816, 2816)]
        + [shape(22, 1024, F32), shape(8, 1024, F32)]
        + [shape(1, 8, F32), shape(1, 8, F32), shape(3, 8, F32)],
        (sums, sum_d, sum_o, *weights[:6], small),
        scratch=held((sums, sum_d, sum_o, *weights[:6], small)) + [pltpu.SemaphoreType.DMA((10,))],
        anywhere=10,
        grant=60,
    )
    return (
        result, d_inputs, gain_grad_1[0], gq, gk, gv, gc, grad_taps, go,
        gain_grad_2[0], gg, gu, gd,
    )


def solution(mesh):
    fine = Mesh(mesh.devices.reshape(SIZES), AXES)
    row, vector, taps = P(AXES, None), P(AXES), P(None, AXES)
    return jax.shard_map(
        per_device,
        mesh=fine,
        in_specs=(row, vector, row, vector, row, row, row, row, taps, row, vector, row, row, row),
        out_specs=(row, row, vector, row, row, row, row, taps, row, vector, row, row, row),
        check_vma=False,
    )
```

```python
import functools

import jax
import jax.numpy as jnp
from jax import lax
from jax.experimental import pallas as pl
from jax.experimental.pallas import tpu as pltpu
from jax.sharding import Mesh, PartitionSpec as P

EPSILON = 1e-05
BF = jnp.bfloat16
F32 = jnp.float32

AXES = ("zl", "y", "zh", "x", "core")
SIZES = (2, 4, 2, 4, 2)
GROUP = ("zl", "y", "zh")
TEAM = ("x", "core")
ROWS = 128
COT = 144
BLOCK = 272
TEAM_ROWS = 1024
TILE = 256
KLANE = 32
ONE = 64
STATE = 384
TAIL = 2 * STATE
PAYLOAD = TAIL + 32
MIB = 1024 * 1024
TIMES = {
    "pack_kernel": 2,
    "turn_kernel": 1.5,
    "block_kernel": 1,
    "spread_mixer_kernel": 1.2,
    "state_kernel": 0.2,
    "act_kernel": 14,
    "local_kernel": 0.2,
    "join_kernel": 2.6,
    "mix_sum_kernel": 1,
    "spread_ffn_kernel": 1.8,
    "norm_kernel": 1,
    "ffn_weights_kernel": 3,
    "ffn_own_kernel": 3.8,
    "ffn_other_kernel": 3.8,
    "add_kernel": 0.3,
    "ffn_grad_kernel": 4.2,
    "norm_back_kernel": 1,
    "norm_mid_kernel": 30,
    "send_kernel": 0.7,
    "back_state_kernel": 0.2,
    "back_local_kernel": 0.2,
    "back_join_kernel": 0.2,
    "mixer_grad_kernel": 0.2,
    "back_sum_kernel": 1.6,
    "sum_ffn_kernel": 2,
    "sum_mixer_kernel": 0.8,
    "result_kernel": 0.8,
    "owner_kernel": 2,
}


def from_x(block, hop):
    return lax.ppermute(block, "x", [(i, (i - hop) % 4) for i in range(4)])


def to_x(block, hop):
    return lax.ppermute(block, "x", [(i, (i + hop) % 4) for i in range(4)])


def swap_core(block):
    return lax.ppermute(block, "core", [(0, 1), (1, 0)])


def own_gather(block):
    return [block] + [from_x(block, hop) for hop in (1, 2, 3)]


def other_gather(own):
    return [swap_core(part) for part in (tie(own[0], own[1]), *own[1:])]


def swap_all(parts):
    return [swap_core(part) for part in parts]


def own_scatter(pieces):
    return [to_x(piece, hop) for hop, piece in zip((1, 2, 3), pieces)]


def tie(value, *before):
    return lax.optimization_barrier((value,) + before)[0]


def tie_all(values, *before):
    return list(lax.optimization_barrier((*values, *before)))[: len(values)]


def dot(left, right):
    return jnp.dot(left, right, preferred_element_type=F32)


def dot_nt(left, right):
    return lax.dot_general(left, right, (((1,), (1,)), ((), ())), preferred_element_type=F32)


def dot_tn(left, right):
    return lax.dot_general(left, right, (((0,), (0,)), ((), ())), preferred_element_type=F32)


def iota(shape, dim):
    return lax.broadcasted_iota(jnp.int32, shape, dim)


def one_hot(condition):
    return jnp.where(condition, 1.0, 0.0).astype(BF)


def spread(first, which):
    row, lane = iota((256, 128), 0), iota((256, 128), 1)
    part = row // 16 if which == 0 else row % 16
    return one_hot(lane == first + part)


def q_to_k(head):
    row, lane = iota((128, 128), 0), iota((128, 128), 1)
    low = 16 * head
    return one_hot((lane == row + KLANE) & (row >= low) & (row < low + 16))


def identity():
    return one_hot(iota((128, 128), 0) == iota((128, 128), 1))


def head_lanes(head, rows):
    lane = iota((rows, 128), 1)
    return lane < 64 if head == 0 else lane >= 64


def one_lane(head):
    return 64 if head == 0 else 0


def extended(values, head):
    rows = values.shape[0]
    lane = iota((rows, 128), 1)
    ones = jnp.where(lane == one_lane(head), 1.0, 0.0).astype(values.dtype)
    return jnp.where(head_lanes(head, rows), values, ones)


def column(labels_row):
    return jnp.transpose(jnp.broadcast_to(labels_row, (128, TEAM_ROWS)))


def shift_down(field, by, head_rows):
    moved = pltpu.roll(field, by, 0)
    row = iota(field.shape, 0)
    for at in range(by):
        moved = jnp.where(row == at, head_rows[at : at + 1], moved)
    return moved


def conv_parts(values, tail, labels, carried):
    back_1 = shift_down(values, 1, tail[15:16])
    back_2 = shift_down(values, 2, tail[14:16])
    carried_2 = jnp.broadcast_to(carried, (2, 128))
    mask_1 = shift_down(labels, 1, carried_2) == labels
    mask_2 = shift_down(labels, 2, carried_2) == labels
    return (
        jnp.where(mask_1, back_1, 0.0),
        jnp.where(mask_2, back_2, 0.0),
        mask_1,
        mask_2,
    )


def tile_mask(labels_col, labels_row, i, j):
    col = labels_col[i * TILE : (i + 1) * TILE]
    col = jnp.concatenate([col] * (TILE // 128), 1)
    row = labels_row[:, j * TILE : (j + 1) * TILE]
    return col == row


def block_kernel(inputs_ref, cot_ref, labels_ref, block_ref):
    labels = jnp.broadcast_to(labels_ref[...], (COT - ROWS, ROWS)).astype(F32)
    block_ref[0:ROWS, :] = inputs_ref[...]
    block_ref[ROWS:COT, :] = jnp.zeros((COT - ROWS, 1024), BF)
    block_ref[ROWS:COT, 0:ROWS] = labels.astype(BF)
    block_ref[COT:BLOCK, :] = cot_ref[...]


def turn_kernel(field_ref, out_ref):
    for at in range(0, 1024, TILE):
        out_ref[at : at + TILE, :] = jnp.transpose(field_ref[:, at : at + TILE])


def pack_kernel(wq, wk, wv, wc, wg, wu, wo, wd, small, team_ref, whole_ref):
    turned = jnp.transpose(jnp.concatenate([small[...], jnp.zeros((8, 120), F32)], 1))[0:8]
    one, two = turned[:, 0:1], turned[:, 1:2]
    value, gate_c = wv[...].astype(F32) * one, wc[...].astype(F32) * one
    query, key = wq[...].astype(F32) * one, wk[...].astype(F32) * one
    gate, up = wg[...].astype(F32) * two, wu[...].astype(F32) * two
    spare = jnp.concatenate([turned[:, 2:5], jnp.zeros((8, 61), F32)], 1)
    for t in range(8):
        team_ref[t, :, 0:128] = value[:, t * 128 : (t + 1) * 128].astype(BF)
        team_ref[t, :, 128:256] = gate_c[:, t * 128 : (t + 1) * 128].astype(BF)
        narrow = [query[:, t * 32 : (t + 1) * 32], key[:, t * 32 : (t + 1) * 32], spare]
        team_ref[t, :, 256:384] = jnp.concatenate(narrow, 1).astype(BF)
        for first, wide in ((384, gate), (768, up)):
            part = [wide[:, t * 352 : (t + 1) * 352], jnp.zeros((8, 32), F32)]
            team_ref[t, :, first : first + 384] = jnp.concatenate(part, 1).astype(BF)
    out = wo[...].astype(F32)
    down = wd[...].astype(F32)
    rows = [out[:, :512], out[:, 512:], down[:, :512], down[:, 512:], jnp.zeros((4, 512), F32)]
    whole_ref[...] = jnp.concatenate(rows, 0).astype(BF)


def spread_mixer_kernel(mine_ref, whole_ref, out_ref):
    rows = [mine_ref[:, l * 128 : (l + 1) * 128] for l in range(3)]
    rows += [whole_ref[0:16, l * 128 : (l + 1) * 128] for l in range(4)]
    rows = jnp.concatenate(rows, 0)
    for g in range(16):
        out_ref[g] = rows


def spread_ffn_kernel(mine_ref, whole_ref, out_ref):
    rows = [mine_ref[:, 384 + l * 256 : 640 + l * 256] for l in range(3)]
    rows += [whole_ref[16:64, l * 256 : (l + 1) * 256] for l in range(2)]
    rows = jnp.concatenate(rows, 0)
    for g in range(16):
        out_ref[g] = rows


def ffn_weights_kernel(came_ref, two_ref, down_ref):
    down_ref[352:384, :] = jnp.zeros((32, 1024), BF)
    for g in range(16):
        for l in range(3):
            two_ref[g * 64 : (g + 1) * 64, l * 256 : (l + 1) * 256] = came_ref[g, l * 64 : (l + 1) * 64]
    for g in range(0, 16, 8):
        rows = []
        for at in range(g, g + 8):
            part = [came_ref[at, 192 + l * 48 : 240 + l * 48].astype(F32) for l in range(2)]
            rows.append(jnp.concatenate([p[0:22] for p in part] + [p[22:44] for p in part], 1))
        down_ref[g * 22 : (g + 8) * 22, :] = jnp.concatenate(rows, 0).astype(BF)


def act_kernel(*refs):
    blocks, act_ref, code_ref, cot_ref = refs[:8], refs[8], refs[9], refs[10]
    for place in range(8):
        ref = blocks[place]
        rows = slice(place * ROWS, (place + 1) * ROWS)
        act_ref[rows, :] = unit(ref[0:ROWS, :].astype(F32))[0].astype(BF)
        code_ref[place : place + 1, :] = ref[ROWS:COT, 0:ROWS].astype(F32)[0:1]
        cot_ref[rows, :] = ref[COT:BLOCK, :]


def state_kernel(
    order, act_ref, code_ref, came_ref, pabs_ref, pay_ref, lab_ref, taps_ref, w_ref, wo_ref, rel_ref
):
    for g in range(16):
        for l in range(3):
            w_ref[g * 64 : (g + 1) * 64, l * 128 : (l + 1) * 128] = came_ref[g, l * 64 : (l + 1) * 64]
        part = [came_ref[g, 192 + l * 16 : 208 + l * 16].astype(F32) for l in range(4)]
        rows = jnp.concatenate([p[0:8] for p in part] + [p[8:16] for p in part], 1)
        wo_ref[g * 8 : (g + 1) * 8, :] = rows.astype(BF)
    start = pl.multiple_of(order[8] * 128, 128)
    taps_ref[...] = jnp.transpose(w_ref[pl.ds(start, 128), 256:384].astype(F32))[64:72]
    for half in range(2):
        rows = slice(half * 512, (half + 1) * 512)
        rel_ref[rows, :] = dot(act_ref[rows, :], w_ref[...]).astype(BF)
    lane = iota((ROWS, 128), 1)
    for block in range(8):
        rows = slice(block * ROWS, (block + 1) * ROWS)
        start = pl.multiple_of(order[block] * ROWS, ROWS)
        pabs_ref[rows, :] = rel_ref[pl.ds(start, ROWS), :]
        packed = pabs_ref[rows, 256:384]
        packed = jnp.where(lane == ONE, jnp.ones_like(packed), packed)
        pabs_ref[rows, 256:384] = jnp.where(lane > ONE, jnp.zeros_like(packed), packed)
        lab_ref[:, rows] = code_ref[pl.ds(order[block], 1), :]
    packed = pabs_ref[:, 256:384]
    values = pabs_ref[:, 0:128]
    labels = column(lab_ref[...])
    last = labels[TEAM_ROWS - 1 : TEAM_ROWS]
    keep = labels == last
    turned = dot_nt(identity(), packed).astype(BF)
    for head in range(2):
        ext = jnp.where(keep, extended(values, head), jnp.zeros_like(values))
        first = KLANE + 16 * head
        outer = dot_nt(spread(first, 0), packed) * dot_nt(spread(first, 1), packed)
        at = head * STATE
        pay_ref[at : at + 256, :] = dot(outer.astype(BF), ext).astype(BF)
        pay_ref[at + 256 : at + 384, :] = dot(turned, ext).astype(BF)
    tail = jnp.where(keep, values, jnp.zeros_like(values))
    pay_ref[TAIL : TAIL + 16, :] = tail[TEAM_ROWS - 16 :]
    pay_ref[TAIL + 16 : TAIL + 32, :] = jnp.broadcast_to(last + 1.0, (16, 128)).astype(BF)


def local_kernel(pabs_ref, lab_ref, tot_ref):
    packed = pabs_ref[:, 256:384]
    values = pabs_ref[:, 0:128]
    labels_row = lab_ref[...]
    labels = column(labels_row)
    order = iota((TILE, TILE), 0) >= iota((TILE, TILE), 1)
    moved = [dot(packed, q_to_k(head)).astype(BF) for head in range(2)]
    ext = [extended(values, head) for head in range(2)]
    count = TEAM_ROWS // TILE
    for i in range(count):
        rows = slice(i * TILE, (i + 1) * TILE)
        total = [jnp.zeros((TILE, 128), F32) for _ in range(2)]
        for j in range(i + 1):
            cols = slice(j * TILE, (j + 1) * TILE)
            mask = tile_mask(labels, labels_row, i, j)
            if i == j:
                mask = mask & order
            for head in range(2):
                inner = dot_nt(moved[head][rows], packed[cols])
                weight = 1.0 + inner * (0.25 + inner * (1.0 / 32.0))
                weight = jnp.where(mask, weight, 0.0).astype(BF)
                total[head] = total[head] + dot(weight, ext[head][cols])
        for head in range(2):
            tot_ref[head, rows, :] = total[head]


def normalised(total, head):
    lane = iota(total.shape, 1)
    mass = jnp.sum(jnp.where(lane == one_lane(head), total, 0.0), 1, keepdims=True)
    inside = head_lanes(head, total.shape[0])
    attended = jnp.where(inside, total / mass, 0.0)
    mean = jnp.sum(attended * attended, 1, keepdims=True) * (1.0 / 64.0)
    return attended, mass, lax.rsqrt(mean + EPSILON)


def carried_query(packed, head):
    lane = iota(packed.shape, 1)
    moved = dot(packed, q_to_k(head)) * 0.25
    return jnp.where(lane == ONE, 1.0, moved).astype(BF)


def join_kernel(order, pabs_ref, lab_ref, local_ref, came_ref, taps_ref, wo_ref, tot_ref, mixed_ref, *send_refs):
    packed = pabs_ref[:, 256:384]
    values = pabs_ref[:, 0:128].astype(F32)
    labels = column(lab_ref[...])
    carried = came_ref[TAIL + 16 : TAIL + 17, :].astype(F32) - 1.0
    usable = labels == carried
    attn = jnp.zeros((TEAM_ROWS, 128), F32)
    for head in range(2):
        at = head * STATE
        first = 16 * head
        outer = dot_nt(packed, spread(first, 0)) * dot_nt(packed, spread(first, 1))
        brought = dot(outer.astype(BF), came_ref[at : at + 256, :]) * (1.0 / 32.0)
        brought = brought + dot(carried_query(packed, head), came_ref[at + 256 : at + 384, :])
        total = local_ref[head] + jnp.where(usable, brought, 0.0)
        tot_ref[head] = total
        attended, _, scale = normalised(total, head)
        attn = attn + attended * scale
    tail = came_ref[TAIL : TAIL + 16, :].astype(F32)
    back_1, back_2, _, _ = conv_parts(values, tail, labels, carried)
    conv = taps_ref[0:1] * values + taps_ref[1:2] * back_1 + taps_ref[2:3] * back_2
    mixed = (attn + conv * pabs_ref[:, 128:256].astype(F32)).astype(BF)
    for block in range(8):
        start = pl.multiple_of(order[block] * ROWS, ROWS)
        mixed_ref[pl.ds(start, ROWS), :] = mixed[block * ROWS : (block + 1) * ROWS]
    part = dot(mixed_ref[512:, :], wo_ref[...])
    for hop in range(4):
        send_refs[hop][...] = part[hop * ROWS : (hop + 1) * ROWS].astype(BF)


def split_sum(total, got_refs, own_ref, piece_refs):
    own_ref[...] = total(0) + got_refs[0][...].astype(F32)
    for hop in (1, 2, 3):
        piece_refs[hop - 1][...] = (total(hop) + got_refs[hop][...].astype(F32)).astype(BF)


def mix_sum_kernel(left_ref, right_ref, *refs):
    total = dot(left_ref[0:512, :], right_ref[...])
    split_sum(lambda hop: total[hop * ROWS : (hop + 1) * ROWS], refs[:4], refs[4], refs[5:])


def add_kernel(mine_ref, *refs):
    split_sum(lambda hop: mine_ref[hop * ROWS : (hop + 1) * ROWS, :], refs[:4], refs[4], refs[5:])


def back_sum_kernel(left_ref, right_ref, *refs):
    total = dot_nt(left_ref[0:512, :], right_ref[...])
    split_sum(lambda hop: total[hop * ROWS : (hop + 1) * ROWS], refs[:4], refs[4], refs[5:])


def send_kernel(left_ref, right_ref, *send_refs):
    total = dot(left_ref[...], right_ref[...])
    for hop in range(4):
        send_refs[hop][...] = total[hop * ROWS : (hop + 1) * ROWS].astype(BF)


def norm_kernel(field_ref, own_ref, a_ref, b_ref, c_ref, after_ref, act_ref):
    came = a_ref[...].astype(F32) + b_ref[...].astype(F32) + c_ref[...].astype(F32)
    after = field_ref[...].astype(F32) + own_ref[...] + came
    after_ref[...] = after
    act_ref[...] = unit(after)[0].astype(BF)


def result_kernel(after_ref, own_ref, a_ref, b_ref, c_ref, out_ref):
    came = a_ref[...].astype(F32) + b_ref[...].astype(F32) + c_ref[...].astype(F32)
    out_ref[...] = (after_ref[...] + own_ref[...] + came).astype(BF)


def norm_back_kernel(field_ref, base_ref, own_ref, a_ref, b_ref, c_ref, *out_refs):
    upstream = a_ref[...].astype(F32) + b_ref[...].astype(F32) + c_ref[...].astype(F32)
    upstream = upstream + own_ref[...]
    field = field_ref[...].astype(F32)
    total = base_ref[...].astype(F32) + unit_back(field, unit(field)[1], upstream)
    for ref in out_refs:
        ref[...] = total.astype(ref.dtype)


def norm_mid_kernel(*refs):
    norm_back_kernel(*refs)


def ffn_own_kernel(*refs):
    ffn_kernel(*refs, half=0)


def ffn_other_kernel(*refs):
    ffn_kernel(*refs, half=1)


def ffn_kernel(*refs, half):
    acts, (cot_ref, w_ref, wd_ref) = refs[0:4], refs[4:7]
    hidden_ref, pair_ref, part_refs = refs[7], refs[8], refs[9:]
    for at in range(2):
        rows = slice(at * TILE, (at + 1) * TILE)
        act = jnp.concatenate([ref[...] for ref in acts[2 * at : 2 * at + 2]], 0)
        both = dot(act, w_ref[...])
        gate, up = both[:, 0:384], both[:, 384:768]
        d_hidden = dot_nt(cot_ref[half * 512 + at * TILE : half * 512 + (at + 1) * TILE, :], wd_ref[...])
        sigma = 1.0 / (1.0 + jnp.exp(-gate))
        swish = gate * sigma
        hidden_ref[rows, :] = (swish * up).astype(BF)
        pair_ref[rows, 0:384] = (d_hidden * up * sigma * (1.0 + gate * (1.0 - sigma))).astype(BF)
        pair_ref[rows, 384:768] = (d_hidden * swish).astype(BF)
        part = dot_nt(pair_ref[rows, :], w_ref[...])
        if len(part_refs) == 1:
            part_refs[0][rows, :] = part
        else:
            part_refs[2 * at][...] = part[0:ROWS].astype(BF)
            part_refs[2 * at + 1][...] = part[ROWS:].astype(BF)


def ffn_grad_kernel(*refs):
    acts, (cot_ref, pair_1, pair_2, hid_1, hid_2) = refs[0:8], refs[8:13]
    out_ref, act_ref, sum_ref = refs[13:]
    for place in range(8):
        act_ref[place * ROWS : (place + 1) * ROWS, :] = acts[place][...]
    for at in range(0, 1024, TILE):
        cols = slice(at, at + TILE)
        total = dot_tn(act_ref[0:512, cols], pair_1[...]) + dot_tn(act_ref[512:, cols], pair_2[...])
        for g in range(4):
            for l in range(3):
                part = total[g * 64 : (g + 1) * 64, l * 256 : (l + 1) * 256]
                out_ref[at // 64 + g, l * 64 : (l + 1) * 64] = part.astype(BF)
    for at in range(0, 384, 128):
        cols = slice(at, at + 128)
        total = dot_tn(hid_1[:, cols], cot_ref[0:512, :]) + dot_tn(hid_2[:, cols], cot_ref[512:, :])
        sum_ref[cols, :] = total
    for g in range(16):
        rows = sum_ref[g * 22 : (g + 1) * 22, :]
        for l in range(2):
            left, right = rows[:, l * 256 : (l + 1) * 256], rows[:, 512 + l * 256 : 768 + l * 256]
            part = jnp.concatenate([left, right, jnp.zeros((4, 256), F32)], 0)
            out_ref[g, 192 + l * 48 : 240 + l * 48] = part.astype(BF)


def sum_ffn_kernel(came_ref, two_ref, down_ref):
    total = came_ref[0].astype(F32)
    for g in range(1, 16):
        total = total + came_ref[g].astype(F32)
    two_ref[...] = total[0:192]
    down_ref[...] = total[192:288]


def owner_kernel(*refs):
    sum_ref, down_ref, out_ref, wq, wk, wv, wc, wg, wu, small = refs[:10]
    gq, gk, gv, gc, gg, gu, gd, go, d1_ref, d2_ref, dt_ref = refs[10:]
    parts = [down_ref[l * 48 : l * 48 + 48] for l in range(2)]
    gd[...] = jnp.concatenate([p[0:22] for p in parts] + [p[22:44] for p in parts], 1)
    parts = [out_ref[l * 16 : l * 16 + 16] for l in range(4)]
    go[...] = jnp.concatenate([p[0:8] for p in parts] + [p[8:16] for p in parts], 1)
    turned = jnp.transpose(jnp.concatenate([small[...], jnp.zeros((8, 120), F32)], 1))[0:8]
    taps = jnp.zeros((8, 128), F32)
    for t in range(8):
        taps = taps + sum_ref[t, :, 256:384]
    dt_ref[...] = jnp.transpose(taps)[64:67, 0:8]
    diagonal = iota((8, 128), 0) == iota((8, 128), 1)
    one, two = turned[:, 0:1], turned[:, 1:2]
    raw = [sum_ref[t] for t in range(8)]
    value = jnp.concatenate([part[:, 0:128] for part in raw], 1)
    gate_c = jnp.concatenate([part[:, 128:256] for part in raw], 1)
    query = jnp.concatenate([part[:, 256:288] for part in raw], 1)
    key = jnp.concatenate([part[:, 288:320] for part in raw], 1)
    gate = jnp.concatenate([part[:, 384:736] for part in raw], 1)
    up = jnp.concatenate([part[:, 768:1120] for part in raw], 1)
    total = jnp.zeros((8, 1), F32)
    for weight, field, out in ((wq, query, gq), (wk, key, gk), (wv, value, gv), (wc, gate_c, gc)):
        total = total + jnp.sum(weight[...].astype(F32) * field, 1, keepdims=True)
        out[...] = field * one
    d1_ref[...] = jnp.sum(jnp.where(diagonal, total, 0.0), 0, keepdims=True)[:, 0:8]
    total = jnp.zeros((8, 1), F32)
    for weight, field, out in ((wg, gate, gg), (wu, up, gu)):
        total = total + jnp.sum(weight[...].astype(F32) * field, 1, keepdims=True)
        out[...] = field * two
    d2_ref[...] = jnp.sum(jnp.where(diagonal, total, 0.0), 0, keepdims=True)[:, 0:8]


def back_state_kernel(order, *refs):
    blocks, (pabs_ref, lab_ref, tot_ref, came_ref, taps_ref, wo_ref) = refs[:8], refs[8:14]
    de_ref, dvconv_ref, dgate_ref, dtaps_ref, pay_ref, dm_ref = refs[14:]
    for place in range(8):
        start = pl.multiple_of(order[9 + place] * ROWS, ROWS)
        dm_ref[pl.ds(start, ROWS), :] = dot_nt(blocks[place][...], wo_ref[...])
    d_mixed = dm_ref[...]
    packed = pabs_ref[:, 256:384]
    values = pabs_ref[:, 0:128].astype(F32)
    labels = column(lab_ref[...])
    carried = came_ref[TAIL + 16 : TAIL + 17, :].astype(F32) - 1.0
    usable = labels == carried
    lane = iota((TEAM_ROWS, 128), 1)
    for head in range(2):
        attended, mass, scale = normalised(tot_ref[head], head)
        d_attn = jnp.where(head_lanes(head, TEAM_ROWS), d_mixed, 0.0)
        pull = jnp.sum(d_attn * attended, 1, keepdims=True) * (1.0 / 64.0)
        d_att = scale * (d_attn - attended * (scale * scale * pull))
        d_mass = -jnp.sum(d_att * attended, 1, keepdims=True) / mass
        d_ext = jnp.where(lane == one_lane(head), d_mass, d_att / mass).astype(BF)
        de_ref[head] = d_ext
        d_ext = jnp.where(usable, d_ext, jnp.zeros_like(d_ext))
        first = 16 * head
        at = head * STATE
        outer = dot_nt(spread(first, 0), packed) * dot_nt(spread(first, 1), packed)
        pay_ref[at : at + 256, :] = (dot(outer.astype(BF), d_ext) * (1.0 / 32.0)).astype(BF)
        turned = dot_nt(identity(), carried_query(packed, head)).astype(BF)
        pay_ref[at + 256 : at + 384, :] = dot(turned, d_ext).astype(BF)
    tail = came_ref[TAIL : TAIL + 16, :].astype(F32)
    back_1, back_2, mask_1, mask_2 = conv_parts(values, tail, labels, carried)
    conv = taps_ref[0:1] * values + taps_ref[1:2] * back_1 + taps_ref[2:3] * back_2
    dgate_ref[...] = (d_mixed * conv).astype(BF)
    d_conv = d_mixed * pabs_ref[:, 128:256].astype(F32)
    row8 = iota((8, 128), 0)
    sums = [jnp.sum(d_conv * part, 0, keepdims=True) for part in (values, back_1, back_2)]
    d_taps = jnp.zeros((8, 128), F32)
    for at in range(3):
        d_taps = jnp.where(row8 == at, sums[at], d_taps)
    dtaps_ref[...] = d_taps
    part_1 = jnp.where(mask_1, taps_ref[1:2] * d_conv, 0.0)
    part_2 = jnp.where(mask_2, taps_ref[2:3] * d_conv, 0.0)
    row = iota((TEAM_ROWS, 128), 0)
    up_1 = jnp.where(row < TEAM_ROWS - 1, pltpu.roll(part_1, TEAM_ROWS - 1, 0), 0.0)
    up_2 = jnp.where(row < TEAM_ROWS - 2, pltpu.roll(part_2, TEAM_ROWS - 2, 0), 0.0)
    dvconv_ref[...] = taps_ref[0:1] * d_conv + up_1 + up_2
    row16 = iota((16, 128), 0)
    edge = jnp.where(row16 == 14, part_2[0:1], 0.0)
    edge = jnp.where(row16 == 15, part_1[0:1] + part_2[1:2], edge)
    pay_ref[TAIL : TAIL + 16, :] = edge.astype(BF)
    pay_ref[TAIL + 16 : TAIL + 32, :] = jnp.zeros((16, 128), BF)


def back_local_kernel(pabs_ref, lab_ref, de_ref, came_ref, dqk_ref, dv_ref, dqt_ref):
    packed = pabs_ref[:, 256:384]
    values = pabs_ref[:, 0:128]
    labels_row = lab_ref[...]
    labels = column(labels_row)
    order = iota((TILE, TILE), 0) <= iota((TILE, TILE), 1)
    moved = [dot(packed, q_to_k(head)).astype(BF) for head in range(2)]
    keys_t = [dot_nt(q_to_k(head), packed).astype(BF) for head in range(2)]
    ext = [extended(values, head) for head in range(2)]
    inside = [head_lanes(head, TILE) for head in range(2)]
    count = TEAM_ROWS // TILE
    dqt_ref[...] = jnp.zeros((128, TEAM_ROWS), F32)
    for j in range(count):
        cols = slice(j * TILE, (j + 1) * TILE)
        d_key = jnp.zeros((TILE, 128), F32)
        d_val = jnp.zeros((TILE, 128), F32)
        for i in range(j, count):
            rows = slice(i * TILE, (i + 1) * TILE)
            mask = tile_mask(labels, labels_row, j, i)
            if i == j:
                mask = mask & order
            for head in range(2):
                d_ext = de_ref[head, rows, :]
                inner = dot_nt(packed[cols], moved[head][rows])
                weight = 1.0 + inner * (0.25 + inner * (1.0 / 32.0))
                weight = jnp.where(mask, weight, 0.0).astype(BF)
                d_weight = dot_nt(ext[head][cols], d_ext)
                d_inner = jnp.where(mask, d_weight * (0.25 + inner * (1.0 / 16.0)), 0.0).astype(BF)
                d_sum = jnp.where(inside[head], d_ext, jnp.zeros_like(d_ext))
                d_val = d_val + dot(weight, d_sum)
                d_key = d_key + dot(d_inner, moved[head][rows])
                dqt_ref[:, rows] += dot(keys_t[head][:, cols], d_inner)
        dqk_ref[cols, :] = d_key
        dv_ref[cols, :] = d_val
    carried = came_ref[TAIL + 16 : TAIL + 17, :].astype(F32) - 1.0
    usable = labels == carried
    total = dqk_ref[...] + jnp.transpose(dqt_ref[...])
    for head in range(2):
        d_ext = de_ref[head]
        d_ext = jnp.where(usable, d_ext, jnp.zeros_like(d_ext))
        at = head * STATE
        first = 16 * head
        d_outer = dot_nt(d_ext, came_ref[at : at + 256, :]) * dot_nt(packed, spread(first, 1))
        total = total + dot((d_outer * (1.0 / 16.0)).astype(BF), spread(first, 0))
        d_line = dot_nt(d_ext, came_ref[at + 256 : at + 384, :]) * 0.25
        total = total + dot_nt(d_line.astype(BF), q_to_k(head))
    dqk_ref[...] = total


def back_join_kernel(order, pabs_ref, lab_ref, dqk_ref, dv_ref, dvconv_ref, dgate_ref, came_ref, w_ref, out_ref, *send_refs):
    packed = pabs_ref[:, 256:384]
    values = pabs_ref[:, 0:128]
    labels = column(lab_ref[...])
    keep = labels == labels[TEAM_ROWS - 1 : TEAM_ROWS]
    lane = iota((TEAM_ROWS, 128), 1)
    d_val = dv_ref[...] + dvconv_ref[...]
    d_qk = dqk_ref[...]
    edge = jnp.where(keep[TEAM_ROWS - 16 :], came_ref[TAIL : TAIL + 16, :].astype(F32), 0.0)
    edge = jnp.concatenate([jnp.zeros((TEAM_ROWS - 16, 128), F32), edge], 0)
    d_val = d_val + edge
    for head in range(2):
        at = head * STATE
        first = KLANE + 16 * head
        d_two = came_ref[at : at + 256, :]
        d_one = came_ref[at + 256 : at + 384, :]
        ext = jnp.where(keep, extended(values, head), jnp.zeros_like(values))
        left = dot_nt(packed, spread(first, 0))
        right = dot_nt(packed, spread(first, 1))
        key_lanes = (lane >= first) & (lane < first + 16)
        line = jnp.where(key_lanes | (lane == ONE), packed, jnp.zeros_like(packed))
        d_ext = dot((left * right).astype(BF), d_two) + dot(line, d_one)
        d_val = d_val + jnp.where(keep & head_lanes(head, TEAM_ROWS), d_ext, 0.0)
        d_outer = dot_nt(ext, d_two) * right
        d_qk = d_qk + dot((d_outer * 2.0).astype(BF), spread(first, 0))
        d_qk = d_qk + jnp.where(key_lanes, dot_nt(ext, d_one), 0.0)
    d_val = d_val.astype(BF)
    d_qk = d_qk.astype(BF)
    for block in range(8):
        start = pl.multiple_of(order[block] * ROWS, ROWS)
        rows = slice(block * ROWS, (block + 1) * ROWS)
        out_ref[pl.ds(start, ROWS), 0:128] = d_val[rows]
        out_ref[pl.ds(start, ROWS), 128:256] = dgate_ref[rows, :]
        out_ref[pl.ds(start, ROWS), 256:384] = d_qk[rows]
    part = dot_nt(out_ref[512:, :], w_ref[...])
    for hop in range(4):
        send_refs[hop][...] = part[hop * ROWS : (hop + 1) * ROWS].astype(BF)


def mixer_grad_kernel(order, *refs):
    blocks, (mixed_ref, dtaps_ref, act_ref, dp_ref) = refs[:8], refs[8:12]
    grad_ref, sum_ref = refs[12:]
    for at in range(0, 1024, TILE):
        sum_ref[at : at + TILE, :] = dot(act_ref[at : at + TILE, :], dp_ref[...])
    start = pl.multiple_of(order[8] * 128, 128)
    spare = [jnp.zeros((64, 128), F32), dtaps_ref[...], jnp.zeros((56, 128), F32)]
    sum_ref[pl.ds(start, 128), 256:384] += jnp.transpose(jnp.concatenate(spare, 0))
    d_out = jnp.zeros((128, 1024), F32)
    for place in range(8):
        rows = slice(place * ROWS, (place + 1) * ROWS)
        d_out = d_out + dot_tn(mixed_ref[rows, :], blocks[place][...])
    for g in range(16):
        for l in range(3):
            part = sum_ref[g * 64 : (g + 1) * 64, l * 128 : (l + 1) * 128]
            grad_ref[g, l * 64 : (l + 1) * 64] = part.astype(BF)
        rows = d_out[g * 8 : (g + 1) * 8]
        for l in range(4):
            part = [rows[:, l * 128 : (l + 1) * 128], rows[:, 512 + l * 128 : 640 + l * 128]]
            grad_ref[g, 192 + l * 16 : 208 + l * 16] = jnp.concatenate(part, 0).astype(BF)


def sum_mixer_kernel(came_ref, other_ref, sum_ref, out_ref):
    total = came_ref[0].astype(F32)
    for g in range(1, 16):
        total = total + came_ref[g].astype(F32)
    for l in range(3):
        for t in range(8):
            rows = slice(l * 64 + t * 8, l * 64 + t * 8 + 8)
            sum_ref[t, :, l * 128 : (l + 1) * 128] = total[rows]
            sum_ref[t, :, 384 + l * 256 : 640 + l * 256] = other_ref[rows, :]
    out_ref[...] = total[192:256]


def call(kernel, outs, args, ordered=False, scratch=(), far=(), far_outs=(), lazy=False, grant=16):
    specs = [pl.BlockSpec(memory_space=pltpu.HBM if i in far else pltpu.VMEM) for i in range(len(args))]
    if ordered:
        specs[0] = pl.BlockSpec(memory_space=pltpu.SMEM)
    out_specs = [
        pl.BlockSpec(memory_space=pltpu.HBM if i in far_outs else pltpu.VMEM) for i in range(len(outs))
    ]
    rooms = [pltpu.VMEM(args[i].shape, args[i].dtype) for i in far]
    rooms += [pltpu.VMEM(outs[i].shape, outs[i].dtype) for i in far_outs]
    sems = [pltpu.SemaphoreType.DMA((len(rooms),))] if rooms else []

    def body(*refs):
        ins, results = list(refs[: len(args)]), list(refs[len(args) : len(args) + len(outs)])
        own = refs[len(args) + len(outs) :]
        own, room = own[: len(scratch)], own[len(scratch) :]
        reads, writes, sent = [], [], set()
        for at, i in enumerate(far):
            reads.append(pltpu.make_async_copy(ins[i], room[at], room[-1].at[at]))
            ins[i] = room[at]
        for at, i in enumerate(far_outs, len(far)):
            writes.append(pltpu.make_async_copy(room[at], results[i], room[-1].at[at]))
            results[i] = room[at]
        for copy in reads:
            copy.start()

        def put(at):
            sent.add(at)
            writes[at].start()

        def get(at):
            reads[at].wait()

        if lazy:
            kernel(*ins, *results, *own, get=get, put=put)
        else:
            for copy in reads:
                copy.wait()
            kernel(*ins, *results, *own)
        for at in range(len(writes)):
            if at not in sent:
                put(at)
        for copy in writes:
            copy.wait()

    micros = TIMES[kernel.__name__]
    return pl.pallas_call(
        body,
        out_shape=tuple(outs),
        in_specs=specs,
        out_specs=tuple(out_specs),
        scratch_shapes=list(scratch) + rooms + sems,
        cost_estimate=pl.CostEstimate(
            flops=int(micros * 1.15e9), bytes_accessed=int(micros * 3.6e6), transcendentals=0
        ),
        compiler_params=pltpu.CompilerParams(vmem_limit_bytes=grant * MIB),
    )(*args)


def shape(*sizes):
    return jax.ShapeDtypeStruct(sizes[:-1], sizes[-1])


def exchange(blocks, axes):
    return lax.all_to_all(blocks, axes, 0, 0, tiled=True)


def unit(field):
    scale = lax.rsqrt(jnp.mean(field * field, -1, keepdims=True) + EPSILON)
    return field * scale, scale


def unit_back(field, scale, upstream):
    pull = jnp.mean(field * upstream, -1, keepdims=True)
    return scale * upstream - field * (scale * scale * scale * pull)


def per_device(
    inputs, segments, cotangent, attn_gain, w_query, w_key, w_value, w_conv_gate,
    conv_kernel, w_output, ffn_gain, w_ffn_gate, w_ffn_up, w_ffn_down,
):
    x, core = lax.axis_index("x"), lax.axis_index("core")
    block = jnp.arange(8, dtype=jnp.int32)
    order = ((block % 2) ^ core) * 4 + (block // 2 - x) % 4
    back = 2 * ((block % 4 + x) % 4) + ((block // 4) ^ core)
    order = jnp.concatenate([order, jnp.full((1,), x * 2 + core, jnp.int32), back])
    small = jnp.concatenate([attn_gain[None], ffn_gain[None], conv_kernel], 0).astype(F32)
    small = jnp.pad(small, ((0, 3), (0, 0)))
    to_team = [(f, (f % 16) * 8 + f // 16) for f in range(128)]
    to_owner = [(place, f) for f, place in to_team]

    weights = (
        w_query, w_key, w_value, w_conv_gate, w_ffn_gate, w_ffn_up, w_output, w_ffn_down, small,
    )
    pack, whole = call(
        pack_kernel,
        [shape(8, 8, 1152, BF), shape(64, 512, BF)],
        weights,
        far=range(9),
        grant=60,
    )
    mine = exchange(pack, TEAM).reshape(64, 1152)
    ready = whole
    whole = lax.ppermute(whole, AXES, to_team)
    (tiles,) = call(spread_mixer_kernel, [shape(16, 256, 128, BF)], (mine, whole))
    mixer_came = exchange(tiles, GROUP)

    (block,) = call(
        block_kernel,
        [shape(BLOCK, 1024, BF)],
        (tie(inputs, ready), cotangent, segments[None]),
    )
    own_x = own_gather(block)
    other_x = other_gather(own_x)

    act_one, codes, cot = call(
        act_kernel,
        [shape(TEAM_ROWS, 1024, BF), shape(8, 128, F32), shape(TEAM_ROWS, 1024, BF)],
        (*own_x, *other_x),
    )
    pabs, payload, labels, taps, weight_1, weight_o = call(
        state_kernel,
        [
            shape(TEAM_ROWS, 384, BF),
            shape(PAYLOAD, 128, BF),
            shape(1, TEAM_ROWS, F32),
            shape(8, 128, F32),
            shape(1024, 384, BF),
            shape(128, 1024, BF),
        ],
        (order, act_one, codes, mixer_came),
        True,
        [pltpu.VMEM((TEAM_ROWS, 384), BF)],
    )
    came = lax.ppermute(payload, "zh", [(0, 1)])
    (local,) = call(local_kernel, [shape(2, TEAM_ROWS, 128, F32)], (pabs, labels))
    rows_f, rows_b = shape(ROWS, 1024, F32), shape(ROWS, 1024, BF)
    total, mixed, *sends = call(
        join_kernel,
        [shape(2, TEAM_ROWS, 128, F32), shape(TEAM_ROWS, 128, BF)] + [rows_b] * 4,
        (order, pabs, labels, local, came, taps, weight_o),
        True,
    )
    pieces = [rows_f] + [rows_b] * 3
    got = swap_all(sends)
    own, *rest = call(mix_sum_kernel, pieces, (mixed, weight_o, *got))
    (tiles,) = call(spread_ffn_kernel, [shape(16, 288, 256, BF)], (tie(mine, mixer_came), whole))
    ffn_came = exchange(tie(tiles, mixed), GROUP)
    after_mixer, own_two = call(norm_kernel, [rows_f, rows_b], (inputs, own, *own_scatter(rest)))
    (act_turned,) = call(turn_kernel, [shape(1024, TEAM_ROWS, BF)], (tie(act_one, own),))

    own_act = own_gather(tie(own_two, act_turned))
    weight_2, weight_d = call(
        ffn_weights_kernel,
        [shape(1024, 768, BF), shape(384, 1024, BF)],
        (tie(ffn_came, own_act[1]),),
        grant=60,
    )
    other_act = other_gather(own_act)
    halves = [shape(512, 384, BF), shape(512, 768, BF)]
    other_hidden, other_pair, *sends = call(
        ffn_other_kernel, halves + [rows_b] * 4, (*other_act, cot, weight_2, weight_d)
    )
    got = swap_all(sends)
    own_hidden, own_pair, part = call(
        ffn_own_kernel,
        halves + [shape(512, 1024, F32)],
        (*own_act, cot, weight_2, weight_d),
    )
    own, *rest = call(add_kernel, pieces, (part, *got))
    (grad_2,) = call(
        ffn_grad_kernel,
        [shape(16, 288, 256, BF)],
        (
            *own_act, *other_act, tie(cot, own),
            own_pair, other_pair, own_hidden, other_hidden,
        ),
        scratch=[
            pltpu.VMEM((1024, 1024), BF),
            pltpu.VMEM((384, 1024), F32),
        ],
    )
    two_came = own_scatter(rest)
    d_after, own_branch = call(
        norm_mid_kernel,
        [rows_f, rows_b],
        (after_mixer, cotangent, own, *two_came),
        far=range(6),
        far_outs=(0, 1),
        grant=60,
    )
    own_branch = tie(own_branch, grad_2)
    grad_2 = exchange(grad_2, GROUP)
    sends = call(send_kernel, [rows_b] * 4, (tie(other_hidden, own_branch), weight_d))
    got = swap_all(sends)
    own_branch = own_gather(own_branch)
    d_branch = (*own_branch, *other_gather(own_branch))
    result_own, *rest = call(mix_sum_kernel, pieces, (own_hidden, weight_d, *got))
    result_came = own_scatter(tie_all(rest, own_branch[1]))

    d_ext, d_val_conv, d_gate_c, d_taps, payload = call(
        back_state_kernel,
        [
            shape(2, TEAM_ROWS, 128, BF),
            shape(TEAM_ROWS, 128, F32),
            shape(TEAM_ROWS, 128, BF),
            shape(8, 128, F32),
            shape(PAYLOAD, 128, BF),
        ],
        (order, *d_branch, pabs, labels, total, came, taps, weight_o),
        True,
        [pltpu.VMEM((TEAM_ROWS, 128), F32)],
    )
    came_2 = lax.ppermute(payload, "zh", [(1, 0)])
    d_qk, d_val = call(
        back_local_kernel,
        [shape(TEAM_ROWS, 128, F32), shape(TEAM_ROWS, 128, F32)],
        (pabs, labels, d_ext, came),
        scratch=[pltpu.VMEM((128, TEAM_ROWS), F32)],
    )
    d_projected, *sends = call(
        back_join_kernel,
        [shape(TEAM_ROWS, 384, BF)] + [rows_b] * 4,
        (
            order, pabs, labels, d_qk, d_val, d_val_conv, d_gate_c, tie(came_2, *result_came),
            weight_1,
        ),
        True,
    )
    got = swap_all(sends)
    (grad_1,) = call(
        mixer_grad_kernel,
        [shape(16, 256, 128, BF)],
        (order, *d_branch, mixed, d_taps, act_turned, d_projected),
        True,
        [pltpu.VMEM((TEAM_ROWS, 384), F32)],
    )
    sum_2, sum_d = call(
        sum_ffn_kernel, [shape(192, 256, F32), shape(96, 256, F32)], (grad_2,)
    )
    own, *rest = call(
        back_sum_kernel,
        pieces,
        (d_projected, weight_1, *got),
        far=range(6),
        far_outs=range(4),
        grant=60,
    )
    grad_1 = exchange(tie(grad_1, grad_2, *got), GROUP)
    last = own_scatter(rest)
    grad_1 = tie(grad_1, last[0])
    (d_inputs,) = call(norm_back_kernel, [rows_b], (inputs, d_after, own, *last))
    (result,) = call(result_kernel, [rows_b], (after_mixer, result_own, *result_came))

    sum_d = lax.ppermute(sum_d, AXES, to_owner)
    sums, sum_o = call(
        sum_mixer_kernel, [shape(8, 8, 1152, F32), shape(64, 128, F32)], (grad_1, sum_2)
    )
    sum_o = lax.ppermute(sum_o, AXES, to_owner)
    sums = exchange(sums, TEAM)
    gq, gk, gv, gc, gg, gu, gd, go, gain_grad_1, gain_grad_2, grad_taps = call(
        owner_kernel,
        [shape(8, cols, F32) for cols in (256, 256, 1024, 1024, 2816, 2816)]
        + [shape(22, 1024, F32), shape(8, 1024, F32)]
        + [shape(1, 8, F32), shape(1, 8, F32), shape(3, 8, F32)],
        (sums, sum_d, sum_o, *weights[:6], small),
        far=range(10),
        grant=60,
    )
    return (
        result, d_inputs, gain_grad_1[0], gq, gk, gv, gc, grad_taps, go,
        gain_grad_2[0], gg, gu, gd,
    )


def solution(mesh):
    fine = Mesh(mesh.devices.reshape(SIZES), AXES)
    row, vector, taps = P(AXES, None), P(AXES), P(None, AXES)
    return jax.shard_map(
        per_device,
        mesh=fine,
        in_specs=(row, vector, row, vector, row, row, row, row, taps, row, vector, row, row, row),
        out_specs=(row, row, vector, row, row, row, row, taps, row, vector, row, row, row),
        check_vma=False,
    )
```

```python
import functools

import jax
import jax.numpy as jnp
from jax import lax
from jax.experimental import pallas as pl
from jax.experimental.pallas import tpu as pltpu
from jax.sharding import Mesh, PartitionSpec as P

EPSILON = 1e-05
BF = jnp.bfloat16
F32 = jnp.float32

AXES = ("zl", "y", "zh", "x", "core")
SIZES = (2, 4, 2, 4, 2)
GROUP = ("zl", "y", "zh")
TEAM = ("x", "core")
ROWS = 128
COT = 144
BLOCK = 272
TEAM_ROWS = 1024
TILE = 256
KLANE = 32
ONE = 64
STATE = 384
TAIL = 2 * STATE
PAYLOAD = TAIL + 32
MIB = 1024 * 1024
TIMES = {
    "pack_kernel": 2,
    "turn_kernel": 1.5,
    "block_kernel": 1,
    "spread_mixer_kernel": 1.2,
    "state_kernel": 0.2,
    "act_kernel": 14,
    "local_kernel": 0.2,
    "join_kernel": 2.6,
    "mix_sum_kernel": 1,
    "spread_ffn_kernel": 1.8,
    "norm_kernel": 12,
    "ffn_weights_kernel": 3,
    "ffn_own_kernel": 3.8,
    "ffn_other_kernel": 3.8,
    "add_kernel": 0.3,
    "ffn_grad_kernel": 4.2,
    "norm_back_kernel": 1,
    "norm_mid_kernel": 30,
    "send_kernel": 0.7,
    "back_state_kernel": 0.2,
    "back_local_kernel": 0.2,
    "back_join_kernel": 0.2,
    "mixer_grad_kernel": 0.2,
    "back_sum_kernel": 1.6,
    "sum_ffn_kernel": 2,
    "sum_mixer_kernel": 0.8,
    "result_kernel": 0.8,
    "owner_kernel": 2,
}


def from_x(block, hop):
    return lax.ppermute(block, "x", [(i, (i - hop) % 4) for i in range(4)])


def to_x(block, hop):
    return lax.ppermute(block, "x", [(i, (i + hop) % 4) for i in range(4)])


def swap_core(block):
    return lax.ppermute(block, "core", [(0, 1), (1, 0)])


def own_gather(block):
    return [block] + [from_x(block, hop) for hop in (1, 2, 3)]


def other_gather(own):
    return [swap_core(part) for part in (tie(own[0], own[1]), *own[1:])]


def swap_all(parts):
    return [swap_core(part) for part in parts]


def own_scatter(pieces):
    return [to_x(piece, hop) for hop, piece in zip((1, 2, 3), pieces)]


def tie(value, *before):
    return lax.optimization_barrier((value,) + before)[0]


def tie_all(values, *before):
    return list(lax.optimization_barrier((*values, *before)))[: len(values)]


def dot(left, right):
    return jnp.dot(left, right, preferred_element_type=F32)


def dot_nt(left, right):
    return lax.dot_general(left, right, (((1,), (1,)), ((), ())), preferred_element_type=F32)


def dot_tn(left, right):
    return lax.dot_general(left, right, (((0,), (0,)), ((), ())), preferred_element_type=F32)


def iota(shape, dim):
    return lax.broadcasted_iota(jnp.int32, shape, dim)


def one_hot(condition):
    return jnp.where(condition, 1.0, 0.0).astype(BF)


def spread(first, which):
    row, lane = iota((256, 128), 0), iota((256, 128), 1)
    part = row // 16 if which == 0 else row % 16
    return one_hot(lane == first + part)


def q_to_k(head):
    row, lane = iota((128, 128), 0), iota((128, 128), 1)
    low = 16 * head
    return one_hot((lane == row + KLANE) & (row >= low) & (row < low + 16))


def identity():
    return one_hot(iota((128, 128), 0) == iota((128, 128), 1))


def head_lanes(head, rows):
    lane = iota((rows, 128), 1)
    return lane < 64 if head == 0 else lane >= 64


def one_lane(head):
    return 64 if head == 0 else 0


def extended(values, head):
    rows = values.shape[0]
    lane = iota((rows, 128), 1)
    ones = jnp.where(lane == one_lane(head), 1.0, 0.0).astype(values.dtype)
    return jnp.where(head_lanes(head, rows), values, ones)


def column(labels_row):
    return jnp.transpose(jnp.broadcast_to(labels_row, (128, TEAM_ROWS)))


def shift_down(field, by, head_rows):
    moved = pltpu.roll(field, by, 0)
    row = iota(field.shape, 0)
    for at in range(by):
        moved = jnp.where(row == at, head_rows[at : at + 1], moved)
    return moved


def conv_parts(values, tail, labels, carried):
    back_1 = shift_down(values, 1, tail[15:16])
    back_2 = shift_down(values, 2, tail[14:16])
    carried_2 = jnp.broadcast_to(carried, (2, 128))
    mask_1 = shift_down(labels, 1, carried_2) == labels
    mask_2 = shift_down(labels, 2, carried_2) == labels
    return (
        jnp.where(mask_1, back_1, 0.0),
        jnp.where(mask_2, back_2, 0.0),
        mask_1,
        mask_2,
    )


def tile_mask(labels_col, labels_row, i, j):
    col = labels_col[i * TILE : (i + 1) * TILE]
    col = jnp.concatenate([col] * (TILE // 128), 1)
    row = labels_row[:, j * TILE : (j + 1) * TILE]
    return col == row


def block_kernel(inputs_ref, cot_ref, labels_ref, block_ref):
    labels = jnp.broadcast_to(labels_ref[...], (COT - ROWS, ROWS)).astype(F32)
    block_ref[0:ROWS, :] = inputs_ref[...]
    block_ref[ROWS:COT, :] = jnp.zeros((COT - ROWS, 1024), BF)
    block_ref[ROWS:COT, 0:ROWS] = labels.astype(BF)
    block_ref[COT:BLOCK, :] = cot_ref[...]


def turn_kernel(field_ref, out_ref):
    for at in range(0, 1024, TILE):
        out_ref[at : at + TILE, :] = jnp.transpose(field_ref[:, at : at + TILE])


def pack_kernel(wq, wk, wv, wc, wg, wu, wo, wd, small, team_ref, whole_ref):
    turned = jnp.transpose(jnp.concatenate([small[...], jnp.zeros((8, 120), F32)], 1))[0:8]
    one, two = turned[:, 0:1], turned[:, 1:2]
    value, gate_c = wv[...].astype(F32) * one, wc[...].astype(F32) * one
    query, key = wq[...].astype(F32) * one, wk[...].astype(F32) * one
    gate, up = wg[...].astype(F32) * two, wu[...].astype(F32) * two
    spare = jnp.concatenate([turned[:, 2:5], jnp.zeros((8, 61), F32)], 1)
    for t in range(8):
        team_ref[t, :, 0:128] = value[:, t * 128 : (t + 1) * 128].astype(BF)
        team_ref[t, :, 128:256] = gate_c[:, t * 128 : (t + 1) * 128].astype(BF)
        narrow = [query[:, t * 32 : (t + 1) * 32], key[:, t * 32 : (t + 1) * 32], spare]
        team_ref[t, :, 256:384] = jnp.concatenate(narrow, 1).astype(BF)
        for first, wide in ((384, gate), (768, up)):
            part = [wide[:, t * 352 : (t + 1) * 352], jnp.zeros((8, 32), F32)]
            team_ref[t, :, first : first + 384] = jnp.concatenate(part, 1).astype(BF)
    out = wo[...].astype(F32)
    down = wd[...].astype(F32)
    rows = [out[:, :512], out[:, 512:], down[:, :512], down[:, 512:], jnp.zeros((4, 512), F32)]
    whole_ref[...] = jnp.concatenate(rows, 0).astype(BF)


def spread_mixer_kernel(mine_ref, whole_ref, out_ref):
    rows = [mine_ref[:, l * 128 : (l + 1) * 128] for l in range(3)]
    rows += [whole_ref[0:16, l * 128 : (l + 1) * 128] for l in range(4)]
    rows = jnp.concatenate(rows, 0)
    for g in range(16):
        out_ref[g] = rows


def spread_ffn_kernel(mine_ref, whole_ref, out_ref):
    rows = [mine_ref[:, 384 + l * 256 : 640 + l * 256] for l in range(3)]
    rows += [whole_ref[16:64, l * 256 : (l + 1) * 256] for l in range(2)]
    rows = jnp.concatenate(rows, 0)
    for g in range(16):
        out_ref[g] = rows


def ffn_weights_kernel(came_ref, two_ref, down_ref):
    down_ref[352:384, :] = jnp.zeros((32, 1024), BF)
    for g in range(16):
        for l in range(3):
            two_ref[g * 64 : (g + 1) * 64, l * 256 : (l + 1) * 256] = came_ref[g, l * 64 : (l + 1) * 64]
    for g in range(0, 16, 8):
        rows = []
        for at in range(g, g + 8):
            part = [came_ref[at, 192 + l * 48 : 240 + l * 48].astype(F32) for l in range(2)]
            rows.append(jnp.concatenate([p[0:22] for p in part] + [p[22:44] for p in part], 1))
        down_ref[g * 22 : (g + 8) * 22, :] = jnp.concatenate(rows, 0).astype(BF)


def act_kernel(*refs):
    blocks, act_ref, code_ref, cot_ref = refs[:8], refs[8], refs[9], refs[10]
    for place in range(8):
        ref = blocks[place]
        rows = slice(place * ROWS, (place + 1) * ROWS)
        act_ref[rows, :] = unit(ref[0:ROWS, :].astype(F32))[0].astype(BF)
        code_ref[place : place + 1, :] = ref[ROWS:COT, 0:ROWS].astype(F32)[0:1]
        cot_ref[rows, :] = ref[COT:BLOCK, :]


def state_kernel(
    order, act_ref, code_ref, came_ref, pabs_ref, pay_ref, lab_ref, taps_ref, w_ref, wo_ref, rel_ref
):
    for g in range(16):
        for l in range(3):
            w_ref[g * 64 : (g + 1) * 64, l * 128 : (l + 1) * 128] = came_ref[g, l * 64 : (l + 1) * 64]
        part = [came_ref[g, 192 + l * 16 : 208 + l * 16].astype(F32) for l in range(4)]
        rows = jnp.concatenate([p[0:8] for p in part] + [p[8:16] for p in part], 1)
        wo_ref[g * 8 : (g + 1) * 8, :] = rows.astype(BF)
    start = pl.multiple_of(order[8] * 128, 128)
    taps_ref[...] = jnp.transpose(w_ref[pl.ds(start, 128), 256:384].astype(F32))[64:72]
    for half in range(2):
        rows = slice(half * 512, (half + 1) * 512)
        rel_ref[rows, :] = dot(act_ref[rows, :], w_ref[...]).astype(BF)
    lane = iota((ROWS, 128), 1)
    for block in range(8):
        rows = slice(block * ROWS, (block + 1) * ROWS)
        start = pl.multiple_of(order[block] * ROWS, ROWS)
        pabs_ref[rows, :] = rel_ref[pl.ds(start, ROWS), :]
        packed = pabs_ref[rows, 256:384]
        packed = jnp.where(lane == ONE, jnp.ones_like(packed), packed)
        pabs_ref[rows, 256:384] = jnp.where(lane > ONE, jnp.zeros_like(packed), packed)
        lab_ref[:, rows] = code_ref[pl.ds(order[block], 1), :]
    packed = pabs_ref[:, 256:384]
    values = pabs_ref[:, 0:128]
    labels = column(lab_ref[...])
    last = labels[TEAM_ROWS - 1 : TEAM_ROWS]
    keep = labels == last
    turned = dot_nt(identity(), packed).astype(BF)
    for head in range(2):
        ext = jnp.where(keep, extended(values, head), jnp.zeros_like(values))
        first = KLANE + 16 * head
        outer = dot_nt(spread(first, 0), packed) * dot_nt(spread(first, 1), packed)
        at = head * STATE
        pay_ref[at : at + 256, :] = dot(outer.astype(BF), ext).astype(BF)
        pay_ref[at + 256 : at + 384, :] = dot(turned, ext).astype(BF)
    tail = jnp.where(keep, values, jnp.zeros_like(values))
    pay_ref[TAIL : TAIL + 16, :] = tail[TEAM_ROWS - 16 :]
    pay_ref[TAIL + 16 : TAIL + 32, :] = jnp.broadcast_to(last + 1.0, (16, 128)).astype(BF)


def local_kernel(pabs_ref, lab_ref, tot_ref):
    packed = pabs_ref[:, 256:384]
    values = pabs_ref[:, 0:128]
    labels_row = lab_ref[...]
    labels = column(labels_row)
    order = iota((TILE, TILE), 0) >= iota((TILE, TILE), 1)
    moved = [dot(packed, q_to_k(head)).astype(BF) for head in range(2)]
    ext = [extended(values, head) for head in range(2)]
    count = TEAM_ROWS // TILE
    for i in range(count):
        rows = slice(i * TILE, (i + 1) * TILE)
        total = [jnp.zeros((TILE, 128), F32) for _ in range(2)]
        for j in range(i + 1):
            cols = slice(j * TILE, (j + 1) * TILE)
            mask = tile_mask(labels, labels_row, i, j)
            if i == j:
                mask = mask & order
            for head in range(2):
                inner = dot_nt(moved[head][rows], packed[cols])
                weight = 1.0 + inner * (0.25 + inner * (1.0 / 32.0))
                weight = jnp.where(mask, weight, 0.0).astype(BF)
                total[head] = total[head] + dot(weight, ext[head][cols])
        for head in range(2):
            tot_ref[head, rows, :] = total[head]


def normalised(total, head):
    lane = iota(total.shape, 1)
    mass = jnp.sum(jnp.where(lane == one_lane(head), total, 0.0), 1, keepdims=True)
    inside = head_lanes(head, total.shape[0])
    attended = jnp.where(inside, total / mass, 0.0)
    mean = jnp.sum(attended * attended, 1, keepdims=True) * (1.0 / 64.0)
    return attended, mass, lax.rsqrt(mean + EPSILON)


def carried_query(packed, head):
    lane = iota(packed.shape, 1)
    moved = dot(packed, q_to_k(head)) * 0.25
    return jnp.where(lane == ONE, 1.0, moved).astype(BF)


def join_kernel(order, pabs_ref, lab_ref, local_ref, came_ref, taps_ref, wo_ref, tot_ref, mixed_ref, *send_refs):
    packed = pabs_ref[:, 256:384]
    values = pabs_ref[:, 0:128].astype(F32)
    labels = column(lab_ref[...])
    carried = came_ref[TAIL + 16 : TAIL + 17, :].astype(F32) - 1.0
    usable = labels == carried
    attn = jnp.zeros((TEAM_ROWS, 128), F32)
    for head in range(2):
        at = head * STATE
        first = 16 * head
        outer = dot_nt(packed, spread(first, 0)) * dot_nt(packed, spread(first, 1))
        brought = dot(outer.astype(BF), came_ref[at : at + 256, :]) * (1.0 / 32.0)
        brought = brought + dot(carried_query(packed, head), came_ref[at + 256 : at + 384, :])
        total = local_ref[head] + jnp.where(usable, brought, 0.0)
        tot_ref[head] = total
        attended, _, scale = normalised(total, head)
        attn = attn + attended * scale
    tail = came_ref[TAIL : TAIL + 16, :].astype(F32)
    back_1, back_2, _, _ = conv_parts(values, tail, labels, carried)
    conv = taps_ref[0:1] * values + taps_ref[1:2] * back_1 + taps_ref[2:3] * back_2
    mixed = (attn + conv * pabs_ref[:, 128:256].astype(F32)).astype(BF)
    for block in range(8):
        start = pl.multiple_of(order[block] * ROWS, ROWS)
        mixed_ref[pl.ds(start, ROWS), :] = mixed[block * ROWS : (block + 1) * ROWS]
    part = dot(mixed_ref[512:, :], wo_ref[...])
    for hop in range(4):
        send_refs[hop][...] = part[hop * ROWS : (hop + 1) * ROWS].astype(BF)


def split_sum(total, got_refs, own_ref, piece_refs):
    own_ref[...] = total(0) + got_refs[0][...].astype(F32)
    for hop in (1, 2, 3):
        piece_refs[hop - 1][...] = (total(hop) + got_refs[hop][...].astype(F32)).astype(BF)


def mix_sum_kernel(left_ref, right_ref, *refs):
    total = dot(left_ref[0:512, :], right_ref[...])
    split_sum(lambda hop: total[hop * ROWS : (hop + 1) * ROWS], refs[:4], refs[4], refs[5:])


def add_kernel(mine_ref, *refs):
    split_sum(lambda hop: mine_ref[hop * ROWS : (hop + 1) * ROWS, :], refs[:4], refs[4], refs[5:])


def back_sum_kernel(left_ref, right_ref, *refs):
    total = dot_nt(left_ref[0:512, :], right_ref[...])
    split_sum(lambda hop: total[hop * ROWS : (hop + 1) * ROWS], refs[:4], refs[4], refs[5:])


def send_kernel(left_ref, right_ref, *send_refs):
    total = dot(left_ref[...], right_ref[...])
    for hop in range(4):
        send_refs[hop][...] = total[hop * ROWS : (hop + 1) * ROWS].astype(BF)


def norm_kernel(field_ref, own_ref, a_ref, b_ref, c_ref, after_ref, act_ref):
    came = a_ref[...].astype(F32) + b_ref[...].astype(F32) + c_ref[...].astype(F32)
    after = field_ref[...].astype(F32) + own_ref[...] + came
    after_ref[...] = after
    act_ref[...] = unit(after)[0].astype(BF)


def result_kernel(after_ref, own_ref, a_ref, b_ref, c_ref, out_ref):
    came = a_ref[...].astype(F32) + b_ref[...].astype(F32) + c_ref[...].astype(F32)
    out_ref[...] = (after_ref[...] + own_ref[...] + came).astype(BF)


def norm_back_kernel(field_ref, base_ref, own_ref, a_ref, b_ref, c_ref, *out_refs):
    upstream = a_ref[...].astype(F32) + b_ref[...].astype(F32) + c_ref[...].astype(F32)
    upstream = upstream + own_ref[...]
    field = field_ref[...].astype(F32)
    total = base_ref[...].astype(F32) + unit_back(field, unit(field)[1], upstream)
    for ref in out_refs:
        ref[...] = total.astype(ref.dtype)


def norm_mid_kernel(*refs):
    norm_back_kernel(*refs)


def ffn_own_kernel(*refs):
    ffn_kernel(*refs, half=0)


def ffn_other_kernel(*refs):
    ffn_kernel(*refs, half=1)


def ffn_kernel(*refs, half):
    acts, (cot_ref, w_ref, wd_ref) = refs[0:4], refs[4:7]
    hidden_ref, pair_ref, part_refs = refs[7], refs[8], refs[9:]
    for at in range(2):
        rows = slice(at * TILE, (at + 1) * TILE)
        act = jnp.concatenate([ref[...] for ref in acts[2 * at : 2 * at + 2]], 0)
        both = dot(act, w_ref[...])
        gate, up = both[:, 0:384], both[:, 384:768]
        d_hidden = dot_nt(cot_ref[half * 512 + at * TILE : half * 512 + (at + 1) * TILE, :], wd_ref[...])
        sigma = 1.0 / (1.0 + jnp.exp(-gate))
        swish = gate * sigma
        hidden_ref[rows, :] = (swish * up).astype(BF)
        pair_ref[rows, 0:384] = (d_hidden * up * sigma * (1.0 + gate * (1.0 - sigma))).astype(BF)
        pair_ref[rows, 384:768] = (d_hidden * swish).astype(BF)
        part = dot_nt(pair_ref[rows, :], w_ref[...])
        if len(part_refs) == 1:
            part_refs[0][rows, :] = part
        else:
            part_refs[2 * at][...] = part[0:ROWS].astype(BF)
            part_refs[2 * at + 1][...] = part[ROWS:].astype(BF)


def ffn_grad_kernel(*refs):
    acts, (cot_ref, pair_1, pair_2, hid_1, hid_2) = refs[0:8], refs[8:13]
    out_ref, act_ref, sum_ref = refs[13:]
    for place in range(8):
        act_ref[place * ROWS : (place + 1) * ROWS, :] = acts[place][...]
    for at in range(0, 1024, TILE):
        cols = slice(at, at + TILE)
        total = dot_tn(act_ref[0:512, cols], pair_1[...]) + dot_tn(act_ref[512:, cols], pair_2[...])
        for g in range(4):
            for l in range(3):
                part = total[g * 64 : (g + 1) * 64, l * 256 : (l + 1) * 256]
                out_ref[at // 64 + g, l * 64 : (l + 1) * 64] = part.astype(BF)
    for at in range(0, 384, 128):
        cols = slice(at, at + 128)
        total = dot_tn(hid_1[:, cols], cot_ref[0:512, :]) + dot_tn(hid_2[:, cols], cot_ref[512:, :])
        sum_ref[cols, :] = total
    for g in range(16):
        rows = sum_ref[g * 22 : (g + 1) * 22, :]
        for l in range(2):
            left, right = rows[:, l * 256 : (l + 1) * 256], rows[:, 512 + l * 256 : 768 + l * 256]
            part = jnp.concatenate([left, right, jnp.zeros((4, 256), F32)], 0)
            out_ref[g, 192 + l * 48 : 240 + l * 48] = part.astype(BF)


def sum_ffn_kernel(came_ref, two_ref, down_ref):
    total = came_ref[0].astype(F32)
    for g in range(1, 16):
        total = total + came_ref[g].astype(F32)
    two_ref[...] = total[0:192]
    down_ref[...] = total[192:288]


def owner_kernel(*refs):
    sum_ref, down_ref, out_ref, wq, wk, wv, wc, wg, wu, small = refs[:10]
    gq, gk, gv, gc, gg, gu, gd, go, d1_ref, d2_ref, dt_ref = refs[10:]
    parts = [down_ref[l * 48 : l * 48 + 48] for l in range(2)]
    gd[...] = jnp.concatenate([p[0:22] for p in parts] + [p[22:44] for p in parts], 1)
    parts = [out_ref[l * 16 : l * 16 + 16] for l in range(4)]
    go[...] = jnp.concatenate([p[0:8] for p in parts] + [p[8:16] for p in parts], 1)
    turned = jnp.transpose(jnp.concatenate([small[...], jnp.zeros((8, 120), F32)], 1))[0:8]
    taps = jnp.zeros((8, 128), F32)
    for t in range(8):
        taps = taps + sum_ref[t, :, 256:384]
    dt_ref[...] = jnp.transpose(taps)[64:67, 0:8]
    diagonal = iota((8, 128), 0) == iota((8, 128), 1)
    one, two = turned[:, 0:1], turned[:, 1:2]
    raw = [sum_ref[t] for t in range(8)]
    value = jnp.concatenate([part[:, 0:128] for part in raw], 1)
    gate_c = jnp.concatenate([part[:, 128:256] for part in raw], 1)
    query = jnp.concatenate([part[:, 256:288] for part in raw], 1)
    key = jnp.concatenate([part[:, 288:320] for part in raw], 1)
    gate = jnp.concatenate([part[:, 384:736] for part in raw], 1)
    up = jnp.concatenate([part[:, 768:1120] for part in raw], 1)
    total = jnp.zeros((8, 1), F32)
    for weight, field, out in ((wq, query, gq), (wk, key, gk), (wv, value, gv), (wc, gate_c, gc)):
        total = total + jnp.sum(weight[...].astype(F32) * field, 1, keepdims=True)
        out[...] = field * one
    d1_ref[...] = jnp.sum(jnp.where(diagonal, total, 0.0), 0, keepdims=True)[:, 0:8]
    total = jnp.zeros((8, 1), F32)
    for weight, field, out in ((wg, gate, gg), (wu, up, gu)):
        total = total + jnp.sum(weight[...].astype(F32) * field, 1, keepdims=True)
        out[...] = field * two
    d2_ref[...] = jnp.sum(jnp.where(diagonal, total, 0.0), 0, keepdims=True)[:, 0:8]


def back_state_kernel(order, *refs):
    blocks, (pabs_ref, lab_ref, tot_ref, came_ref, taps_ref, wo_ref) = refs[:8], refs[8:14]
    de_ref, dvconv_ref, dgate_ref, dtaps_ref, pay_ref, dm_ref = refs[14:]
    for place in range(8):
        start = pl.multiple_of(order[9 + place] * ROWS, ROWS)
        dm_ref[pl.ds(start, ROWS), :] = dot_nt(blocks[place][...], wo_ref[...])
    d_mixed = dm_ref[...]
    packed = pabs_ref[:, 256:384]
    values = pabs_ref[:, 0:128].astype(F32)
    labels = column(lab_ref[...])
    carried = came_ref[TAIL + 16 : TAIL + 17, :].astype(F32) - 1.0
    usable = labels == carried
    lane = iota((TEAM_ROWS, 128), 1)
    for head in range(2):
        attended, mass, scale = normalised(tot_ref[head], head)
        d_attn = jnp.where(head_lanes(head, TEAM_ROWS), d_mixed, 0.0)
        pull = jnp.sum(d_attn * attended, 1, keepdims=True) * (1.0 / 64.0)
        d_att = scale * (d_attn - attended * (scale * scale * pull))
        d_mass = -jnp.sum(d_att * attended, 1, keepdims=True) / mass
        d_ext = jnp.where(lane == one_lane(head), d_mass, d_att / mass).astype(BF)
        de_ref[head] = d_ext
        d_ext = jnp.where(usable, d_ext, jnp.zeros_like(d_ext))
        first = 16 * head
        at = head * STATE
        outer = dot_nt(spread(first, 0), packed) * dot_nt(spread(first, 1), packed)
        pay_ref[at : at + 256, :] = (dot(outer.astype(BF), d_ext) * (1.0 / 32.0)).astype(BF)
        turned = dot_nt(identity(), carried_query(packed, head)).astype(BF)
        pay_ref[at + 256 : at + 384, :] = dot(turned, d_ext).astype(BF)
    tail = came_ref[TAIL : TAIL + 16, :].astype(F32)
    back_1, back_2, mask_1, mask_2 = conv_parts(values, tail, labels, carried)
    conv = taps_ref[0:1] * values + taps_ref[1:2] * back_1 + taps_ref[2:3] * back_2
    dgate_ref[...] = (d_mixed * conv).astype(BF)
    d_conv = d_mixed * pabs_ref[:, 128:256].astype(F32)
    row8 = iota((8, 128), 0)
    sums = [jnp.sum(d_conv * part, 0, keepdims=True) for part in (values, back_1, back_2)]
    d_taps = jnp.zeros((8, 128), F32)
    for at in range(3):
        d_taps = jnp.where(row8 == at, sums[at], d_taps)
    dtaps_ref[...] = d_taps
    part_1 = jnp.where(mask_1, taps_ref[1:2] * d_conv, 0.0)
    part_2 = jnp.where(mask_2, taps_ref[2:3] * d_conv, 0.0)
    row = iota((TEAM_ROWS, 128), 0)
    up_1 = jnp.where(row < TEAM_ROWS - 1, pltpu.roll(part_1, TEAM_ROWS - 1, 0), 0.0)
    up_2 = jnp.where(row < TEAM_ROWS - 2, pltpu.roll(part_2, TEAM_ROWS - 2, 0), 0.0)
    dvconv_ref[...] = taps_ref[0:1] * d_conv + up_1 + up_2
    row16 = iota((16, 128), 0)
    edge = jnp.where(row16 == 14, part_2[0:1], 0.0)
    edge = jnp.where(row16 == 15, part_1[0:1] + part_2[1:2], edge)
    pay_ref[TAIL : TAIL + 16, :] = edge.astype(BF)
    pay_ref[TAIL + 16 : TAIL + 32, :] = jnp.zeros((16, 128), BF)


def back_local_kernel(pabs_ref, lab_ref, de_ref, came_ref, dqk_ref, dv_ref, dqt_ref):
    packed = pabs_ref[:, 256:384]
    values = pabs_ref[:, 0:128]
    labels_row = lab_ref[...]
    labels = column(labels_row)
    order = iota((TILE, TILE), 0) <= iota((TILE, TILE), 1)
    moved = [dot(packed, q_to_k(head)).astype(BF) for head in range(2)]
    keys_t = [dot_nt(q_to_k(head), packed).astype(BF) for head in range(2)]
    ext = [extended(values, head) for head in range(2)]
    inside = [head_lanes(head, TILE) for head in range(2)]
    count = TEAM_ROWS // TILE
    dqt_ref[...] = jnp.zeros((128, TEAM_ROWS), F32)
    for j in range(count):
        cols = slice(j * TILE, (j + 1) * TILE)
        d_key = jnp.zeros((TILE, 128), F32)
        d_val = jnp.zeros((TILE, 128), F32)
        for i in range(j, count):
            rows = slice(i * TILE, (i + 1) * TILE)
            mask = tile_mask(labels, labels_row, j, i)
            if i == j:
                mask = mask & order
            for head in range(2):
                d_ext = de_ref[head, rows, :]
                inner = dot_nt(packed[cols], moved[head][rows])
                weight = 1.0 + inner * (0.25 + inner * (1.0 / 32.0))
                weight = jnp.where(mask, weight, 0.0).astype(BF)
                d_weight = dot_nt(ext[head][cols], d_ext)
                d_inner = jnp.where(mask, d_weight * (0.25 + inner * (1.0 / 16.0)), 0.0).astype(BF)
                d_sum = jnp.where(inside[head], d_ext, jnp.zeros_like(d_ext))
                d_val = d_val + dot(weight, d_sum)
                d_key = d_key + dot(d_inner, moved[head][rows])
                dqt_ref[:, rows] += dot(keys_t[head][:, cols], d_inner)
        dqk_ref[cols, :] = d_key
        dv_ref[cols, :] = d_val
    carried = came_ref[TAIL + 16 : TAIL + 17, :].astype(F32) - 1.0
    usable = labels == carried
    total = dqk_ref[...] + jnp.transpose(dqt_ref[...])
    for head in range(2):
        d_ext = de_ref[head]
        d_ext = jnp.where(usable, d_ext, jnp.zeros_like(d_ext))
        at = head * STATE
        first = 16 * head
        d_outer = dot_nt(d_ext, came_ref[at : at + 256, :]) * dot_nt(packed, spread(first, 1))
        total = total + dot((d_outer * (1.0 / 16.0)).astype(BF), spread(first, 0))
        d_line = dot_nt(d_ext, came_ref[at + 256 : at + 384, :]) * 0.25
        total = total + dot_nt(d_line.astype(BF), q_to_k(head))
    dqk_ref[...] = total


def back_join_kernel(order, pabs_ref, lab_ref, dqk_ref, dv_ref, dvconv_ref, dgate_ref, came_ref, w_ref, out_ref, *send_refs):
    packed = pabs_ref[:, 256:384]
    values = pabs_ref[:, 0:128]
    labels = column(lab_ref[...])
    keep = labels == labels[TEAM_ROWS - 1 : TEAM_ROWS]
    lane = iota((TEAM_ROWS, 128), 1)
    d_val = dv_ref[...] + dvconv_ref[...]
    d_qk = dqk_ref[...]
    edge = jnp.where(keep[TEAM_ROWS - 16 :], came_ref[TAIL : TAIL + 16, :].astype(F32), 0.0)
    edge = jnp.concatenate([jnp.zeros((TEAM_ROWS - 16, 128), F32), edge], 0)
    d_val = d_val + edge
    for head in range(2):
        at = head * STATE
        first = KLANE + 16 * head
        d_two = came_ref[at : at + 256, :]
        d_one = came_ref[at + 256 : at + 384, :]
        ext = jnp.where(keep, extended(values, head), jnp.zeros_like(values))
        left = dot_nt(packed, spread(first, 0))
        right = dot_nt(packed, spread(first, 1))
        key_lanes = (lane >= first) & (lane < first + 16)
        line = jnp.where(key_lanes | (lane == ONE), packed, jnp.zeros_like(packed))
        d_ext = dot((left * right).astype(BF), d_two) + dot(line, d_one)
        d_val = d_val + jnp.where(keep & head_lanes(head, TEAM_ROWS), d_ext, 0.0)
        d_outer = dot_nt(ext, d_two) * right
        d_qk = d_qk + dot((d_outer * 2.0).astype(BF), spread(first, 0))
        d_qk = d_qk + jnp.where(key_lanes, dot_nt(ext, d_one), 0.0)
    d_val = d_val.astype(BF)
    d_qk = d_qk.astype(BF)
    for block in range(8):
        start = pl.multiple_of(order[block] * ROWS, ROWS)
        rows = slice(block * ROWS, (block + 1) * ROWS)
        out_ref[pl.ds(start, ROWS), 0:128] = d_val[rows]
        out_ref[pl.ds(start, ROWS), 128:256] = dgate_ref[rows, :]
        out_ref[pl.ds(start, ROWS), 256:384] = d_qk[rows]
    part = dot_nt(out_ref[512:, :], w_ref[...])
    for hop in range(4):
        send_refs[hop][...] = part[hop * ROWS : (hop + 1) * ROWS].astype(BF)


def mixer_grad_kernel(order, *refs):
    blocks, (mixed_ref, dtaps_ref, act_ref, dp_ref) = refs[:8], refs[8:12]
    grad_ref, sum_ref = refs[12:]
    for at in range(0, 1024, TILE):
        sum_ref[at : at + TILE, :] = dot(act_ref[at : at + TILE, :], dp_ref[...])
    start = pl.multiple_of(order[8] * 128, 128)
    spare = [jnp.zeros((64, 128), F32), dtaps_ref[...], jnp.zeros((56, 128), F32)]
    sum_ref[pl.ds(start, 128), 256:384] += jnp.transpose(jnp.concatenate(spare, 0))
    d_out = jnp.zeros((128, 1024), F32)
    for place in range(8):
        rows = slice(place * ROWS, (place + 1) * ROWS)
        d_out = d_out + dot_tn(mixed_ref[rows, :], blocks[place][...])
    for g in range(16):
        for l in range(3):
            part = sum_ref[g * 64 : (g + 1) * 64, l * 128 : (l + 1) * 128]
            grad_ref[g, l * 64 : (l + 1) * 64] = part.astype(BF)
        rows = d_out[g * 8 : (g + 1) * 8]
        for l in range(4):
            part = [rows[:, l * 128 : (l + 1) * 128], rows[:, 512 + l * 128 : 640 + l * 128]]
            grad_ref[g, 192 + l * 16 : 208 + l * 16] = jnp.concatenate(part, 0).astype(BF)


def sum_mixer_kernel(came_ref, other_ref, sum_ref, out_ref):
    total = came_ref[0].astype(F32)
    for g in range(1, 16):
        total = total + came_ref[g].astype(F32)
    for l in range(3):
        for t in range(8):
            rows = slice(l * 64 + t * 8, l * 64 + t * 8 + 8)
            sum_ref[t, :, l * 128 : (l + 1) * 128] = total[rows]
            sum_ref[t, :, 384 + l * 256 : 640 + l * 256] = other_ref[rows, :]
    out_ref[...] = total[192:256]


def call(kernel, outs, args, ordered=False, scratch=(), far=(), far_outs=(), lazy=False, grant=16):
    specs = [pl.BlockSpec(memory_space=pltpu.HBM if i in far else pltpu.VMEM) for i in range(len(args))]
    if ordered:
        specs[0] = pl.BlockSpec(memory_space=pltpu.SMEM)
    out_specs = [
        pl.BlockSpec(memory_space=pltpu.HBM if i in far_outs else pltpu.VMEM) for i in range(len(outs))
    ]
    rooms = [pltpu.VMEM(args[i].shape, args[i].dtype) for i in far]
    rooms += [pltpu.VMEM(outs[i].shape, outs[i].dtype) for i in far_outs]
    sems = [pltpu.SemaphoreType.DMA((len(rooms),))] if rooms else []

    def body(*refs):
        ins, results = list(refs[: len(args)]), list(refs[len(args) : len(args) + len(outs)])
        own = refs[len(args) + len(outs) :]
        own, room = own[: len(scratch)], own[len(scratch) :]
        reads, writes, sent = [], [], set()
        for at, i in enumerate(far):
            reads.append(pltpu.make_async_copy(ins[i], room[at], room[-1].at[at]))
            ins[i] = room[at]
        for at, i in enumerate(far_outs, len(far)):
            writes.append(pltpu.make_async_copy(room[at], results[i], room[-1].at[at]))
            results[i] = room[at]
        for copy in reads:
            copy.start()

        def put(at):
            sent.add(at)
            writes[at].start()

        def get(at):
            reads[at].wait()

        if lazy:
            kernel(*ins, *results, *own, get=get, put=put)
        else:
            for copy in reads:
                copy.wait()
            kernel(*ins, *results, *own)
        for at in range(len(writes)):
            if at not in sent:
                put(at)
        for copy in writes:
            copy.wait()

    micros = TIMES[kernel.__name__]
    return pl.pallas_call(
        body,
        out_shape=tuple(outs),
        in_specs=specs,
        out_specs=tuple(out_specs),
        scratch_shapes=list(scratch) + rooms + sems,
        cost_estimate=pl.CostEstimate(
            flops=int(micros * 1.15e9), bytes_accessed=int(micros * 3.6e6), transcendentals=0
        ),
        compiler_params=pltpu.CompilerParams(vmem_limit_bytes=grant * MIB),
    )(*args)


def shape(*sizes):
    return jax.ShapeDtypeStruct(sizes[:-1], sizes[-1])


def exchange(blocks, axes):
    return lax.all_to_all(blocks, axes, 0, 0, tiled=True)


def unit(field):
    scale = lax.rsqrt(jnp.mean(field * field, -1, keepdims=True) + EPSILON)
    return field * scale, scale


def unit_back(field, scale, upstream):
    pull = jnp.mean(field * upstream, -1, keepdims=True)
    return scale * upstream - field * (scale * scale * scale * pull)


def per_device(
    inputs, segments, cotangent, attn_gain, w_query, w_key, w_value, w_conv_gate,
    conv_kernel, w_output, ffn_gain, w_ffn_gate, w_ffn_up, w_ffn_down,
):
    x, core = lax.axis_index("x"), lax.axis_index("core")
    block = jnp.arange(8, dtype=jnp.int32)
    order = ((block % 2) ^ core) * 4 + (block // 2 - x) % 4
    back = 2 * ((block % 4 + x) % 4) + ((block // 4) ^ core)
    order = jnp.concatenate([order, jnp.full((1,), x * 2 + core, jnp.int32), back])
    small = jnp.concatenate([attn_gain[None], ffn_gain[None], conv_kernel], 0).astype(F32)
    small = jnp.pad(small, ((0, 3), (0, 0)))
    to_team = [(f, (f % 16) * 8 + f // 16) for f in range(128)]
    to_owner = [(place, f) for f, place in to_team]

    weights = (
        w_query, w_key, w_value, w_conv_gate, w_ffn_gate, w_ffn_up, w_output, w_ffn_down, small,
    )
    pack, whole = call(
        pack_kernel,
        [shape(8, 8, 1152, BF), shape(64, 512, BF)],
        weights,
        far=range(9),
        grant=60,
    )
    mine = exchange(pack, TEAM).reshape(64, 1152)
    ready = whole
    whole = lax.ppermute(whole, AXES, to_team)
    (tiles,) = call(spread_mixer_kernel, [shape(16, 256, 128, BF)], (mine, whole))
    mixer_came = exchange(tiles, GROUP)

    (block,) = call(
        block_kernel,
        [shape(BLOCK, 1024, BF)],
        (tie(inputs, ready), cotangent, segments[None]),
    )
    own_x = own_gather(block)
    other_x = other_gather(own_x)

    act_one, codes, cot = call(
        act_kernel,
        [shape(TEAM_ROWS, 1024, BF), shape(8, 128, F32), shape(TEAM_ROWS, 1024, BF)],
        (*own_x, *other_x),
    )
    pabs, payload, labels, taps, weight_1, weight_o = call(
        state_kernel,
        [
            shape(TEAM_ROWS, 384, BF),
            shape(PAYLOAD, 128, BF),
            shape(1, TEAM_ROWS, F32),
            shape(8, 128, F32),
            shape(1024, 384, BF),
            shape(128, 1024, BF),
        ],
        (order, act_one, codes, mixer_came),
        True,
        [pltpu.VMEM((TEAM_ROWS, 384), BF)],
    )
    came = lax.ppermute(payload, "zh", [(0, 1)])
    (local,) = call(local_kernel, [shape(2, TEAM_ROWS, 128, F32)], (pabs, labels))
    rows_f, rows_b = shape(ROWS, 1024, F32), shape(ROWS, 1024, BF)
    total, mixed, *sends = call(
        join_kernel,
        [shape(2, TEAM_ROWS, 128, F32), shape(TEAM_ROWS, 128, BF)] + [rows_b] * 4,
        (order, pabs, labels, local, came, taps, weight_o),
        True,
    )
    pieces = [rows_f] + [rows_b] * 3
    got = swap_all(sends)
    own, *rest = call(mix_sum_kernel, pieces, (mixed, weight_o, *got))
    (tiles,) = call(spread_ffn_kernel, [shape(16, 288, 256, BF)], (tie(mine, mixer_came), whole))
    ffn_came = exchange(tie(tiles, payload), GROUP)
    after_mixer, own_two = call(norm_kernel, [rows_f, rows_b], (inputs, own, *own_scatter(rest)))
    (act_turned,) = call(turn_kernel, [shape(1024, TEAM_ROWS, BF)], (tie(act_one, own),))

    own_act = own_gather(tie(own_two, act_turned))
    weight_2, weight_d = call(
        ffn_weights_kernel,
        [shape(1024, 768, BF), shape(384, 1024, BF)],
        (tie(ffn_came, own_act[1]),),
        grant=60,
    )
    other_act = other_gather(own_act)
    halves = [shape(512, 384, BF), shape(512, 768, BF)]
    other_hidden, other_pair, *sends = call(
        ffn_other_kernel, halves + [rows_b] * 4, (*other_act, cot, weight_2, weight_d)
    )
    got = swap_all(sends)
    own_hidden, own_pair, part = call(
        ffn_own_kernel,
        halves + [shape(512, 1024, F32)],
        (*own_act, cot, weight_2, weight_d),
    )
    own, *rest = call(add_kernel, pieces, (part, *got))
    (grad_2,) = call(
        ffn_grad_kernel,
        [shape(16, 288, 256, BF)],
        (
            *own_act, *other_act, tie(cot, own),
            own_pair, other_pair, own_hidden, other_hidden,
        ),
        scratch=[
            pltpu.VMEM((1024, 1024), BF),
            pltpu.VMEM((384, 1024), F32),
        ],
    )
    two_came = own_scatter(rest)
    d_after, own_branch = call(
        norm_mid_kernel,
        [rows_f, rows_b],
        (after_mixer, cotangent, own, *two_came),
        far=range(6),
        far_outs=(0, 1),
        grant=60,
    )
    own_branch = tie(own_branch, grad_2)
    grad_2 = exchange(grad_2, GROUP)
    sends = call(send_kernel, [rows_b] * 4, (tie(other_hidden, own_branch), weight_d))
    got = swap_all(sends)
    own_branch = own_gather(own_branch)
    d_branch = (*own_branch, *other_gather(own_branch))
    result_own, *rest = call(mix_sum_kernel, pieces, (own_hidden, weight_d, *got))
    result_came = own_scatter(tie_all(rest, own_branch[1]))
    (result,) = call(result_kernel, [rows_b], (after_mixer, result_own, *result_came))

    d_ext, d_val_conv, d_gate_c, d_taps, payload = call(
        back_state_kernel,
        [
            shape(2, TEAM_ROWS, 128, BF),
            shape(TEAM_ROWS, 128, F32),
            shape(TEAM_ROWS, 128, BF),
            shape(8, 128, F32),
            shape(PAYLOAD, 128, BF),
        ],
        (order, *d_branch, pabs, labels, total, came, taps, weight_o),
        True,
        [pltpu.VMEM((TEAM_ROWS, 128), F32)],
    )
    came_2 = lax.ppermute(payload, "zh", [(1, 0)])
    d_qk, d_val = call(
        back_local_kernel,
        [shape(TEAM_ROWS, 128, F32), shape(TEAM_ROWS, 128, F32)],
        (pabs, labels, d_ext, came),
        scratch=[pltpu.VMEM((128, TEAM_ROWS), F32)],
    )
    d_projected, *sends = call(
        back_join_kernel,
        [shape(TEAM_ROWS, 384, BF)] + [rows_b] * 4,
        (
            order, pabs, labels, d_qk, d_val, d_val_conv, d_gate_c, tie(came_2, result),
            weight_1,
        ),
        True,
    )
    got = swap_all(sends)
    (grad_1,) = call(
        mixer_grad_kernel,
        [shape(16, 256, 128, BF)],
        (order, *d_branch, mixed, d_taps, act_turned, d_projected),
        True,
        [pltpu.VMEM((TEAM_ROWS, 384), F32)],
    )
    sum_2, sum_d = call(
        sum_ffn_kernel, [shape(192, 256, F32), shape(96, 256, F32)], (grad_2,)
    )
    own, *rest = call(
        back_sum_kernel,
        pieces,
        (d_projected, weight_1, *got),
        far=range(6),
        far_outs=range(4),
        grant=60,
    )
    grad_1 = exchange(tie(grad_1, grad_2, *got), GROUP)
    last = own_scatter(rest)
    grad_1 = tie(grad_1, last[0])
    (d_inputs,) = call(norm_back_kernel, [rows_b], (inputs, d_after, own, *last))

    sum_d = lax.ppermute(sum_d, AXES, to_owner)
    sums, sum_o = call(
        sum_mixer_kernel, [shape(8, 8, 1152, F32), shape(64, 128, F32)], (grad_1, sum_2)
    )
    sum_o = lax.ppermute(sum_o, AXES, to_owner)
    sums = exchange(sums, TEAM)
    gq, gk, gv, gc, gg, gu, gd, go, gain_grad_1, gain_grad_2, grad_taps = call(
        owner_kernel,
        [shape(8, cols, F32) for cols in (256, 256, 1024, 1024, 2816, 2816)]
        + [shape(22, 1024, F32), shape(8, 1024, F32)]
        + [shape(1, 8, F32), shape(1, 8, F32), shape(3, 8, F32)],
        (sums, sum_d, sum_o, *weights[:6], small),
        far=range(10),
        grant=60,
    )
    return (
        result, d_inputs, gain_grad_1[0], gq, gk, gv, gc, grad_taps, go,
        gain_grad_2[0], gg, gu, gd,
    )


def solution(mesh):
    fine = Mesh(mesh.devices.reshape(SIZES), AXES)
    row, vector, taps = P(AXES, None), P(AXES), P(None, AXES)
    return jax.shard_map(
        per_device,
        mesh=fine,
        in_specs=(row, vector, row, vector, row, row, row, row, taps, row, vector, row, row, row),
        out_specs=(row, row, vector, row, row, row, row, taps, row, vector, row, row, row),
        check_vma=False,
    )
```

```python
import functools

import jax
import jax.numpy as jnp
from jax import lax
from jax.experimental import pallas as pl
from jax.experimental.pallas import tpu as pltpu
from jax.sharding import Mesh, PartitionSpec as P

EPSILON = 1e-05
BF = jnp.bfloat16
F32 = jnp.float32

AXES = ("zl", "y", "zh", "x", "core")
SIZES = (2, 4, 2, 4, 2)
GROUP = ("zl", "y", "zh")
TEAM = ("x", "core")
ROWS = 128
COT = 144
BLOCK = 272
TEAM_ROWS = 1024
TILE = 256
KLANE = 32
ONE = 64
STATE = 384
TAIL = 2 * STATE
PAYLOAD = TAIL + 32
MIB = 1024 * 1024
TIMES = {
    "pack_kernel": 2,
    "turn_kernel": 1.5,
    "block_kernel": 1,
    "spread_mixer_kernel": 1.2,
    "state_kernel": 0.2,
    "act_kernel": 14,
    "local_kernel": 0.2,
    "join_kernel": 2.6,
    "mix_sum_kernel": 1,
    "spread_ffn_kernel": 1.8,
    "norm_kernel": 12,
    "ffn_weights_kernel": 3,
    "ffn_own_kernel": 3.8,
    "ffn_other_kernel": 3.8,
    "add_kernel": 0.3,
    "ffn_grad_kernel": 4.2,
    "norm_back_kernel": 1,
    "norm_mid_kernel": 30,
    "send_kernel": 0.7,
    "back_state_kernel": 0.2,
    "back_local_kernel": 0.2,
    "back_join_kernel": 0.2,
    "mixer_grad_kernel": 0.2,
    "back_sum_kernel": 1.6,
    "sum_ffn_kernel": 2,
    "sum_mixer_kernel": 0.8,
    "result_kernel": 0.8,
    "owner_kernel": 2,
}


def from_x(block, hop):
    return lax.ppermute(block, "x", [(i, (i - hop) % 4) for i in range(4)])


def to_x(block, hop):
    return lax.ppermute(block, "x", [(i, (i + hop) % 4) for i in range(4)])


def swap_core(block):
    return lax.ppermute(block, "core", [(0, 1), (1, 0)])


def own_gather(block):
    return [block] + [from_x(block, hop) for hop in (1, 2, 3)]


def other_gather(own):
    return [swap_core(part) for part in (tie(own[0], own[1]), *own[1:])]


def swap_all(parts):
    return [swap_core(part) for part in parts]


def own_scatter(pieces):
    return [to_x(piece, hop) for hop, piece in zip((1, 2, 3), pieces)]


def tie(value, *before):
    return lax.optimization_barrier((value,) + before)[0]


def tie_all(values, *before):
    return list(lax.optimization_barrier((*values, *before)))[: len(values)]


def dot(left, right):
    return jnp.dot(left, right, preferred_element_type=F32)


def dot_nt(left, right):
    return lax.dot_general(left, right, (((1,), (1,)), ((), ())), preferred_element_type=F32)


def dot_tn(left, right):
    return lax.dot_general(left, right, (((0,), (0,)), ((), ())), preferred_element_type=F32)


def iota(shape, dim):
    return lax.broadcasted_iota(jnp.int32, shape, dim)


def one_hot(condition):
    return jnp.where(condition, 1.0, 0.0).astype(BF)


def spread(first, which):
    row, lane = iota((256, 128), 0), iota((256, 128), 1)
    part = row // 16 if which == 0 else row % 16
    return one_hot(lane == first + part)


def q_to_k(head):
    row, lane = iota((128, 128), 0), iota((128, 128), 1)
    low = 16 * head
    return one_hot((lane == row + KLANE) & (row >= low) & (row < low + 16))


def identity():
    return one_hot(iota((128, 128), 0) == iota((128, 128), 1))


def head_lanes(head, rows):
    lane = iota((rows, 128), 1)
    return lane < 64 if head == 0 else lane >= 64


def one_lane(head):
    return 64 if head == 0 else 0


def extended(values, head):
    rows = values.shape[0]
    lane = iota((rows, 128), 1)
    ones = jnp.where(lane == one_lane(head), 1.0, 0.0).astype(values.dtype)
    return jnp.where(head_lanes(head, rows), values, ones)


def column(labels_row):
    return jnp.transpose(jnp.broadcast_to(labels_row, (128, TEAM_ROWS)))


def shift_down(field, by, head_rows):
    moved = pltpu.roll(field, by, 0)
    row = iota(field.shape, 0)
    for at in range(by):
        moved = jnp.where(row == at, head_rows[at : at + 1], moved)
    return moved


def conv_parts(values, tail, labels, carried):
    back_1 = shift_down(values, 1, tail[15:16])
    back_2 = shift_down(values, 2, tail[14:16])
    carried_2 = jnp.broadcast_to(carried, (2, 128))
    mask_1 = shift_down(labels, 1, carried_2) == labels
    mask_2 = shift_down(labels, 2, carried_2) == labels
    return (
        jnp.where(mask_1, back_1, 0.0),
        jnp.where(mask_2, back_2, 0.0),
        mask_1,
        mask_2,
    )


def tile_mask(labels_col, labels_row, i, j):
    col = labels_col[i * TILE : (i + 1) * TILE]
    col = jnp.concatenate([col] * (TILE // 128), 1)
    row = labels_row[:, j * TILE : (j + 1) * TILE]
    return col == row


def block_kernel(inputs_ref, cot_ref, labels_ref, block_ref):
    labels = jnp.broadcast_to(labels_ref[...], (COT - ROWS, ROWS)).astype(F32)
    block_ref[0:ROWS, :] = inputs_ref[...]
    block_ref[ROWS:COT, :] = jnp.zeros((COT - ROWS, 1024), BF)
    block_ref[ROWS:COT, 0:ROWS] = labels.astype(BF)
    block_ref[COT:BLOCK, :] = cot_ref[...]


def turn_kernel(field_ref, out_ref):
    for at in range(0, 1024, TILE):
        out_ref[at : at + TILE, :] = jnp.transpose(field_ref[:, at : at + TILE])


def small_rows(gain_1, gain_2, taps):
    rows = [gain_1[...].astype(F32), gain_2[...].astype(F32), taps[...].astype(F32)]
    rows = jnp.concatenate(rows + [jnp.zeros((3, 8), F32)], 0)
    return jnp.transpose(jnp.concatenate([rows, jnp.zeros((8, 120), F32)], 1))[0:8]


def pack_kernel(wq, wk, wv, wc, wg, wu, wo, wd, gain_1, gain_2, taps, team_ref, whole_ref):
    turned = small_rows(gain_1, gain_2, taps)
    one, two = turned[:, 0:1], turned[:, 1:2]
    value, gate_c = wv[...].astype(F32) * one, wc[...].astype(F32) * one
    query, key = wq[...].astype(F32) * one, wk[...].astype(F32) * one
    gate, up = wg[...].astype(F32) * two, wu[...].astype(F32) * two
    spare = jnp.concatenate([turned[:, 2:5], jnp.zeros((8, 61), F32)], 1)
    for t in range(8):
        team_ref[t, :, 0:128] = value[:, t * 128 : (t + 1) * 128].astype(BF)
        team_ref[t, :, 128:256] = gate_c[:, t * 128 : (t + 1) * 128].astype(BF)
        narrow = [query[:, t * 32 : (t + 1) * 32], key[:, t * 32 : (t + 1) * 32], spare]
        team_ref[t, :, 256:384] = jnp.concatenate(narrow, 1).astype(BF)
        for first, wide in ((384, gate), (768, up)):
            part = [wide[:, t * 352 : (t + 1) * 352], jnp.zeros((8, 32), F32)]
            team_ref[t, :, first : first + 384] = jnp.concatenate(part, 1).astype(BF)
    out = wo[...].astype(F32)
    down = wd[...].astype(F32)
    rows = [out[:, :512], out[:, 512:], down[:, :512], down[:, 512:], jnp.zeros((4, 512), F32)]
    whole_ref[...] = jnp.concatenate(rows, 0).astype(BF)


def spread_mixer_kernel(mine_ref, whole_ref, out_ref):
    rows = [mine_ref[:, l * 128 : (l + 1) * 128] for l in range(3)]
    rows += [whole_ref[0:16, l * 128 : (l + 1) * 128] for l in range(4)]
    rows = jnp.concatenate(rows, 0)
    for g in range(16):
        out_ref[g] = rows


def spread_ffn_kernel(mine_ref, whole_ref, out_ref):
    rows = [mine_ref[:, 384 + l * 256 : 640 + l * 256] for l in range(3)]
    rows += [whole_ref[16:64, l * 256 : (l + 1) * 256] for l in range(2)]
    rows = jnp.concatenate(rows, 0)
    for g in range(16):
        out_ref[g] = rows


def ffn_weights_kernel(came_ref, two_ref, down_ref):
    down_ref[352:384, :] = jnp.zeros((32, 1024), BF)
    for g in range(16):
        for l in range(3):
            two_ref[g * 64 : (g + 1) * 64, l * 256 : (l + 1) * 256] = came_ref[g, l * 64 : (l + 1) * 64]
    for g in range(0, 16, 8):
        rows = []
        for at in range(g, g + 8):
            part = [came_ref[at, 192 + l * 48 : 240 + l * 48].astype(F32) for l in range(2)]
            rows.append(jnp.concatenate([p[0:22] for p in part] + [p[22:44] for p in part], 1))
        down_ref[g * 22 : (g + 8) * 22, :] = jnp.concatenate(rows, 0).astype(BF)


def act_kernel(*refs):
    blocks, act_ref, code_ref, cot_ref = refs[:8], refs[8], refs[9], refs[10]
    for place in range(8):
        ref = blocks[place]
        rows = slice(place * ROWS, (place + 1) * ROWS)
        act_ref[rows, :] = unit(ref[0:ROWS, :].astype(F32))[0].astype(BF)
        code_ref[place : place + 1, :] = ref[ROWS:COT, 0:ROWS].astype(F32)[0:1]
        cot_ref[rows, :] = ref[COT:BLOCK, :]


def state_kernel(
    order, act_ref, code_ref, came_ref, pabs_ref, pay_ref, lab_ref, taps_ref, w_ref, wo_ref, rel_ref
):
    for g in range(16):
        for l in range(3):
            w_ref[g * 64 : (g + 1) * 64, l * 128 : (l + 1) * 128] = came_ref[g, l * 64 : (l + 1) * 64]
        part = [came_ref[g, 192 + l * 16 : 208 + l * 16].astype(F32) for l in range(4)]
        rows = jnp.concatenate([p[0:8] for p in part] + [p[8:16] for p in part], 1)
        wo_ref[g * 8 : (g + 1) * 8, :] = rows.astype(BF)
    start = pl.multiple_of(order[8] * 128, 128)
    taps_ref[...] = jnp.transpose(w_ref[pl.ds(start, 128), 256:384].astype(F32))[64:72]
    for half in range(2):
        rows = slice(half * 512, (half + 1) * 512)
        rel_ref[rows, :] = dot(act_ref[rows, :], w_ref[...]).astype(BF)
    lane = iota((ROWS, 128), 1)
    for block in range(8):
        rows = slice(block * ROWS, (block + 1) * ROWS)
        start = pl.multiple_of(order[block] * ROWS, ROWS)
        pabs_ref[rows, :] = rel_ref[pl.ds(start, ROWS), :]
        packed = pabs_ref[rows, 256:384]
        packed = jnp.where(lane == ONE, jnp.ones_like(packed), packed)
        pabs_ref[rows, 256:384] = jnp.where(lane > ONE, jnp.zeros_like(packed), packed)
        lab_ref[:, rows] = code_ref[pl.ds(order[block], 1), :]
    packed = pabs_ref[:, 256:384]
    values = pabs_ref[:, 0:128]
    labels = column(lab_ref[...])
    last = labels[TEAM_ROWS - 1 : TEAM_ROWS]
    keep = labels == last
    turned = dot_nt(identity(), packed).astype(BF)
    for head in range(2):
        ext = jnp.where(keep, extended(values, head), jnp.zeros_like(values))
        first = KLANE + 16 * head
        outer = dot_nt(spread(first, 0), packed) * dot_nt(spread(first, 1), packed)
        at = head * STATE
        pay_ref[at : at + 256, :] = dot(outer.astype(BF), ext).astype(BF)
        pay_ref[at + 256 : at + 384, :] = dot(turned, ext).astype(BF)
    tail = jnp.where(keep, values, jnp.zeros_like(values))
    pay_ref[TAIL : TAIL + 16, :] = tail[TEAM_ROWS - 16 :]
    pay_ref[TAIL + 16 : TAIL + 32, :] = jnp.broadcast_to(last + 1.0, (16, 128)).astype(BF)


def local_kernel(pabs_ref, lab_ref, tot_ref):
    packed = pabs_ref[:, 256:384]
    values = pabs_ref[:, 0:128]
    labels_row = lab_ref[...]
    labels = column(labels_row)
    order = iota((TILE, TILE), 0) >= iota((TILE, TILE), 1)
    moved = [dot(packed, q_to_k(head)).astype(BF) for head in range(2)]
    ext = [extended(values, head) for head in range(2)]
    count = TEAM_ROWS // TILE
    for i in range(count):
        rows = slice(i * TILE, (i + 1) * TILE)
        total = [jnp.zeros((TILE, 128), F32) for _ in range(2)]
        for j in range(i + 1):
            cols = slice(j * TILE, (j + 1) * TILE)
            mask = tile_mask(labels, labels_row, i, j)
            if i == j:
                mask = mask & order
            for head in range(2):
                inner = dot_nt(moved[head][rows], packed[cols])
                weight = 1.0 + inner * (0.25 + inner * (1.0 / 32.0))
                weight = jnp.where(mask, weight, 0.0).astype(BF)
                total[head] = total[head] + dot(weight, ext[head][cols])
        for head in range(2):
            tot_ref[head, rows, :] = total[head]


def normalised(total, head):
    lane = iota(total.shape, 1)
    mass = jnp.sum(jnp.where(lane == one_lane(head), total, 0.0), 1, keepdims=True)
    inside = head_lanes(head, total.shape[0])
    attended = jnp.where(inside, total / mass, 0.0)
    mean = jnp.sum(attended * attended, 1, keepdims=True) * (1.0 / 64.0)
    return attended, mass, lax.rsqrt(mean + EPSILON)


def carried_query(packed, head):
    lane = iota(packed.shape, 1)
    moved = dot(packed, q_to_k(head)) * 0.25
    return jnp.where(lane == ONE, 1.0, moved).astype(BF)


def join_kernel(order, pabs_ref, lab_ref, local_ref, came_ref, taps_ref, wo_ref, tot_ref, mixed_ref, *send_refs):
    packed = pabs_ref[:, 256:384]
    values = pabs_ref[:, 0:128].astype(F32)
    labels = column(lab_ref[...])
    carried = came_ref[TAIL + 16 : TAIL + 17, :].astype(F32) - 1.0
    usable = labels == carried
    attn = jnp.zeros((TEAM_ROWS, 128), F32)
    for head in range(2):
        at = head * STATE
        first = 16 * head
        outer = dot_nt(packed, spread(first, 0)) * dot_nt(packed, spread(first, 1))
        brought = dot(outer.astype(BF), came_ref[at : at + 256, :]) * (1.0 / 32.0)
        brought = brought + dot(carried_query(packed, head), came_ref[at + 256 : at + 384, :])
        total = local_ref[head] + jnp.where(usable, brought, 0.0)
        tot_ref[head] = total
        attended, _, scale = normalised(total, head)
        attn = attn + attended * scale
    tail = came_ref[TAIL : TAIL + 16, :].astype(F32)
    back_1, back_2, _, _ = conv_parts(values, tail, labels, carried)
    conv = taps_ref[0:1] * values + taps_ref[1:2] * back_1 + taps_ref[2:3] * back_2
    mixed = (attn + conv * pabs_ref[:, 128:256].astype(F32)).astype(BF)
    for block in range(8):
        start = pl.multiple_of(order[block] * ROWS, ROWS)
        mixed_ref[pl.ds(start, ROWS), :] = mixed[block * ROWS : (block + 1) * ROWS]
    part = dot(mixed_ref[512:, :], wo_ref[...])
    for hop in range(4):
        send_refs[hop][...] = part[hop * ROWS : (hop + 1) * ROWS].astype(BF)


def split_sum(total, got_refs, own_ref, piece_refs):
    own_ref[...] = total(0) + got_refs[0][...].astype(F32)
    for hop in (1, 2, 3):
        piece_refs[hop - 1][...] = (total(hop) + got_refs[hop][...].astype(F32)).astype(BF)


def mix_sum_kernel(left_ref, right_ref, *refs):
    total = dot(left_ref[0:512, :], right_ref[...])
    split_sum(lambda hop: total[hop * ROWS : (hop + 1) * ROWS], refs[:4], refs[4], refs[5:])


def add_kernel(mine_ref, *refs):
    split_sum(lambda hop: mine_ref[hop * ROWS : (hop + 1) * ROWS, :], refs[:4], refs[4], refs[5:])


def back_sum_kernel(left_ref, right_ref, *refs):
    total = dot_nt(left_ref[0:512, :], right_ref[...])
    split_sum(lambda hop: total[hop * ROWS : (hop + 1) * ROWS], refs[:4], refs[4], refs[5:])


def send_kernel(left_ref, right_ref, *send_refs):
    total = dot(left_ref[...], right_ref[...])
    for hop in range(4):
        send_refs[hop][...] = total[hop * ROWS : (hop + 1) * ROWS].astype(BF)


def norm_kernel(field_ref, own_ref, a_ref, b_ref, c_ref, after_ref, act_ref):
    came = a_ref[...].astype(F32) + b_ref[...].astype(F32) + c_ref[...].astype(F32)
    after = field_ref[...].astype(F32) + own_ref[...] + came
    after_ref[...] = after
    act_ref[...] = unit(after)[0].astype(BF)


def result_kernel(after_ref, own_ref, a_ref, b_ref, c_ref, out_ref):
    came = a_ref[...].astype(F32) + b_ref[...].astype(F32) + c_ref[...].astype(F32)
    out_ref[...] = (after_ref[...] + own_ref[...] + came).astype(BF)


def norm_back_kernel(field_ref, base_ref, own_ref, a_ref, b_ref, c_ref, *out_refs):
    upstream = a_ref[...].astype(F32) + b_ref[...].astype(F32) + c_ref[...].astype(F32)
    upstream = upstream + own_ref[...]
    field = field_ref[...].astype(F32)
    total = base_ref[...].astype(F32) + unit_back(field, unit(field)[1], upstream)
    for ref in out_refs:
        ref[...] = total.astype(ref.dtype)


def norm_mid_kernel(*refs):
    norm_back_kernel(*refs)


def ffn_own_kernel(*refs):
    ffn_kernel(*refs, half=0)


def ffn_other_kernel(*refs):
    ffn_kernel(*refs, half=1)


def ffn_kernel(*refs, half):
    acts, (cot_ref, w_ref, wd_ref) = refs[0:4], refs[4:7]
    hidden_ref, pair_ref, part_refs = refs[7], refs[8], refs[9:]
    for at in range(2):
        rows = slice(at * TILE, (at + 1) * TILE)
        act = jnp.concatenate([ref[...] for ref in acts[2 * at : 2 * at + 2]], 0)
        both = dot(act, w_ref[...])
        gate, up = both[:, 0:384], both[:, 384:768]
        d_hidden = dot_nt(cot_ref[half * 512 + at * TILE : half * 512 + (at + 1) * TILE, :], wd_ref[...])
        sigma = 1.0 / (1.0 + jnp.exp(-gate))
        swish = gate * sigma
        hidden_ref[rows, :] = (swish * up).astype(BF)
        pair_ref[rows, 0:384] = (d_hidden * up * sigma * (1.0 + gate * (1.0 - sigma))).astype(BF)
        pair_ref[rows, 384:768] = (d_hidden * swish).astype(BF)
        part = dot_nt(pair_ref[rows, :], w_ref[...])
        if len(part_refs) == 1:
            part_refs[0][rows, :] = part
        else:
            part_refs[2 * at][...] = part[0:ROWS].astype(BF)
            part_refs[2 * at + 1][...] = part[ROWS:].astype(BF)


def ffn_grad_kernel(*refs):
    acts, (cot_ref, pair_1, pair_2, hid_1, hid_2) = refs[0:8], refs[8:13]
    out_ref, act_ref, sum_ref = refs[13:]
    for place in range(8):
        act_ref[place * ROWS : (place + 1) * ROWS, :] = acts[place][...]
    for at in range(0, 1024, TILE):
        cols = slice(at, at + TILE)
        total = dot_tn(act_ref[0:512, cols], pair_1[...]) + dot_tn(act_ref[512:, cols], pair_2[...])
        for g in range(4):
            for l in range(3):
                part = total[g * 64 : (g + 1) * 64, l * 256 : (l + 1) * 256]
                out_ref[at // 64 + g, l * 64 : (l + 1) * 64] = part.astype(BF)
    for at in range(0, 384, 128):
        cols = slice(at, at + 128)
        total = dot_tn(hid_1[:, cols], cot_ref[0:512, :]) + dot_tn(hid_2[:, cols], cot_ref[512:, :])
        sum_ref[cols, :] = total
    for g in range(16):
        rows = sum_ref[g * 22 : (g + 1) * 22, :]
        for l in range(2):
            left, right = rows[:, l * 256 : (l + 1) * 256], rows[:, 512 + l * 256 : 768 + l * 256]
            part = jnp.concatenate([left, right, jnp.zeros((4, 256), F32)], 0)
            out_ref[g, 192 + l * 48 : 240 + l * 48] = part.astype(BF)


def sum_ffn_kernel(came_ref, two_ref, down_ref):
    total = came_ref[0].astype(F32)
    for g in range(1, 16):
        total = total + came_ref[g].astype(F32)
    two_ref[...] = total[0:192]
    down_ref[...] = total[192:288]


def owner_kernel(*refs):
    sum_ref, down_ref, out_ref, wq, wk, wv, wc, wg, wu, *small = refs[:12]
    gq, gk, gv, gc, gg, gu, gd, go, d1_ref, d2_ref, dt_ref = refs[12:]
    parts = [down_ref[l * 48 : l * 48 + 48] for l in range(2)]
    gd[...] = jnp.concatenate([p[0:22] for p in parts] + [p[22:44] for p in parts], 1)
    parts = [out_ref[l * 16 : l * 16 + 16] for l in range(4)]
    go[...] = jnp.concatenate([p[0:8] for p in parts] + [p[8:16] for p in parts], 1)
    turned = small_rows(*small)
    taps = jnp.zeros((8, 128), F32)
    for t in range(8):
        taps = taps + sum_ref[t, :, 256:384]
    dt_ref[...] = jnp.transpose(taps)[64:67, 0:8]
    diagonal = iota((8, 128), 0) == iota((8, 128), 1)
    one, two = turned[:, 0:1], turned[:, 1:2]
    raw = [sum_ref[t] for t in range(8)]
    value = jnp.concatenate([part[:, 0:128] for part in raw], 1)
    gate_c = jnp.concatenate([part[:, 128:256] for part in raw], 1)
    query = jnp.concatenate([part[:, 256:288] for part in raw], 1)
    key = jnp.concatenate([part[:, 288:320] for part in raw], 1)
    gate = jnp.concatenate([part[:, 384:736] for part in raw], 1)
    up = jnp.concatenate([part[:, 768:1120] for part in raw], 1)
    total = jnp.zeros((8, 1), F32)
    for weight, field, out in ((wq, query, gq), (wk, key, gk), (wv, value, gv), (wc, gate_c, gc)):
        total = total + jnp.sum(weight[...].astype(F32) * field, 1, keepdims=True)
        out[...] = field * one
    d1_ref[...] = jnp.sum(jnp.where(diagonal, total, 0.0), 0, keepdims=True)[:, 0:8]
    total = jnp.zeros((8, 1), F32)
    for weight, field, out in ((wg, gate, gg), (wu, up, gu)):
        total = total + jnp.sum(weight[...].astype(F32) * field, 1, keepdims=True)
        out[...] = field * two
    d2_ref[...] = jnp.sum(jnp.where(diagonal, total, 0.0), 0, keepdims=True)[:, 0:8]


def back_state_kernel(order, *refs):
    blocks, (pabs_ref, lab_ref, tot_ref, came_ref, taps_ref, wo_ref) = refs[:8], refs[8:14]
    de_ref, dvconv_ref, dgate_ref, dtaps_ref, pay_ref, dm_ref = refs[14:]
    for place in range(8):
        start = pl.multiple_of(order[9 + place] * ROWS, ROWS)
        dm_ref[pl.ds(start, ROWS), :] = dot_nt(blocks[place][...], wo_ref[...])
    d_mixed = dm_ref[...]
    packed = pabs_ref[:, 256:384]
    values = pabs_ref[:, 0:128].astype(F32)
    labels = column(lab_ref[...])
    carried = came_ref[TAIL + 16 : TAIL + 17, :].astype(F32) - 1.0
    usable = labels == carried
    lane = iota((TEAM_ROWS, 128), 1)
    for head in range(2):
        attended, mass, scale = normalised(tot_ref[head], head)
        d_attn = jnp.where(head_lanes(head, TEAM_ROWS), d_mixed, 0.0)
        pull = jnp.sum(d_attn * attended, 1, keepdims=True) * (1.0 / 64.0)
        d_att = scale * (d_attn - attended * (scale * scale * pull))
        d_mass = -jnp.sum(d_att * attended, 1, keepdims=True) / mass
        d_ext = jnp.where(lane == one_lane(head), d_mass, d_att / mass).astype(BF)
        de_ref[head] = d_ext
        d_ext = jnp.where(usable, d_ext, jnp.zeros_like(d_ext))
        first = 16 * head
        at = head * STATE
        outer = dot_nt(spread(first, 0), packed) * dot_nt(spread(first, 1), packed)
        pay_ref[at : at + 256, :] = (dot(outer.astype(BF), d_ext) * (1.0 / 32.0)).astype(BF)
        turned = dot_nt(identity(), carried_query(packed, head)).astype(BF)
        pay_ref[at + 256 : at + 384, :] = dot(turned, d_ext).astype(BF)
    tail = came_ref[TAIL : TAIL + 16, :].astype(F32)
    back_1, back_2, mask_1, mask_2 = conv_parts(values, tail, labels, carried)
    conv = taps_ref[0:1] * values + taps_ref[1:2] * back_1 + taps_ref[2:3] * back_2
    dgate_ref[...] = (d_mixed * conv).astype(BF)
    d_conv = d_mixed * pabs_ref[:, 128:256].astype(F32)
    row8 = iota((8, 128), 0)
    sums = [jnp.sum(d_conv * part, 0, keepdims=True) for part in (values, back_1, back_2)]
    d_taps = jnp.zeros((8, 128), F32)
    for at in range(3):
        d_taps = jnp.where(row8 == at, sums[at], d_taps)
    dtaps_ref[...] = d_taps
    part_1 = jnp.where(mask_1, taps_ref[1:2] * d_conv, 0.0)
    part_2 = jnp.where(mask_2, taps_ref[2:3] * d_conv, 0.0)
    row = iota((TEAM_ROWS, 128), 0)
    up_1 = jnp.where(row < TEAM_ROWS - 1, pltpu.roll(part_1, TEAM_ROWS - 1, 0), 0.0)
    up_2 = jnp.where(row < TEAM_ROWS - 2, pltpu.roll(part_2, TEAM_ROWS - 2, 0), 0.0)
    dvconv_ref[...] = taps_ref[0:1] * d_conv + up_1 + up_2
    row16 = iota((16, 128), 0)
    edge = jnp.where(row16 == 14, part_2[0:1], 0.0)
    edge = jnp.where(row16 == 15, part_1[0:1] + part_2[1:2], edge)
    pay_ref[TAIL : TAIL + 16, :] = edge.astype(BF)
    pay_ref[TAIL + 16 : TAIL + 32, :] = jnp.zeros((16, 128), BF)


def back_local_kernel(pabs_ref, lab_ref, de_ref, came_ref, dqk_ref, dv_ref, dqt_ref):
    packed = pabs_ref[:, 256:384]
    values = pabs_ref[:, 0:128]
    labels_row = lab_ref[...]
    labels = column(labels_row)
    order = iota((TILE, TILE), 0) <= iota((TILE, TILE), 1)
    moved = [dot(packed, q_to_k(head)).astype(BF) for head in range(2)]
    keys_t = [dot_nt(q_to_k(head), packed).astype(BF) for head in range(2)]
    ext = [extended(values, head) for head in range(2)]
    inside = [head_lanes(head, TILE) for head in range(2)]
    count = TEAM_ROWS // TILE
    dqt_ref[...] = jnp.zeros((128, TEAM_ROWS), F32)
    for j in range(count):
        cols = slice(j * TILE, (j + 1) * TILE)
        d_key = jnp.zeros((TILE, 128), F32)
        d_val = jnp.zeros((TILE, 128), F32)
        for i in range(j, count):
            rows = slice(i * TILE, (i + 1) * TILE)
            mask = tile_mask(labels, labels_row, j, i)
            if i == j:
                mask = mask & order
            for head in range(2):
                d_ext = de_ref[head, rows, :]
                inner = dot_nt(packed[cols], moved[head][rows])
                weight = 1.0 + inner * (0.25 + inner * (1.0 / 32.0))
                weight = jnp.where(mask, weight, 0.0).astype(BF)
                d_weight = dot_nt(ext[head][cols], d_ext)
                d_inner = jnp.where(mask, d_weight * (0.25 + inner * (1.0 / 16.0)), 0.0).astype(BF)
                d_sum = jnp.where(inside[head], d_ext, jnp.zeros_like(d_ext))
                d_val = d_val + dot(weight, d_sum)
                d_key = d_key + dot(d_inner, moved[head][rows])
                dqt_ref[:, rows] += dot(keys_t[head][:, cols], d_inner)
        dqk_ref[cols, :] = d_key
        dv_ref[cols, :] = d_val
    carried = came_ref[TAIL + 16 : TAIL + 17, :].astype(F32) - 1.0
    usable = labels == carried
    total = dqk_ref[...] + jnp.transpose(dqt_ref[...])
    for head in range(2):
        d_ext = de_ref[head]
        d_ext = jnp.where(usable, d_ext, jnp.zeros_like(d_ext))
        at = head * STATE
        first = 16 * head
        d_outer = dot_nt(d_ext, came_ref[at : at + 256, :]) * dot_nt(packed, spread(first, 1))
        total = total + dot((d_outer * (1.0 / 16.0)).astype(BF), spread(first, 0))
        d_line = dot_nt(d_ext, came_ref[at + 256 : at + 384, :]) * 0.25
        total = total + dot_nt(d_line.astype(BF), q_to_k(head))
    dqk_ref[...] = total


def back_join_kernel(order, pabs_ref, lab_ref, dqk_ref, dv_ref, dvconv_ref, dgate_ref, came_ref, w_ref, out_ref, *send_refs):
    packed = pabs_ref[:, 256:384]
    values = pabs_ref[:, 0:128]
    labels = column(lab_ref[...])
    keep = labels == labels[TEAM_ROWS - 1 : TEAM_ROWS]
    lane = iota((TEAM_ROWS, 128), 1)
    d_val = dv_ref[...] + dvconv_ref[...]
    d_qk = dqk_ref[...]
    edge = jnp.where(keep[TEAM_ROWS - 16 :], came_ref[TAIL : TAIL + 16, :].astype(F32), 0.0)
    edge = jnp.concatenate([jnp.zeros((TEAM_ROWS - 16, 128), F32), edge], 0)
    d_val = d_val + edge
    for head in range(2):
        at = head * STATE
        first = KLANE + 16 * head
        d_two = came_ref[at : at + 256, :]
        d_one = came_ref[at + 256 : at + 384, :]
        ext = jnp.where(keep, extended(values, head), jnp.zeros_like(values))
        left = dot_nt(packed, spread(first, 0))
        right = dot_nt(packed, spread(first, 1))
        key_lanes = (lane >= first) & (lane < first + 16)
        line = jnp.where(key_lanes | (lane == ONE), packed, jnp.zeros_like(packed))
        d_ext = dot((left * right).astype(BF), d_two) + dot(line, d_one)
        d_val = d_val + jnp.where(keep & head_lanes(head, TEAM_ROWS), d_ext, 0.0)
        d_outer = dot_nt(ext, d_two) * right
        d_qk = d_qk + dot((d_outer * 2.0).astype(BF), spread(first, 0))
        d_qk = d_qk + jnp.where(key_lanes, dot_nt(ext, d_one), 0.0)
    d_val = d_val.astype(BF)
    d_qk = d_qk.astype(BF)
    for block in range(8):
        start = pl.multiple_of(order[block] * ROWS, ROWS)
        rows = slice(block * ROWS, (block + 1) * ROWS)
        out_ref[pl.ds(start, ROWS), 0:128] = d_val[rows]
        out_ref[pl.ds(start, ROWS), 128:256] = dgate_ref[rows, :]
        out_ref[pl.ds(start, ROWS), 256:384] = d_qk[rows]
    part = dot_nt(out_ref[512:, :], w_ref[...])
    for hop in range(4):
        send_refs[hop][...] = part[hop * ROWS : (hop + 1) * ROWS].astype(BF)


def mixer_grad_kernel(order, *refs):
    blocks, (mixed_ref, dtaps_ref, act_ref, dp_ref) = refs[:8], refs[8:12]
    grad_ref, sum_ref = refs[12:]
    for at in range(0, 1024, TILE):
        sum_ref[at : at + TILE, :] = dot(act_ref[at : at + TILE, :], dp_ref[...])
    start = pl.multiple_of(order[8] * 128, 128)
    spare = [jnp.zeros((64, 128), F32), dtaps_ref[...], jnp.zeros((56, 128), F32)]
    sum_ref[pl.ds(start, 128), 256:384] += jnp.transpose(jnp.concatenate(spare, 0))
    d_out = jnp.zeros((128, 1024), F32)
    for place in range(8):
        rows = slice(place * ROWS, (place + 1) * ROWS)
        d_out = d_out + dot_tn(mixed_ref[rows, :], blocks[place][...])
    for g in range(16):
        for l in range(3):
            part = sum_ref[g * 64 : (g + 1) * 64, l * 128 : (l + 1) * 128]
            grad_ref[g, l * 64 : (l + 1) * 64] = part.astype(BF)
        rows = d_out[g * 8 : (g + 1) * 8]
        for l in range(4):
            part = [rows[:, l * 128 : (l + 1) * 128], rows[:, 512 + l * 128 : 640 + l * 128]]
            grad_ref[g, 192 + l * 16 : 208 + l * 16] = jnp.concatenate(part, 0).astype(BF)


def sum_mixer_kernel(came_ref, other_ref, sum_ref, out_ref):
    total = came_ref[0].astype(F32)
    for g in range(1, 16):
        total = total + came_ref[g].astype(F32)
    for l in range(3):
        for t in range(8):
            rows = slice(l * 64 + t * 8, l * 64 + t * 8 + 8)
            sum_ref[t, :, l * 128 : (l + 1) * 128] = total[rows]
            sum_ref[t, :, 384 + l * 256 : 640 + l * 256] = other_ref[rows, :]
    out_ref[...] = total[192:256]


def call(kernel, outs, args, ordered=False, scratch=(), far=(), far_outs=(), lazy=False, grant=16):
    specs = [pl.BlockSpec(memory_space=pltpu.HBM if i in far else pltpu.VMEM) for i in range(len(args))]
    if ordered:
        specs[0] = pl.BlockSpec(memory_space=pltpu.SMEM)
    out_specs = [
        pl.BlockSpec(memory_space=pltpu.HBM if i in far_outs else pltpu.VMEM) for i in range(len(outs))
    ]
    rooms = [pltpu.VMEM(args[i].shape, args[i].dtype) for i in far]
    rooms += [pltpu.VMEM(outs[i].shape, outs[i].dtype) for i in far_outs]
    sems = [pltpu.SemaphoreType.DMA((len(rooms),))] if rooms else []

    def body(*refs):
        ins, results = list(refs[: len(args)]), list(refs[len(args) : len(args) + len(outs)])
        own = refs[len(args) + len(outs) :]
        own, room = own[: len(scratch)], own[len(scratch) :]
        reads, writes, sent = [], [], set()
        for at, i in enumerate(far):
            reads.append(pltpu.make_async_copy(ins[i], room[at], room[-1].at[at]))
            ins[i] = room[at]
        for at, i in enumerate(far_outs, len(far)):
            writes.append(pltpu.make_async_copy(room[at], results[i], room[-1].at[at]))
            results[i] = room[at]
        for copy in reads:
            copy.start()

        def put(at):
            sent.add(at)
            writes[at].start()

        def get(at):
            reads[at].wait()

        if lazy:
            kernel(*ins, *results, *own, get=get, put=put)
        else:
            for copy in reads:
                copy.wait()
            kernel(*ins, *results, *own)
        for at in range(len(writes)):
            if at not in sent:
                put(at)
        for copy in writes:
            copy.wait()

    micros = TIMES[kernel.__name__]
    return pl.pallas_call(
        body,
        out_shape=tuple(outs),
        in_specs=specs,
        out_specs=tuple(out_specs),
        scratch_shapes=list(scratch) + rooms + sems,
        cost_estimate=pl.CostEstimate(
            flops=int(micros * 1.15e9), bytes_accessed=int(micros * 3.6e6), transcendentals=0
        ),
        compiler_params=pltpu.CompilerParams(vmem_limit_bytes=grant * MIB),
    )(*args)


def shape(*sizes):
    return jax.ShapeDtypeStruct(sizes[:-1], sizes[-1])


def exchange(blocks, axes):
    return lax.all_to_all(blocks, axes, 0, 0, tiled=True)


def unit(field):
    scale = lax.rsqrt(jnp.mean(field * field, -1, keepdims=True) + EPSILON)
    return field * scale, scale


def unit_back(field, scale, upstream):
    pull = jnp.mean(field * upstream, -1, keepdims=True)
    return scale * upstream - field * (scale * scale * scale * pull)


def per_device(
    inputs, segments, cotangent, attn_gain, w_query, w_key, w_value, w_conv_gate,
    conv_kernel, w_output, ffn_gain, w_ffn_gate, w_ffn_up, w_ffn_down,
):
    x, core = lax.axis_index("x"), lax.axis_index("core")
    block = jnp.arange(8, dtype=jnp.int32)
    order = ((block % 2) ^ core) * 4 + (block // 2 - x) % 4
    back = 2 * ((block % 4 + x) % 4) + ((block // 4) ^ core)
    order = jnp.concatenate([order, jnp.full((1,), x * 2 + core, jnp.int32), back])
    small = (attn_gain[None], ffn_gain[None], conv_kernel)
    to_team = [(f, (f % 16) * 8 + f // 16) for f in range(128)]
    to_owner = [(place, f) for f, place in to_team]

    weights = (
        w_query, w_key, w_value, w_conv_gate, w_ffn_gate, w_ffn_up, w_output, w_ffn_down, *small,
    )
    pack, whole = call(
        pack_kernel,
        [shape(8, 8, 1152, BF), shape(64, 512, BF)],
        weights,
        far=range(11),
        grant=60,
    )
    mine = exchange(pack, TEAM).reshape(64, 1152)
    ready = whole
    whole = lax.ppermute(whole, AXES, to_team)
    (tiles,) = call(spread_mixer_kernel, [shape(16, 256, 128, BF)], (mine, whole))
    mixer_came = exchange(tiles, GROUP)

    (block,) = call(
        block_kernel,
        [shape(BLOCK, 1024, BF)],
        (tie(inputs, ready), cotangent, segments[None]),
    )
    own_x = own_gather(block)
    other_x = other_gather(own_x)

    act_one, codes, cot = call(
        act_kernel,
        [shape(TEAM_ROWS, 1024, BF), shape(8, 128, F32), shape(TEAM_ROWS, 1024, BF)],
        (*own_x, *other_x),
    )
    pabs, payload, labels, taps, weight_1, weight_o = call(
        state_kernel,
        [
            shape(TEAM_ROWS, 384, BF),
            shape(PAYLOAD, 128, BF),
            shape(1, TEAM_ROWS, F32),
            shape(8, 128, F32),
            shape(1024, 384, BF),
            shape(128, 1024, BF),
        ],
        (order, act_one, codes, mixer_came),
        True,
        [pltpu.VMEM((TEAM_ROWS, 384), BF)],
    )
    came = lax.ppermute(payload, "zh", [(0, 1)])
    (local,) = call(local_kernel, [shape(2, TEAM_ROWS, 128, F32)], (pabs, labels))
    rows_f, rows_b = shape(ROWS, 1024, F32), shape(ROWS, 1024, BF)
    total, mixed, *sends = call(
        join_kernel,
        [shape(2, TEAM_ROWS, 128, F32), shape(TEAM_ROWS, 128, BF)] + [rows_b] * 4,
        (order, pabs, labels, local, came, taps, weight_o),
        True,
    )
    pieces = [rows_f] + [rows_b] * 3
    got = swap_all(sends)
    own, *rest = call(mix_sum_kernel, pieces, (mixed, weight_o, *got))
    (tiles,) = call(spread_ffn_kernel, [shape(16, 288, 256, BF)], (tie(mine, mixer_came), whole))
    ffn_came = exchange(tie(tiles, payload), GROUP)
    after_mixer, own_two = call(norm_kernel, [rows_f, rows_b], (inputs, own, *own_scatter(rest)))
    (act_turned,) = call(turn_kernel, [shape(1024, TEAM_ROWS, BF)], (tie(act_one, own),))

    own_act = own_gather(tie(own_two, act_turned))
    weight_2, weight_d = call(
        ffn_weights_kernel,
        [shape(1024, 768, BF), shape(384, 1024, BF)],
        (tie(ffn_came, own_act[1]),),
        grant=60,
    )
    other_act = other_gather(own_act)
    halves = [shape(512, 384, BF), shape(512, 768, BF)]
    other_hidden, other_pair, *sends = call(
        ffn_other_kernel, halves + [rows_b] * 4, (*other_act, cot, weight_2, weight_d)
    )
    got = swap_all(sends)
    own_hidden, own_pair, part = call(
        ffn_own_kernel,
        halves + [shape(512, 1024, F32)],
        (*own_act, cot, weight_2, weight_d),
    )
    own, *rest = call(add_kernel, pieces, (part, *got))
    (grad_2,) = call(
        ffn_grad_kernel,
        [shape(16, 288, 256, BF)],
        (
            *own_act, *other_act, tie(cot, own),
            own_pair, other_pair, own_hidden, other_hidden,
        ),
        scratch=[
            pltpu.VMEM((1024, 1024), BF),
            pltpu.VMEM((384, 1024), F32),
        ],
    )
    two_came = own_scatter(rest)
    d_after, own_branch = call(
        norm_mid_kernel,
        [rows_f, rows_b],
        (after_mixer, cotangent, own, *two_came),
        far=range(6),
        far_outs=(0, 1),
        grant=60,
    )
    own_branch = tie(own_branch, grad_2)
    grad_2 = exchange(grad_2, GROUP)
    sends = call(send_kernel, [rows_b] * 4, (tie(other_hidden, own_branch), weight_d))
    got = swap_all(sends)
    own_branch = own_gather(own_branch)
    d_branch = (*own_branch, *other_gather(own_branch))
    result_own, *rest = call(mix_sum_kernel, pieces, (own_hidden, weight_d, *got))
    result_came = own_scatter(tie_all(rest, own_branch[1]))
    (result,) = call(result_kernel, [rows_b], (after_mixer, result_own, *result_came))

    d_ext, d_val_conv, d_gate_c, d_taps, payload = call(
        back_state_kernel,
        [
            shape(2, TEAM_ROWS, 128, BF),
            shape(TEAM_ROWS, 128, F32),
            shape(TEAM_ROWS, 128, BF),
            shape(8, 128, F32),
            shape(PAYLOAD, 128, BF),
        ],
        (order, *d_branch, pabs, labels, total, came, taps, weight_o),
        True,
        [pltpu.VMEM((TEAM_ROWS, 128), F32)],
    )
    came_2 = lax.ppermute(payload, "zh", [(1, 0)])
    d_qk, d_val = call(
        back_local_kernel,
        [shape(TEAM_ROWS, 128, F32), shape(TEAM_ROWS, 128, F32)],
        (pabs, labels, d_ext, came),
        scratch=[pltpu.VMEM((128, TEAM_ROWS), F32)],
    )
    d_projected, *sends = call(
        back_join_kernel,
        [shape(TEAM_ROWS, 384, BF)] + [rows_b] * 4,
        (
            order, pabs, labels, d_qk, d_val, d_val_conv, d_gate_c, tie(came_2, result),
            weight_1,
        ),
        True,
    )
    got = swap_all(sends)
    (grad_1,) = call(
        mixer_grad_kernel,
        [shape(16, 256, 128, BF)],
        (order, *d_branch, mixed, d_taps, act_turned, d_projected),
        True,
        [pltpu.VMEM((TEAM_ROWS, 384), F32)],
    )
    sum_2, sum_d = call(
        sum_ffn_kernel, [shape(192, 256, F32), shape(96, 256, F32)], (grad_2,)
    )
    own, *rest = call(
        back_sum_kernel,
        pieces,
        (d_projected, weight_1, *got),
        far=range(6),
        far_outs=range(4),
        grant=60,
    )
    grad_1 = exchange(tie(grad_1, grad_2, *got), GROUP)
    last = own_scatter(rest)
    grad_1 = tie(grad_1, last[0])
    (d_inputs,) = call(norm_back_kernel, [rows_b], (inputs, d_after, own, *last))

    sum_d = lax.ppermute(sum_d, AXES, to_owner)
    sums, sum_o = call(
        sum_mixer_kernel, [shape(8, 8, 1152, F32), shape(64, 128, F32)], (grad_1, sum_2)
    )
    sum_o = lax.ppermute(sum_o, AXES, to_owner)
    sums = exchange(sums, TEAM)
    gq, gk, gv, gc, gg, gu, gd, go, gain_grad_1, gain_grad_2, grad_taps = call(
        owner_kernel,
        [shape(8, cols, F32) for cols in (256, 256, 1024, 1024, 2816, 2816)]
        + [shape(22, 1024, F32), shape(8, 1024, F32)]
        + [shape(1, 8, F32), shape(1, 8, F32), shape(3, 8, F32)],
        (sums, sum_d, sum_o, *weights[:6], *small),
        far=range(12),
        grant=60,
    )
    return (
        result, d_inputs, gain_grad_1[0], gq, gk, gv, gc, grad_taps, go,
        gain_grad_2[0], gg, gu, gd,
    )


def solution(mesh):
    fine = Mesh(mesh.devices.reshape(SIZES), AXES)
    row, vector, taps = P(AXES, None), P(AXES), P(None, AXES)
    return jax.shard_map(
        per_device,
        mesh=fine,
        in_specs=(row, vector, row, vector, row, row, row, row, taps, row, vector, row, row, row),
        out_specs=(row, row, vector, row, row, row, row, taps, row, vector, row, row, row),
        check_vma=False,
    )
```

```python
import functools

import jax
import jax.numpy as jnp
from jax import lax
from jax.experimental import pallas as pl
from jax.experimental.pallas import tpu as pltpu
from jax.sharding import Mesh, PartitionSpec as P

EPSILON = 1e-05
BF = jnp.bfloat16
F32 = jnp.float32

AXES = ("zl", "y", "zh", "x", "core")
SIZES = (2, 4, 2, 4, 2)
GROUP = ("zl", "y", "zh")
TEAM = ("x", "core")
ROWS = 128
COT = 144
BLOCK = 272
TEAM_ROWS = 1024
TILE = 256
KLANE = 32
ONE = 64
STATE = 384
TAIL = 2 * STATE
PAYLOAD = TAIL + 32
MIB = 1024 * 1024
TIMES = {
    "pack_kernel": 2,
    "turn_kernel": 1.5,
    "block_kernel": 1,
    "spread_mixer_kernel": 1.2,
    "state_kernel": 0.2,
    "act_kernel": 14,
    "local_kernel": 0.2,
    "join_kernel": 2.6,
    "mix_sum_kernel": 1,
    "spread_ffn_kernel": 1.8,
    "norm_kernel": 12,
    "ffn_weights_kernel": 3,
    "ffn_own_kernel": 3.8,
    "ffn_other_kernel": 3.8,
    "add_kernel": 0.3,
    "ffn_grad_kernel": 4.2,
    "norm_back_kernel": 1,
    "norm_mid_kernel": 30,
    "send_kernel": 0.7,
    "back_state_kernel": 0.2,
    "back_local_kernel": 0.2,
    "back_join_kernel": 0.2,
    "mixer_grad_kernel": 0.2,
    "back_sum_kernel": 1.6,
    "sum_ffn_kernel": 2,
    "sum_mixer_kernel": 0.8,
    "result_kernel": 0.8,
    "owner_kernel": 2,
}


def from_x(block, hop):
    return lax.ppermute(block, "x", [(i, (i - hop) % 4) for i in range(4)])


def to_x(block, hop):
    return lax.ppermute(block, "x", [(i, (i + hop) % 4) for i in range(4)])


def swap_core(block):
    return lax.ppermute(block, "core", [(0, 1), (1, 0)])


def own_gather(block):
    return [block] + [from_x(block, hop) for hop in (1, 2, 3)]


def other_gather(own):
    return [swap_core(part) for part in (tie(own[0], own[1]), *own[1:])]


def swap_all(parts):
    return [swap_core(part) for part in parts]


def own_scatter(pieces):
    return [to_x(piece, hop) for hop, piece in zip((1, 2, 3), pieces)]


def tie(value, *before):
    return lax.optimization_barrier((value,) + before)[0]


def tie_all(values, *before):
    return list(lax.optimization_barrier((*values, *before)))[: len(values)]


def dot(left, right):
    return jnp.dot(left, right, preferred_element_type=F32)


def dot_nt(left, right):
    return lax.dot_general(left, right, (((1,), (1,)), ((), ())), preferred_element_type=F32)


def dot_tn(left, right):
    return lax.dot_general(left, right, (((0,), (0,)), ((), ())), preferred_element_type=F32)


def iota(shape, dim):
    return lax.broadcasted_iota(jnp.int32, shape, dim)


def one_hot(condition):
    return jnp.where(condition, 1.0, 0.0).astype(BF)


def spread(first, which):
    row, lane = iota((256, 128), 0), iota((256, 128), 1)
    part = row // 16 if which == 0 else row % 16
    return one_hot(lane == first + part)


def q_to_k(head):
    row, lane = iota((128, 128), 0), iota((128, 128), 1)
    low = 16 * head
    return one_hot((lane == row + KLANE) & (row >= low) & (row < low + 16))


def identity():
    return one_hot(iota((128, 128), 0) == iota((128, 128), 1))


def head_lanes(head, rows):
    lane = iota((rows, 128), 1)
    return lane < 64 if head == 0 else lane >= 64


def one_lane(head):
    return 64 if head == 0 else 0


def extended(values, head):
    rows = values.shape[0]
    lane = iota((rows, 128), 1)
    ones = jnp.where(lane == one_lane(head), 1.0, 0.0).astype(values.dtype)
    return jnp.where(head_lanes(head, rows), values, ones)


def column(labels_row):
    return jnp.transpose(jnp.broadcast_to(labels_row, (128, TEAM_ROWS)))


def shift_down(field, by, head_rows):
    moved = pltpu.roll(field, by, 0)
    row = iota(field.shape, 0)
    for at in range(by):
        moved = jnp.where(row == at, head_rows[at : at + 1], moved)
    return moved


def conv_parts(values, tail, labels, carried):
    back_1 = shift_down(values, 1, tail[15:16])
    back_2 = shift_down(values, 2, tail[14:16])
    carried_2 = jnp.broadcast_to(carried, (2, 128))
    mask_1 = shift_down(labels, 1, carried_2) == labels
    mask_2 = shift_down(labels, 2, carried_2) == labels
    return (
        jnp.where(mask_1, back_1, 0.0),
        jnp.where(mask_2, back_2, 0.0),
        mask_1,
        mask_2,
    )


def tile_mask(labels_col, labels_row, i, j):
    col = labels_col[i * TILE : (i + 1) * TILE]
    col = jnp.concatenate([col] * (TILE // 128), 1)
    row = labels_row[:, j * TILE : (j + 1) * TILE]
    return col == row


def block_kernel(inputs_ref, cot_ref, labels_ref, block_ref):
    labels = jnp.broadcast_to(labels_ref[...], (COT - ROWS, ROWS)).astype(F32)
    block_ref[0:ROWS, :] = inputs_ref[...]
    block_ref[ROWS:COT, :] = jnp.zeros((COT - ROWS, 1024), BF)
    block_ref[ROWS:COT, 0:ROWS] = labels.astype(BF)
    block_ref[COT:BLOCK, :] = cot_ref[...]


def turn_kernel(field_ref, out_ref):
    for at in range(0, 1024, TILE):
        out_ref[at : at + TILE, :] = jnp.transpose(field_ref[:, at : at + TILE])


def small_rows(gain_1, gain_2, taps):
    rows = [gain_1[...].astype(F32), gain_2[...].astype(F32), taps[...].astype(F32)]
    rows = jnp.concatenate(rows + [jnp.zeros((3, 8), F32)], 0)
    return jnp.transpose(jnp.concatenate([rows, jnp.zeros((8, 120), F32)], 1))[0:8]


def pack_kernel(wq, wk, wv, wc, wg, wu, wo, wd, gain_1, gain_2, taps, team_ref, whole_ref):
    turned = small_rows(gain_1, gain_2, taps)
    one, two = turned[:, 0:1], turned[:, 1:2]
    value, gate_c = wv[...].astype(F32) * one, wc[...].astype(F32) * one
    query, key = wq[...].astype(F32) * one, wk[...].astype(F32) * one
    gate, up = wg[...].astype(F32) * two, wu[...].astype(F32) * two
    spare = jnp.concatenate([turned[:, 2:5], jnp.zeros((8, 61), F32)], 1)
    for t in range(8):
        team_ref[t, :, 0:128] = value[:, t * 128 : (t + 1) * 128].astype(BF)
        team_ref[t, :, 128:256] = gate_c[:, t * 128 : (t + 1) * 128].astype(BF)
        narrow = [query[:, t * 32 : (t + 1) * 32], key[:, t * 32 : (t + 1) * 32], spare]
        team_ref[t, :, 256:384] = jnp.concatenate(narrow, 1).astype(BF)
        for first, wide in ((384, gate), (768, up)):
            part = [wide[:, t * 352 : (t + 1) * 352], jnp.zeros((8, 32), F32)]
            team_ref[t, :, first : first + 384] = jnp.concatenate(part, 1).astype(BF)
    out = wo[...].astype(F32)
    down = wd[...].astype(F32)
    rows = [out[:, :512], out[:, 512:], down[:, :512], down[:, 512:], jnp.zeros((4, 512), F32)]
    whole_ref[...] = jnp.concatenate(rows, 0).astype(BF)


def spread_mixer_kernel(mine_ref, whole_ref, out_ref):
    rows = [mine_ref[:, l * 128 : (l + 1) * 128] for l in range(3)]
    rows += [whole_ref[0:16, l * 128 : (l + 1) * 128] for l in range(4)]
    rows = jnp.concatenate(rows, 0)
    for g in range(16):
        out_ref[g] = rows


def spread_ffn_kernel(mine_ref, whole_ref, out_ref):
    rows = [mine_ref[:, 384 + l * 256 : 640 + l * 256] for l in range(3)]
    rows += [whole_ref[16:64, l * 256 : (l + 1) * 256] for l in range(2)]
    rows = jnp.concatenate(rows, 0)
    for g in range(16):
        out_ref[g] = rows


def ffn_weights_kernel(came_ref, two_ref, down_ref):
    down_ref[352:384, :] = jnp.zeros((32, 1024), BF)
    for g in range(16):
        for l in range(3):
            two_ref[g * 64 : (g + 1) * 64, l * 256 : (l + 1) * 256] = came_ref[g, l * 64 : (l + 1) * 64]
    for g in range(0, 16, 8):
        rows = []
        for at in range(g, g + 8):
            part = [came_ref[at, 192 + l * 48 : 240 + l * 48].astype(F32) for l in range(2)]
            rows.append(jnp.concatenate([p[0:22] for p in part] + [p[22:44] for p in part], 1))
        down_ref[g * 22 : (g + 8) * 22, :] = jnp.concatenate(rows, 0).astype(BF)


def act_kernel(*refs):
    blocks, act_ref, code_ref, cot_ref = refs[:8], refs[8], refs[9], refs[10]
    for place in range(8):
        ref = blocks[place]
        rows = slice(place * ROWS, (place + 1) * ROWS)
        act_ref[rows, :] = unit(ref[0:ROWS, :].astype(F32))[0].astype(BF)
        code_ref[place : place + 1, :] = ref[ROWS:COT, 0:ROWS].astype(F32)[0:1]
        cot_ref[rows, :] = ref[COT:BLOCK, :]


def state_kernel(
    order, act_ref, code_ref, came_ref, pabs_ref, pay_ref, lab_ref, taps_ref, w_ref, wo_ref, rel_ref
):
    for g in range(16):
        for l in range(3):
            w_ref[g * 64 : (g + 1) * 64, l * 128 : (l + 1) * 128] = came_ref[g, l * 64 : (l + 1) * 64]
    for pair in range(8):
        rows = []
        for g in (2 * pair, 2 * pair + 1):
            part = [came_ref[g, 192 + l * 16 : 208 + l * 16].astype(F32) for l in range(4)]
            rows.append(jnp.concatenate([p[0:8] for p in part] + [p[8:16] for p in part], 1))
        wo_ref[pair * 16 : (pair + 1) * 16, :] = jnp.concatenate(rows, 0).astype(BF)
    start = pl.multiple_of(order[8] * 128, 128)
    taps_ref[...] = jnp.transpose(w_ref[pl.ds(start, 128), 256:384].astype(F32))[64:72]
    for half in range(2):
        rows = slice(half * 512, (half + 1) * 512)
        rel_ref[rows, :] = dot(act_ref[rows, :], w_ref[...]).astype(BF)
    lane = iota((ROWS, 128), 1)
    for block in range(8):
        rows = slice(block * ROWS, (block + 1) * ROWS)
        start = pl.multiple_of(order[block] * ROWS, ROWS)
        pabs_ref[rows, :] = rel_ref[pl.ds(start, ROWS), :]
        packed = pabs_ref[rows, 256:384]
        packed = jnp.where(lane == ONE, jnp.ones_like(packed), packed)
        pabs_ref[rows, 256:384] = jnp.where(lane > ONE, jnp.zeros_like(packed), packed)
        lab_ref[:, rows] = code_ref[pl.ds(order[block], 1), :]
    packed = pabs_ref[:, 256:384]
    values = pabs_ref[:, 0:128]
    labels = column(lab_ref[...])
    last = labels[TEAM_ROWS - 1 : TEAM_ROWS]
    keep = labels == last
    turned = dot_nt(identity(), packed).astype(BF)
    for head in range(2):
        ext = jnp.where(keep, extended(values, head), jnp.zeros_like(values))
        first = KLANE + 16 * head
        outer = dot_nt(spread(first, 0), packed) * dot_nt(spread(first, 1), packed)
        at = head * STATE
        pay_ref[at : at + 256, :] = dot(outer.astype(BF), ext).astype(BF)
        pay_ref[at + 256 : at + 384, :] = dot(turned, ext).astype(BF)
    tail = jnp.where(keep, values, jnp.zeros_like(values))
    pay_ref[TAIL : TAIL + 16, :] = tail[TEAM_ROWS - 16 :]
    pay_ref[TAIL + 16 : TAIL + 32, :] = jnp.broadcast_to(last + 1.0, (16, 128)).astype(BF)


def local_kernel(pabs_ref, lab_ref, tot_ref):
    packed = pabs_ref[:, 256:384]
    values = pabs_ref[:, 0:128]
    labels_row = lab_ref[...]
    labels = column(labels_row)
    order = iota((TILE, TILE), 0) >= iota((TILE, TILE), 1)
    moved = [dot(packed, q_to_k(head)).astype(BF) for head in range(2)]
    ext = [extended(values, head) for head in range(2)]
    count = TEAM_ROWS // TILE
    for i in range(count):
        rows = slice(i * TILE, (i + 1) * TILE)
        total = [jnp.zeros((TILE, 128), F32) for _ in range(2)]
        for j in range(i + 1):
            cols = slice(j * TILE, (j + 1) * TILE)
            mask = tile_mask(labels, labels_row, i, j)
            if i == j:
                mask = mask & order
            for head in range(2):
                inner = dot_nt(moved[head][rows], packed[cols])
                weight = 1.0 + inner * (0.25 + inner * (1.0 / 32.0))
                weight = jnp.where(mask, weight, 0.0).astype(BF)
                total[head] = total[head] + dot(weight, ext[head][cols])
        for head in range(2):
            tot_ref[head, rows, :] = total[head]


def normalised(total, head):
    lane = iota(total.shape, 1)
    mass = jnp.sum(jnp.where(lane == one_lane(head), total, 0.0), 1, keepdims=True)
    inside = head_lanes(head, total.shape[0])
    attended = jnp.where(inside, total / mass, 0.0)
    mean = jnp.sum(attended * attended, 1, keepdims=True) * (1.0 / 64.0)
    return attended, mass, lax.rsqrt(mean + EPSILON)


def carried_query(packed, head):
    lane = iota(packed.shape, 1)
    moved = dot(packed, q_to_k(head)) * 0.25
    return jnp.where(lane == ONE, 1.0, moved).astype(BF)


def join_kernel(order, pabs_ref, lab_ref, local_ref, came_ref, taps_ref, wo_ref, tot_ref, mixed_ref, *send_refs):
    packed = pabs_ref[:, 256:384]
    values = pabs_ref[:, 0:128].astype(F32)
    labels = column(lab_ref[...])
    carried = came_ref[TAIL + 16 : TAIL + 32, :].astype(F32)[0:1] - 1.0
    usable = labels == carried
    attn = jnp.zeros((TEAM_ROWS, 128), F32)
    for head in range(2):
        at = head * STATE
        first = 16 * head
        outer = dot_nt(packed, spread(first, 0)) * dot_nt(packed, spread(first, 1))
        brought = dot(outer.astype(BF), came_ref[at : at + 256, :]) * (1.0 / 32.0)
        brought = brought + dot(carried_query(packed, head), came_ref[at + 256 : at + 384, :])
        total = local_ref[head] + jnp.where(usable, brought, 0.0)
        tot_ref[head] = total
        attended, _, scale = normalised(total, head)
        attn = attn + attended * scale
    tail = came_ref[TAIL : TAIL + 16, :].astype(F32)
    back_1, back_2, _, _ = conv_parts(values, tail, labels, carried)
    conv = taps_ref[0:1] * values + taps_ref[1:2] * back_1 + taps_ref[2:3] * back_2
    mixed = (attn + conv * pabs_ref[:, 128:256].astype(F32)).astype(BF)
    for block in range(8):
        start = pl.multiple_of(order[block] * ROWS, ROWS)
        mixed_ref[pl.ds(start, ROWS), :] = mixed[block * ROWS : (block + 1) * ROWS]
    part = dot(mixed_ref[512:, :], wo_ref[...])
    for hop in range(4):
        send_refs[hop][...] = part[hop * ROWS : (hop + 1) * ROWS].astype(BF)


def split_sum(total, got_refs, own_ref, piece_refs):
    own_ref[...] = total(0) + got_refs[0][...].astype(F32)
    for hop in (1, 2, 3):
        piece_refs[hop - 1][...] = (total(hop) + got_refs[hop][...].astype(F32)).astype(BF)


def mix_sum_kernel(left_ref, right_ref, *refs):
    total = dot(left_ref[0:512, :], right_ref[...])
    split_sum(lambda hop: total[hop * ROWS : (hop + 1) * ROWS], refs[:4], refs[4], refs[5:])


def add_kernel(mine_ref, *refs):
    split_sum(lambda hop: mine_ref[hop * ROWS : (hop + 1) * ROWS, :], refs[:4], refs[4], refs[5:])


def back_sum_kernel(left_ref, right_ref, *refs):
    total = dot_nt(left_ref[0:512, :], right_ref[...])
    split_sum(lambda hop: total[hop * ROWS : (hop + 1) * ROWS], refs[:4], refs[4], refs[5:])


def send_kernel(left_ref, right_ref, *send_refs):
    total = dot(left_ref[...], right_ref[...])
    for hop in range(4):
        send_refs[hop][...] = total[hop * ROWS : (hop + 1) * ROWS].astype(BF)


def norm_kernel(field_ref, own_ref, a_ref, b_ref, c_ref, after_ref, act_ref):
    came = a_ref[...].astype(F32) + b_ref[...].astype(F32) + c_ref[...].astype(F32)
    after = field_ref[...].astype(F32) + own_ref[...] + came
    after_ref[...] = after
    act_ref[...] = unit(after)[0].astype(BF)


def result_kernel(after_ref, own_ref, a_ref, b_ref, c_ref, out_ref):
    came = a_ref[...].astype(F32) + b_ref[...].astype(F32) + c_ref[...].astype(F32)
    out_ref[...] = (after_ref[...] + own_ref[...] + came).astype(BF)


def norm_back_kernel(field_ref, base_ref, own_ref, a_ref, b_ref, c_ref, *out_refs):
    upstream = a_ref[...].astype(F32) + b_ref[...].astype(F32) + c_ref[...].astype(F32)
    upstream = upstream + own_ref[...]
    field = field_ref[...].astype(F32)
    total = base_ref[...].astype(F32) + unit_back(field, unit(field)[1], upstream)
    for ref in out_refs:
        ref[...] = total.astype(ref.dtype)


def norm_mid_kernel(*refs):
    norm_back_kernel(*refs)


def ffn_own_kernel(*refs):
    ffn_kernel(*refs, half=0)


def ffn_other_kernel(*refs):
    ffn_kernel(*refs, half=1)


def ffn_kernel(*refs, half):
    acts, (cot_ref, w_ref, wd_ref) = refs[0:4], refs[4:7]
    hidden_ref, pair_ref, part_refs = refs[7], refs[8], refs[9:]
    for at in range(2):
        rows = slice(at * TILE, (at + 1) * TILE)
        act = jnp.concatenate([ref[...] for ref in acts[2 * at : 2 * at + 2]], 0)
        both = dot(act, w_ref[...])
        gate, up = both[:, 0:384], both[:, 384:768]
        d_hidden = dot_nt(cot_ref[half * 512 + at * TILE : half * 512 + (at + 1) * TILE, :], wd_ref[...])
        sigma = 1.0 / (1.0 + jnp.exp(-gate))
        swish = gate * sigma
        hidden_ref[rows, :] = (swish * up).astype(BF)
        pair_ref[rows, 0:384] = (d_hidden * up * sigma * (1.0 + gate * (1.0 - sigma))).astype(BF)
        pair_ref[rows, 384:768] = (d_hidden * swish).astype(BF)
        part = dot_nt(pair_ref[rows, :], w_ref[...])
        if len(part_refs) == 1:
            part_refs[0][rows, :] = part
        else:
            part_refs[2 * at][...] = part[0:ROWS].astype(BF)
            part_refs[2 * at + 1][...] = part[ROWS:].astype(BF)


def ffn_grad_kernel(*refs):
    acts, (cot_ref, pair_1, pair_2, hid_1, hid_2) = refs[0:8], refs[8:13]
    out_ref, act_ref, sum_ref = refs[13:]
    for place in range(8):
        act_ref[place * ROWS : (place + 1) * ROWS, :] = acts[place][...]
    for at in range(0, 1024, TILE):
        cols = slice(at, at + TILE)
        total = dot_tn(act_ref[0:512, cols], pair_1[...]) + dot_tn(act_ref[512:, cols], pair_2[...])
        for g in range(4):
            for l in range(3):
                part = total[g * 64 : (g + 1) * 64, l * 256 : (l + 1) * 256]
                out_ref[at // 64 + g, l * 64 : (l + 1) * 64] = part.astype(BF)
    for at in range(0, 384, 128):
        cols = slice(at, at + 128)
        total = dot_tn(hid_1[:, cols], cot_ref[0:512, :]) + dot_tn(hid_2[:, cols], cot_ref[512:, :])
        sum_ref[cols, :] = total
    for g in range(16):
        rows = sum_ref[g * 22 : (g + 1) * 22, :]
        for l in range(2):
            left, right = rows[:, l * 256 : (l + 1) * 256], rows[:, 512 + l * 256 : 768 + l * 256]
            part = jnp.concatenate([left, right, jnp.zeros((4, 256), F32)], 0)
            out_ref[g, 192 + l * 48 : 240 + l * 48] = part.astype(BF)


def sum_ffn_kernel(came_ref, two_ref, down_ref):
    total = came_ref[0].astype(F32)
    for g in range(1, 16):
        total = total + came_ref[g].astype(F32)
    two_ref[...] = total[0:192]
    down_ref[...] = total[192:288]


def owner_kernel(*refs):
    sum_ref, down_ref, out_ref, wq, wk, wv, wc, wg, wu, *small = refs[:12]
    gq, gk, gv, gc, gg, gu, gd, go, d1_ref, d2_ref, dt_ref = refs[12:]
    parts = [down_ref[l * 48 : l * 48 + 48] for l in range(2)]
    gd[...] = jnp.concatenate([p[0:22] for p in parts] + [p[22:44] for p in parts], 1)
    parts = [out_ref[l * 16 : l * 16 + 16] for l in range(4)]
    go[...] = jnp.concatenate([p[0:8] for p in parts] + [p[8:16] for p in parts], 1)
    turned = small_rows(*small)
    taps = jnp.zeros((8, 128), F32)
    for t in range(8):
        taps = taps + sum_ref[t, :, 256:384]
    dt_ref[...] = jnp.transpose(taps)[64:67, 0:8]
    diagonal = iota((8, 128), 0) == iota((8, 128), 1)
    one, two = turned[:, 0:1], turned[:, 1:2]
    raw = [sum_ref[t] for t in range(8)]
    value = jnp.concatenate([part[:, 0:128] for part in raw], 1)
    gate_c = jnp.concatenate([part[:, 128:256] for part in raw], 1)
    query = jnp.concatenate([part[:, 256:288] for part in raw], 1)
    key = jnp.concatenate([part[:, 288:320] for part in raw], 1)
    gate = jnp.concatenate([part[:, 384:736] for part in raw], 1)
    up = jnp.concatenate([part[:, 768:1120] for part in raw], 1)
    total = jnp.zeros((8, 1), F32)
    for weight, field, out in ((wq, query, gq), (wk, key, gk), (wv, value, gv), (wc, gate_c, gc)):
        total = total + jnp.sum(weight[...].astype(F32) * field, 1, keepdims=True)
        out[...] = field * one
    d1_ref[...] = jnp.sum(jnp.where(diagonal, total, 0.0), 0, keepdims=True)[:, 0:8]
    total = jnp.zeros((8, 1), F32)
    for weight, field, out in ((wg, gate, gg), (wu, up, gu)):
        total = total + jnp.sum(weight[...].astype(F32) * field, 1, keepdims=True)
        out[...] = field * two
    d2_ref[...] = jnp.sum(jnp.where(diagonal, total, 0.0), 0, keepdims=True)[:, 0:8]


def back_state_kernel(order, *refs):
    blocks, (pabs_ref, lab_ref, tot_ref, came_ref, taps_ref, wo_ref) = refs[:8], refs[8:14]
    de_ref, dvconv_ref, dgate_ref, dtaps_ref, pay_ref, dm_ref = refs[14:]
    for place in range(8):
        start = pl.multiple_of(order[9 + place] * ROWS, ROWS)
        dm_ref[pl.ds(start, ROWS), :] = dot_nt(blocks[place][...], wo_ref[...])
    d_mixed = dm_ref[...]
    packed = pabs_ref[:, 256:384]
    values = pabs_ref[:, 0:128].astype(F32)
    labels = column(lab_ref[...])
    carried = came_ref[TAIL + 16 : TAIL + 32, :].astype(F32)[0:1] - 1.0
    usable = labels == carried
    lane = iota((TEAM_ROWS, 128), 1)
    for head in range(2):
        attended, mass, scale = normalised(tot_ref[head], head)
        d_attn = jnp.where(head_lanes(head, TEAM_ROWS), d_mixed, 0.0)
        pull = jnp.sum(d_attn * attended, 1, keepdims=True) * (1.0 / 64.0)
        d_att = scale * (d_attn - attended * (scale * scale * pull))
        d_mass = -jnp.sum(d_att * attended, 1, keepdims=True) / mass
        d_ext = jnp.where(lane == one_lane(head), d_mass, d_att / mass).astype(BF)
        de_ref[head] = d_ext
        d_ext = jnp.where(usable, d_ext, jnp.zeros_like(d_ext))
        first = 16 * head
        at = head * STATE
        outer = dot_nt(spread(first, 0), packed) * dot_nt(spread(first, 1), packed)
        pay_ref[at : at + 256, :] = (dot(outer.astype(BF), d_ext) * (1.0 / 32.0)).astype(BF)
        turned = dot_nt(identity(), carried_query(packed, head)).astype(BF)
        pay_ref[at + 256 : at + 384, :] = dot(turned, d_ext).astype(BF)
    tail = came_ref[TAIL : TAIL + 16, :].astype(F32)
    back_1, back_2, mask_1, mask_2 = conv_parts(values, tail, labels, carried)
    conv = taps_ref[0:1] * values + taps_ref[1:2] * back_1 + taps_ref[2:3] * back_2
    dgate_ref[...] = (d_mixed * conv).astype(BF)
    d_conv = d_mixed * pabs_ref[:, 128:256].astype(F32)
    row8 = iota((8, 128), 0)
    sums = [jnp.sum(d_conv * part, 0, keepdims=True) for part in (values, back_1, back_2)]
    d_taps = jnp.zeros((8, 128), F32)
    for at in range(3):
        d_taps = jnp.where(row8 == at, sums[at], d_taps)
    dtaps_ref[...] = d_taps
    part_1 = jnp.where(mask_1, taps_ref[1:2] * d_conv, 0.0)
    part_2 = jnp.where(mask_2, taps_ref[2:3] * d_conv, 0.0)
    row = iota((TEAM_ROWS, 128), 0)
    up_1 = jnp.where(row < TEAM_ROWS - 1, pltpu.roll(part_1, TEAM_ROWS - 1, 0), 0.0)
    up_2 = jnp.where(row < TEAM_ROWS - 2, pltpu.roll(part_2, TEAM_ROWS - 2, 0), 0.0)
    dvconv_ref[...] = taps_ref[0:1] * d_conv + up_1 + up_2
    row16 = iota((16, 128), 0)
    edge = jnp.where(row16 == 14, part_2[0:1], 0.0)
    edge = jnp.where(row16 == 15, part_1[0:1] + part_2[1:2], edge)
    pay_ref[TAIL : TAIL + 16, :] = edge.astype(BF)
    pay_ref[TAIL + 16 : TAIL + 32, :] = jnp.zeros((16, 128), BF)


def back_local_kernel(pabs_ref, lab_ref, de_ref, came_ref, dqk_ref, dv_ref, dqt_ref):
    packed = pabs_ref[:, 256:384]
    values = pabs_ref[:, 0:128]
    labels_row = lab_ref[...]
    labels = column(labels_row)
    order = iota((TILE, TILE), 0) <= iota((TILE, TILE), 1)
    moved = [dot(packed, q_to_k(head)).astype(BF) for head in range(2)]
    keys_t = [dot_nt(q_to_k(head), packed).astype(BF) for head in range(2)]
    ext = [extended(values, head) for head in range(2)]
    inside = [head_lanes(head, TILE) for head in range(2)]
    count = TEAM_ROWS // TILE
    dqt_ref[...] = jnp.zeros((128, TEAM_ROWS), F32)
    for j in range(count):
        cols = slice(j * TILE, (j + 1) * TILE)
        d_key = jnp.zeros((TILE, 128), F32)
        d_val = jnp.zeros((TILE, 128), F32)
        for i in range(j, count):
            rows = slice(i * TILE, (i + 1) * TILE)
            mask = tile_mask(labels, labels_row, j, i)
            if i == j:
                mask = mask & order
            for head in range(2):
                d_ext = de_ref[head, rows, :]
                inner = dot_nt(packed[cols], moved[head][rows])
                weight = 1.0 + inner * (0.25 + inner * (1.0 / 32.0))
                weight = jnp.where(mask, weight, 0.0).astype(BF)
                d_weight = dot_nt(ext[head][cols], d_ext)
                d_inner = jnp.where(mask, d_weight * (0.25 + inner * (1.0 / 16.0)), 0.0).astype(BF)
                d_sum = jnp.where(inside[head], d_ext, jnp.zeros_like(d_ext))
                d_val = d_val + dot(weight, d_sum)
                d_key = d_key + dot(d_inner, moved[head][rows])
                dqt_ref[:, rows] += dot(keys_t[head][:, cols], d_inner)
        dqk_ref[cols, :] = d_key
        dv_ref[cols, :] = d_val
    carried = came_ref[TAIL + 16 : TAIL + 32, :].astype(F32)[0:1] - 1.0
    usable = labels == carried
    total = dqk_ref[...] + jnp.transpose(dqt_ref[...])
    for head in range(2):
        d_ext = de_ref[head]
        d_ext = jnp.where(usable, d_ext, jnp.zeros_like(d_ext))
        at = head * STATE
        first = 16 * head
        d_outer = dot_nt(d_ext, came_ref[at : at + 256, :]) * dot_nt(packed, spread(first, 1))
        total = total + dot((d_outer * (1.0 / 16.0)).astype(BF), spread(first, 0))
        d_line = dot_nt(d_ext, came_ref[at + 256 : at + 384, :]) * 0.25
        total = total + dot_nt(d_line.astype(BF), q_to_k(head))
    dqk_ref[...] = total


def back_join_kernel(order, pabs_ref, lab_ref, dqk_ref, dv_ref, dvconv_ref, dgate_ref, came_ref, w_ref, out_ref, *send_refs):
    packed = pabs_ref[:, 256:384]
    values = pabs_ref[:, 0:128]
    labels = column(lab_ref[...])
    keep = labels == labels[TEAM_ROWS - 1 : TEAM_ROWS]
    lane = iota((TEAM_ROWS, 128), 1)
    d_val = dv_ref[...] + dvconv_ref[...]
    d_qk = dqk_ref[...]
    edge = jnp.where(keep[TEAM_ROWS - 16 :], came_ref[TAIL : TAIL + 16, :].astype(F32), 0.0)
    edge = jnp.concatenate([jnp.zeros((TEAM_ROWS - 16, 128), F32), edge], 0)
    d_val = d_val + edge
    for head in range(2):
        at = head * STATE
        first = KLANE + 16 * head
        d_two = came_ref[at : at + 256, :]
        d_one = came_ref[at + 256 : at + 384, :]
        ext = jnp.where(keep, extended(values, head), jnp.zeros_like(values))
        left = dot_nt(packed, spread(first, 0))
        right = dot_nt(packed, spread(first, 1))
        key_lanes = (lane >= first) & (lane < first + 16)
        line = jnp.where(key_lanes | (lane == ONE), packed, jnp.zeros_like(packed))
        d_ext = dot((left * right).astype(BF), d_two) + dot(line, d_one)
        d_val = d_val + jnp.where(keep & head_lanes(head, TEAM_ROWS), d_ext, 0.0)
        d_outer = dot_nt(ext, d_two) * right
        d_qk = d_qk + dot((d_outer * 2.0).astype(BF), spread(first, 0))
        d_qk = d_qk + jnp.where(key_lanes, dot_nt(ext, d_one), 0.0)
    d_val = d_val.astype(BF)
    d_qk = d_qk.astype(BF)
    for block in range(8):
        start = pl.multiple_of(order[block] * ROWS, ROWS)
        rows = slice(block * ROWS, (block + 1) * ROWS)
        out_ref[pl.ds(start, ROWS), 0:128] = d_val[rows]
        out_ref[pl.ds(start, ROWS), 128:256] = dgate_ref[rows, :]
        out_ref[pl.ds(start, ROWS), 256:384] = d_qk[rows]
    part = dot_nt(out_ref[512:, :], w_ref[...])
    for hop in range(4):
        send_refs[hop][...] = part[hop * ROWS : (hop + 1) * ROWS].astype(BF)


def mixer_grad_kernel(order, *refs):
    blocks, (mixed_ref, dtaps_ref, act_ref, dp_ref) = refs[:8], refs[8:12]
    grad_ref, sum_ref = refs[12:]
    for at in range(0, 1024, TILE):
        sum_ref[at : at + TILE, :] = dot(act_ref[at : at + TILE, :], dp_ref[...])
    start = pl.multiple_of(order[8] * 128, 128)
    spare = [jnp.zeros((64, 128), F32), dtaps_ref[...], jnp.zeros((56, 128), F32)]
    sum_ref[pl.ds(start, 128), 256:384] += jnp.transpose(jnp.concatenate(spare, 0))
    d_out = jnp.zeros((128, 1024), F32)
    for place in range(8):
        rows = slice(place * ROWS, (place + 1) * ROWS)
        d_out = d_out + dot_tn(mixed_ref[rows, :], blocks[place][...])
    for g in range(16):
        for l in range(3):
            part = sum_ref[g * 64 : (g + 1) * 64, l * 128 : (l + 1) * 128]
            grad_ref[g, l * 64 : (l + 1) * 64] = part.astype(BF)
        rows = d_out[g * 8 : (g + 1) * 8]
        for l in range(4):
            part = [rows[:, l * 128 : (l + 1) * 128], rows[:, 512 + l * 128 : 640 + l * 128]]
            grad_ref[g, 192 + l * 16 : 208 + l * 16] = jnp.concatenate(part, 0).astype(BF)


def sum_mixer_kernel(came_ref, other_ref, sum_ref, out_ref):
    total = came_ref[0].astype(F32)
    for g in range(1, 16):
        total = total + came_ref[g].astype(F32)
    for l in range(3):
        for t in range(8):
            rows = slice(l * 64 + t * 8, l * 64 + t * 8 + 8)
            sum_ref[t, :, l * 128 : (l + 1) * 128] = total[rows]
            sum_ref[t, :, 384 + l * 256 : 640 + l * 256] = other_ref[rows, :]
    out_ref[...] = total[192:256]


def call(kernel, outs, args, ordered=False, scratch=(), far=(), far_outs=(), lazy=False, grant=16):
    specs = [pl.BlockSpec(memory_space=pltpu.HBM if i in far else pltpu.VMEM) for i in range(len(args))]
    if ordered:
        specs[0] = pl.BlockSpec(memory_space=pltpu.SMEM)
    out_specs = [
        pl.BlockSpec(memory_space=pltpu.HBM if i in far_outs else pltpu.VMEM) for i in range(len(outs))
    ]
    rooms = [pltpu.VMEM(args[i].shape, args[i].dtype) for i in far]
    rooms += [pltpu.VMEM(outs[i].shape, outs[i].dtype) for i in far_outs]
    sems = [pltpu.SemaphoreType.DMA((len(rooms),))] if rooms else []

    def body(*refs):
        ins, results = list(refs[: len(args)]), list(refs[len(args) : len(args) + len(outs)])
        own = refs[len(args) + len(outs) :]
        own, room = own[: len(scratch)], own[len(scratch) :]
        reads, writes, sent = [], [], set()
        for at, i in enumerate(far):
            reads.append(pltpu.make_async_copy(ins[i], room[at], room[-1].at[at]))
            ins[i] = room[at]
        for at, i in enumerate(far_outs, len(far)):
            writes.append(pltpu.make_async_copy(room[at], results[i], room[-1].at[at]))
            results[i] = room[at]
        for copy in reads:
            copy.start()

        def put(at):
            sent.add(at)
            writes[at].start()

        def get(at):
            reads[at].wait()

        if lazy:
            kernel(*ins, *results, *own, get=get, put=put)
        else:
            for copy in reads:
                copy.wait()
            kernel(*ins, *results, *own)
        for at in range(len(writes)):
            if at not in sent:
                put(at)
        for copy in writes:
            copy.wait()

    micros = TIMES[kernel.__name__]
    return pl.pallas_call(
        body,
        out_shape=tuple(outs),
        in_specs=specs,
        out_specs=tuple(out_specs),
        scratch_shapes=list(scratch) + rooms + sems,
        cost_estimate=pl.CostEstimate(
            flops=int(micros * 1.15e9), bytes_accessed=int(micros * 3.6e6), transcendentals=0
        ),
        compiler_params=pltpu.CompilerParams(vmem_limit_bytes=grant * MIB),
    )(*args)


def shape(*sizes):
    return jax.ShapeDtypeStruct(sizes[:-1], sizes[-1])


def exchange(blocks, axes):
    return lax.all_to_all(blocks, axes, 0, 0, tiled=True)


def unit(field):
    scale = lax.rsqrt(jnp.mean(field * field, -1, keepdims=True) + EPSILON)
    return field * scale, scale


def unit_back(field, scale, upstream):
    pull = jnp.mean(field * upstream, -1, keepdims=True)
    return scale * upstream - field * (scale * scale * scale * pull)


def per_device(
    inputs, segments, cotangent, attn_gain, w_query, w_key, w_value, w_conv_gate,
    conv_kernel, w_output, ffn_gain, w_ffn_gate, w_ffn_up, w_ffn_down,
):
    x, core = lax.axis_index("x"), lax.axis_index("core")
    block = jnp.arange(8, dtype=jnp.int32)
    order = ((block % 2) ^ core) * 4 + (block // 2 - x) % 4
    back = 2 * ((block % 4 + x) % 4) + ((block // 4) ^ core)
    order = jnp.concatenate([order, jnp.full((1,), x * 2 + core, jnp.int32), back])
    small = (attn_gain[None], ffn_gain[None], conv_kernel)
    to_team = [(f, (f % 16) * 8 + f // 16) for f in range(128)]
    to_owner = [(place, f) for f, place in to_team]

    weights = (
        w_query, w_key, w_value, w_conv_gate, w_ffn_gate, w_ffn_up, w_output, w_ffn_down, *small,
    )
    pack, whole = call(
        pack_kernel,
        [shape(8, 8, 1152, BF), shape(64, 512, BF)],
        weights,
        far=range(11),
        grant=60,
    )
    mine = exchange(pack, TEAM).reshape(64, 1152)
    ready = whole
    whole = lax.ppermute(whole, AXES, to_team)
    (tiles,) = call(spread_mixer_kernel, [shape(16, 256, 128, BF)], (mine, whole))
    mixer_came = exchange(tiles, GROUP)

    (block,) = call(
        block_kernel,
        [shape(BLOCK, 1024, BF)],
        (tie(inputs, ready), cotangent, segments[None]),
    )
    own_x = own_gather(block)
    other_x = other_gather(own_x)

    act_one, codes, cot = call(
        act_kernel,
        [shape(TEAM_ROWS, 1024, BF), shape(8, 128, F32), shape(TEAM_ROWS, 1024, BF)],
        (*own_x, *other_x),
    )
    pabs, payload, labels, taps, weight_1, weight_o = call(
        state_kernel,
        [
            shape(TEAM_ROWS, 384, BF),
            shape(PAYLOAD, 128, BF),
            shape(1, TEAM_ROWS, F32),
            shape(8, 128, F32),
            shape(1024, 384, BF),
            shape(128, 1024, BF),
        ],
        (order, act_one, codes, mixer_came),
        True,
        [pltpu.VMEM((TEAM_ROWS, 384), BF)],
    )
    came = lax.ppermute(payload, "zh", [(0, 1)])
    (local,) = call(local_kernel, [shape(2, TEAM_ROWS, 128, F32)], (pabs, labels))
    rows_f, rows_b = shape(ROWS, 1024, F32), shape(ROWS, 1024, BF)
    total, mixed, *sends = call(
        join_kernel,
        [shape(2, TEAM_ROWS, 128, F32), shape(TEAM_ROWS, 128, BF)] + [rows_b] * 4,
        (order, pabs, labels, local, came, taps, weight_o),
        True,
    )
    pieces = [rows_f] + [rows_b] * 3
    got = swap_all(sends)
    own, *rest = call(mix_sum_kernel, pieces, (mixed, weight_o, *got))
    (tiles,) = call(spread_ffn_kernel, [shape(16, 288, 256, BF)], (tie(mine, mixer_came), whole))
    ffn_came = exchange(tie(tiles, payload), GROUP)
    after_mixer, own_two = call(norm_kernel, [rows_f, rows_b], (inputs, own, *own_scatter(rest)))
    (act_turned,) = call(turn_kernel, [shape(1024, TEAM_ROWS, BF)], (tie(act_one, own),))

    own_act = own_gather(tie(own_two, act_turned))
    weight_2, weight_d = call(
        ffn_weights_kernel,
        [shape(1024, 768, BF), shape(384, 1024, BF)],
        (tie(ffn_came, own_act[1]),),
        grant=60,
    )
    other_act = other_gather(own_act)
    halves = [shape(512, 384, BF), shape(512, 768, BF)]
    other_hidden, other_pair, *sends = call(
        ffn_other_kernel, halves + [rows_b] * 4, (*other_act, cot, weight_2, weight_d)
    )
    got = swap_all(sends)
    own_hidden, own_pair, part = call(
        ffn_own_kernel,
        halves + [shape(512, 1024, F32)],
        (*own_act, cot, weight_2, weight_d),
    )
    own, *rest = call(add_kernel, pieces, (part, *got))
    (grad_2,) = call(
        ffn_grad_kernel,
        [shape(16, 288, 256, BF)],
        (
            *own_act, *other_act, tie(cot, own),
            own_pair, other_pair, own_hidden, other_hidden,
        ),
        scratch=[
            pltpu.VMEM((1024, 1024), BF),
            pltpu.VMEM((384, 1024), F32),
        ],
    )
    two_came = own_scatter(rest)
    d_after, own_branch = call(
        norm_mid_kernel,
        [rows_f, rows_b],
        (after_mixer, cotangent, own, *two_came),
        far=range(6),
        far_outs=(0, 1),
        grant=60,
    )
    own_branch = tie(own_branch, grad_2)
    grad_2 = exchange(grad_2, GROUP)
    sends = call(send_kernel, [rows_b] * 4, (tie(other_hidden, own_branch), weight_d))
    got = swap_all(sends)
    own_branch = own_gather(own_branch)
    d_branch = (*own_branch, *other_gather(own_branch))
    result_own, *rest = call(mix_sum_kernel, pieces, (own_hidden, weight_d, *got))
    result_came = own_scatter(tie_all(rest, own_branch[1]))
    (result,) = call(result_kernel, [rows_b], (after_mixer, result_own, *result_came))

    d_ext, d_val_conv, d_gate_c, d_taps, payload = call(
        back_state_kernel,
        [
            shape(2, TEAM_ROWS, 128, BF),
            shape(TEAM_ROWS, 128, F32),
            shape(TEAM_ROWS, 128, BF),
            shape(8, 128, F32),
            shape(PAYLOAD, 128, BF),
        ],
        (order, *d_branch, pabs, labels, total, came, taps, weight_o),
        True,
        [pltpu.VMEM((TEAM_ROWS, 128), F32)],
    )
    came_2 = lax.ppermute(payload, "zh", [(1, 0)])
    d_qk, d_val = call(
        back_local_kernel,
        [shape(TEAM_ROWS, 128, F32), shape(TEAM_ROWS, 128, F32)],
        (pabs, labels, d_ext, came),
        scratch=[pltpu.VMEM((128, TEAM_ROWS), F32)],
    )
    d_projected, *sends = call(
        back_join_kernel,
        [shape(TEAM_ROWS, 384, BF)] + [rows_b] * 4,
        (
            order, pabs, labels, d_qk, d_val, d_val_conv, d_gate_c, tie(came_2, result),
            weight_1,
        ),
        True,
    )
    got = swap_all(sends)
    (grad_1,) = call(
        mixer_grad_kernel,
        [shape(16, 256, 128, BF)],
        (order, *d_branch, mixed, d_taps, act_turned, d_projected),
        True,
        [pltpu.VMEM((TEAM_ROWS, 384), F32)],
    )
    sum_2, sum_d = call(
        sum_ffn_kernel, [shape(192, 256, F32), shape(96, 256, F32)], (grad_2,)
    )
    own, *rest = call(
        back_sum_kernel,
        pieces,
        (d_projected, weight_1, *got),
        far=range(6),
        far_outs=range(4),
        grant=60,
    )
    grad_1 = exchange(tie(grad_1, grad_2, *got), GROUP)
    last = own_scatter(rest)
    grad_1 = tie(grad_1, last[0])
    (d_inputs,) = call(norm_back_kernel, [rows_b], (inputs, d_after, own, *last))

    sum_d = lax.ppermute(sum_d, AXES, to_owner)
    sums, sum_o = call(
        sum_mixer_kernel, [shape(8, 8, 1152, F32), shape(64, 128, F32)], (grad_1, sum_2)
    )
    sum_o = lax.ppermute(sum_o, AXES, to_owner)
    sums = exchange(sums, TEAM)
    gq, gk, gv, gc, gg, gu, gd, go, gain_grad_1, gain_grad_2, grad_taps = call(
        owner_kernel,
        [shape(8, cols, F32) for cols in (256, 256, 1024, 1024, 2816, 2816)]
        + [shape(22, 1024, F32), shape(8, 1024, F32)]
        + [shape(1, 8, F32), shape(1, 8, F32), shape(3, 8, F32)],
        (sums, sum_d, sum_o, *weights[:6], *small),
        far=range(12),
        grant=60,
    )
    return (
        result, d_inputs, gain_grad_1[0], gq, gk, gv, gc, grad_taps, go,
        gain_grad_2[0], gg, gu, gd,
    )


def solution(mesh):
    fine = Mesh(mesh.devices.reshape(SIZES), AXES)
    row, vector, taps = P(AXES, None), P(AXES), P(None, AXES)
    return jax.shard_map(
        per_device,
        mesh=fine,
        in_specs=(row, vector, row, vector, row, row, row, row, taps, row, vector, row, row, row),
        out_specs=(row, row, vector, row, row, row, row, taps, row, vector, row, row, row),
        check_vma=False,
    )
```
